32 devices in a mesh: tm: 8 (over y, x, core), space: 4 (over z).
Axes of the slice: x: 2, y: 2, z: 4, core: 2. Of those that a mesh axis runs over, the one named last changes fastest.
Arguments:
- frames: bfloat16 [4096, 4, 256], P('tm', 'space'), may hold values from -8 to 8
- patch_cell: int32 [4], P('space'), may hold values from 0 to 2047
- enc_in: bfloat16 [256, 1024], replicated, may hold values from -0.375 to 0.375
- enc_bias: float32 [1024], replicated, may hold values from -3 to 3
- enc_out: bfloat16 [1024, 1024], replicated, may hold values from -0.1875 to 0.1875
- pos_table: bfloat16 [2048, 1024], replicated, may hold values from -3 to 3
- norm_gain: float32 [1024], replicated, may hold values from 0.1 to 1.9
- w_pair: bfloat16 [1024, 4096], replicated, may hold values from -0.1875 to 0.1875
- w_keys: bfloat16 [1024, 256], replicated, may hold values from -0.0234375 to 0.0234375
- w_step: bfloat16 [1024, 32], replicated, may hold values from -0.1875 to 0.1875
- step_bias: float32 [32], replicated, may hold values from -1.5 to 1
- decay_code: int32 [32], replicated, may hold values from 0 to 15
- skip_gain: float32 [32], replicated, may hold values from 0.5 to 1.5
- out_gain: float32 [2048], replicated, may hold values from 0.1 to 1.9
- w_out: bfloat16 [2048, 1024], replicated, may hold values from -0.125 to 0.125
Outputs:
- layer_output: bfloat16 [4096, 4, 1024], P('tm', 'space')
The draws below stay inside these ranges and needn't reach their ends.
All inputs are finite; a program needn't handle non-finite values.
Results may differ from the reference program's by a relative error of at most 0.013.
Values may be sent and summed in bfloat16 or wider, within the bound.
No kernel may reach another device: no remote copies, remote signals or barrier semaphores. Data moves between devices by JAX's collectives and lax.ppermute only.
A program may use at most 128 MiB of HBM per device.

```python
import jax
import jax.numpy as jnp
from jax import lax

D = 1024
PIX = 256
HEADS = 32
HD = 64
N = 128
GRID = 2048
TB = 512
TIME = 4096
PATCHES = 4
N_TM = 8


def draw_frames(key, part):
    key_noise = jax.random.fold_in(key, 11)
    key_level = jax.random.fold_in(key, 12)
    key_shape = jax.random.fold_in(key, 13)
    noise = jnp.clip(jax.random.normal(key_noise, (TIME, PATCHES, PIX), jnp.float32), -5.0, 5.0)
    run_len = TB // 4
    levels = jax.random.uniform(key_level, (TIME // run_len,), jnp.float32, -2.0, 2.0)
    level_rows = jnp.repeat(levels, run_len)
    pattern = jnp.clip(0.7 * jax.random.normal(key_shape, (PATCHES, PIX), jnp.float32), -2.0, 2.0)
    values = noise + level_rows[:, None, None] * pattern[None]
    return jnp.clip(values, -8.0, 8.0).astype(jnp.bfloat16)


def plant(values, own_key, low, high):
    longest = values.shape.index(max(values.shape))
    spots = []
    for shift in (0, 1):
        where = [jax.random.randint(jax.random.fold_in(own_key, axis), (), 0, length) for axis, length in enumerate(values.shape)]
        where[longest] = (where[longest] + shift) % values.shape[longest]
        spots.append(tuple(where))
    return values.at[spots[0]].set(low).at[spots[1]].set(high)


def scatter_about(stream_key, dims, scale, most, kind=jnp.bfloat16):
    drawn = jax.random.normal(stream_key, dims, jnp.float32) * scale
    return jnp.minimum(jnp.maximum(drawn, -most), most).astype(kind)


def setup_inputs(seed: int = 0) -> dict:
    seeds = jax.random.split(jax.random.key(seed), 16)
    frames = draw_frames(jax.random.fold_in(seeds[15], 71), 0)
    patch_cell = plant(jax.random.randint(seeds[1], (PATCHES,), 0, GRID), jax.random.fold_in(seeds[1], 1), 0, GRID - 1).astype(jnp.int32)
    enc_in = scatter_about(seeds[2], (PIX, D), PIX ** -0.5, 0.375)
    enc_bias = scatter_about(seeds[3], (D,), 0.5, 3.0, jnp.float32)
    enc_out = scatter_about(seeds[4], (D, D), D ** -0.5, 0.1875)
    pos_table = scatter_about(seeds[5], (GRID, D), 0.5, 3.0)
    norm_gain = jnp.clip(1.0 + 0.18 * jax.random.normal(seeds[6], (D,), jnp.float32), 0.1, 1.9)
    w_pair = scatter_about(seeds[7], (D, HEADS * 2 * HD), D ** -0.5, 0.1875)
    w_keys = scatter_about(seeds[8], (D, 2 * N), (64 * D) ** -0.5, 0.0234375)
    w_step = scatter_about(seeds[9], (D, HEADS), D ** -0.5, 0.1875)
    step_bias = jnp.clip(jax.random.uniform(seeds[10], (HEADS,), jnp.float32, -1.5, 1.0), -1.5, 1.0)
    decay_code = plant(jax.random.randint(seeds[11], (HEADS,), 0, 16), jax.random.fold_in(seeds[11], 1), 0, 15).astype(jnp.int32)
    skip_gain = jnp.clip(jax.random.uniform(seeds[12], (HEADS,), jnp.float32, 0.5, 1.5), 0.5, 1.5)
    out_gain = jnp.clip(1.0 + 0.18 * jax.random.normal(seeds[13], (HEADS * HD,), jnp.float32), 0.1, 1.9)
    w_out = scatter_about(seeds[14], (HEADS * HD, D), (HEADS * HD) ** -0.5, 0.125)
    return dict(frames=frames, patch_cell=patch_cell, enc_in=enc_in, enc_bias=enc_bias, enc_out=enc_out, pos_table=pos_table, norm_gain=norm_gain, w_pair=w_pair, w_keys=w_keys, w_step=w_step, step_bias=step_bias, decay_code=decay_code, skip_gain=skip_gain, out_gain=out_gain, w_out=w_out)


def rate_table(decay_code):
    return -0.0005 - 0.003 * decay_code.astype(jnp.float32)

def encode(frame_block, pos_rows, enc_in, enc_bias, enc_out, norm_gain):
    hidden = jax.nn.gelu(jnp.dot(frame_block, enc_in, preferred_element_type=jnp.float32) + enc_bias, approximate=True).astype(jnp.bfloat16)
    encoded = (jnp.dot(hidden, enc_out, preferred_element_type=jnp.float32) + pos_rows.astype(jnp.float32)).astype(jnp.bfloat16)
    widened = encoded.astype(jnp.float32)
    normed = (widened * lax.rsqrt(lax.optimization_barrier(jnp.mean(widened * widened, axis=-1, keepdims=True)) + 1e-05) * norm_gain).astype(jnp.bfloat16)
    return (encoded, normed)

def patch_scan(x_vals, z_vals, step_sizes, key_rows, rate_row, skip_row, gain_rows, state_in):
    width = key_rows.shape[-1] // 2
    b_rows = key_rows[:, :width]
    c_rows = key_rows[:, width:]
    cumlog = jnp.cumsum(step_sizes.astype(jnp.float32) * rate_row[None, :], axis=0)
    scores = jnp.dot(c_rows, b_rows.T, preferred_element_type=jnp.float32)
    length = x_vals.shape[0]
    causal = lax.broadcasted_iota(jnp.int32, (length, length), 0) >= lax.broadcasted_iota(jnp.int32, (length, length), 1)
    log_gap = cumlog.T[:, :, None] - cumlog.T[:, None, :]
    weights = (jnp.where(causal[None], jnp.exp(jnp.where(causal[None], log_gap, 0.0)), 0.0) * scores[None]).astype(jnp.bfloat16)
    inner_part = jnp.einsum('hts,shd->thd', weights.astype(jnp.float32), x_vals.astype(jnp.float32))
    to_end = jnp.exp(cumlog[-1][None, :] - cumlog)
    decayed_keys = (to_end[:, :, None] * b_rows.astype(jnp.float32)[:, None, :]).astype(jnp.bfloat16)
    block_state = jnp.einsum('shn,shd->hnd', decayed_keys.astype(jnp.float32), x_vals.astype(jnp.float32))
    carried = jnp.exp(cumlog)[:, :, None] * jnp.einsum('tn,hnd->thd', c_rows.astype(jnp.float32), state_in, precision=lax.Precision.HIGHEST)
    summed = inner_part + carried + skip_row[None, :, None] * x_vals.astype(jnp.float32)
    gated = summed * jax.nn.silu(z_vals.astype(jnp.float32))
    normed = gated * lax.rsqrt(lax.optimization_barrier(jnp.mean(gated * gated, axis=-1, keepdims=True)) + 1e-05) * gain_rows[None]
    new_state = jnp.exp(cumlog[-1])[:, None, None] * state_in + block_state
    return (normed.astype(jnp.bfloat16).reshape(length, -1), new_state)

def reference(frames, patch_cell, enc_in, enc_bias, enc_out, pos_table, norm_gain, w_pair, w_keys, w_step, step_bias, decay_code, skip_gain, out_gain, w_out):
    decay_rates = rate_table(decay_code)
    pos_rows = jnp.take(pos_table, patch_cell, axis=0)
    gain_rows = out_gain.reshape(HEADS, HD)
    split_frames = frames.reshape(N_TM, TB, PATCHES, PIX)

    def one_block(states, frame_block):
        encoded, normed = encode(frame_block, pos_rows, enc_in, enc_bias, enc_out, norm_gain)
        pair_cols = jnp.dot(normed, w_pair, preferred_element_type=jnp.float32).astype(jnp.bfloat16).reshape(TB, PATCHES, HEADS, 2 * HD)
        key_rows = jnp.dot(normed, w_keys, preferred_element_type=jnp.float32).astype(jnp.bfloat16)
        step_sizes = jax.nn.sigmoid(jnp.dot(normed, w_step, preferred_element_type=jnp.float32) + step_bias).astype(jnp.bfloat16)

        def per_patch(packed):
            patch_id, state_in = packed
            pair_one = lax.dynamic_index_in_dim(pair_cols, patch_id, 1, keepdims=False)
            step_one = lax.dynamic_index_in_dim(step_sizes, patch_id, 1, keepdims=False)
            key_one = lax.dynamic_index_in_dim(key_rows, patch_id, 1, keepdims=False)
            return patch_scan(pair_one[..., :HD], pair_one[..., HD:], step_one, key_one, decay_rates, skip_gain, gain_rows, state_in)
        outputs, new_states = lax.map(per_patch, (jnp.arange(PATCHES, dtype=jnp.int32), states))
        merged = jnp.dot(jnp.swapaxes(outputs, 0, 1), w_out, preferred_element_type=jnp.float32)
        return (new_states, (encoded.astype(jnp.float32) + merged).astype(jnp.bfloat16))
    _, result_rows = lax.scan(one_block, jnp.zeros((PATCHES, HEADS, N, HD), jnp.float32), split_frames)
    return result_rows.reshape(TIME, PATCHES, D)
```

```python
import jax
import jax.numpy as jnp
from jax import lax
from jax.sharding import PartitionSpec as P

BF = jnp.bfloat16
F32 = jnp.float32


def dot(a, b):
    return jnp.dot(a, b, preferred_element_type=F32)


def carried_state(state, decay, peers):
    here = lax.axis_index("tm")

    def shifted(value, value_decay, by):
        pairs = [(i, i + by) for i in range(peers - by)]
        got, got_decay = lax.ppermute((value.astype(BF), value_decay), "tm", pairs)
        return got.astype(F32), jnp.where(here < by, 1.0, got_decay)

    before, before_decay = shifted(state, decay, 1)
    reach = 1
    while reach < peers:
        got, got_decay = shifted(before, before_decay, reach)
        before = before + before_decay * got
        before_decay = before_decay * got_decay
        reach *= 2
    return before


def body(frames, patch_cell, enc_in, enc_bias, enc_out, pos_table, norm_gain, w_pair, w_keys, w_step,
         step_bias, decay_code, skip_gain, out_gain, w_out):
    count = frames.shape[0]
    heads = w_step.shape[1]
    head_dim = w_pair.shape[1] // (2 * heads)
    width = w_keys.shape[1] // 2
    flat = heads * head_dim
    rate = -0.0005 - 0.003 * decay_code.astype(F32)
    pos = jnp.take(pos_table, patch_cell, axis=0)
    tokens = frames.reshape(count, frames.shape[2])
    hidden = jax.nn.gelu(dot(tokens, enc_in) + enc_bias, approximate=True).astype(BF)
    encoded = (dot(hidden, enc_out) + pos.astype(F32)).astype(BF)
    wide = encoded.astype(F32)
    normed = (wide * lax.rsqrt(jnp.mean(wide * wide, axis=-1, keepdims=True) + 1e-05) * norm_gain).astype(BF)
    pair = dot(normed, w_pair).astype(BF).reshape(count, heads, 2 * head_dim)
    keys = dot(normed, w_keys).astype(BF)
    step = jax.nn.sigmoid(dot(normed, w_step) + step_bias).astype(BF)
    lower = lax.broadcasted_iota(jnp.int32, (count, count), 0) >= lax.broadcasted_iota(jnp.int32, (count, count), 1)
    cum = dot(lower.astype(BF), step) * rate
    grow, fall = jnp.exp(-cum), jnp.exp(cum)
    x = pair[..., :head_dim]
    gate = pair[..., head_dim:]
    scaled = (x.astype(F32) * grow[:, :, None]).astype(BF).reshape(count, flat)
    b_rows, c_rows = keys[:, :width], keys[:, width:]
    scores = jnp.where(lower, dot(c_rows, b_rows.T), 0.0).astype(BF)
    inner = dot(scores, scaled).reshape(count, heads, head_dim)
    state = dot(b_rows.T, scaled) * jnp.repeat(fall[-1], head_dim)[None]
    entering = carried_state(state, jnp.repeat(fall[-1], head_dim)[None], lax.axis_size("tm"))
    carried = dot(c_rows, entering.astype(BF)).reshape(count, heads, head_dim)
    y = (inner + carried) * fall[:, :, None] + skip_gain[None, :, None] * x.astype(F32)
    g = y * jax.nn.silu(gate.astype(F32))
    mixed = g * lax.rsqrt(jnp.mean(g * g, axis=-1, keepdims=True) + 1e-05) * out_gain.reshape(heads, head_dim)
    merged = dot(mixed.astype(BF).reshape(count, flat), w_out)
    return (wide + merged).astype(BF).reshape(frames.shape[0], 1, -1)


def solution(mesh):
    placed = (P("tm", "space", None), P("space")) + (P(),) * 13
    return jax.shard_map(body, mesh=mesh, in_specs=placed, out_specs=P("tm", "space", None), check_vma=False)
```

```python
import functools

import jax
import jax.numpy as jnp
from jax import lax
from jax.experimental import pallas as pl
from jax.experimental.pallas import tpu as pltpu
from jax.sharding import PartitionSpec as P

BF = jnp.bfloat16
F32 = jnp.float32
VM = pl.BlockSpec(memory_space=pltpu.VMEM)
SM = pl.BlockSpec(memory_space=pltpu.SMEM)
ANY = pl.BlockSpec(memory_space=pl.ANY)
LANES = 128
CHUNK = 256
EXTRA = 16


def dot(a, b):
    return jnp.dot(a, b, preferred_element_type=F32)


def dot_t(a, b):
    return lax.dot_general(a, b, (((1,), (1,)), ((), ())), preferred_element_type=F32)


def iota(shape, axis):
    return lax.broadcasted_iota(jnp.int32, shape, axis)


def params(mib):
    return pltpu.CompilerParams(vmem_limit_bytes=mib * 2**20)


def sds(shape, dtype):
    return jax.ShapeDtypeStruct(shape, dtype)


def spread_heads(first_head, heads, head_dim):
    row = iota((2 * heads, CHUNK), 0)
    lane = iota((2 * heads, CHUNK), 1)
    row = jnp.where(row < heads, row, row - heads)
    return (row == first_head + lane // head_dim).astype(F32).astype(BF)


def split_two(value, heads):
    high = value.astype(BF).astype(F32)
    return jnp.where(iota(value.shape, 1) < heads, high, value - high).astype(BF)


def pick_half(tile_a, tile_b, part):
    half = LANES // 2
    low = iota(tile_a.shape, 1) < half
    if part == 0:
        return jnp.where(low, tile_a, pltpu.roll(tile_b, half, 1))
    return jnp.where(low, pltpu.roll(tile_a, half, 1), tile_b)


def compact(ref, part):
    tiles = [ref[:, i * LANES:(i + 1) * LANES] for i in range(2 * CHUNK // LANES)]
    pairs = [pick_half(tiles[i], tiles[i + 1], part) for i in range(0, len(tiles), 2)]
    return jnp.concatenate(pairs, axis=1)


def weight_copies(w_ref, buf, sem, half, count):
    copies = []
    for j in range(count):
        start = pl.multiple_of((half * count + j) * 2 * CHUNK, 2 * CHUNK)
        copies.append(pltpu.make_async_copy(w_ref.at[:, pl.ds(start, 2 * CHUNK)], buf.at[j], sem.at[j]))
    return copies


def project(j, half, heads, head_dim, count, buf, normed, b_t, grow, fall_end, x_ref, xs_ref, s_ref):
    width = b_t.shape[0]
    per = CHUNK // head_dim
    first = (half * count + j) * per
    cols = slice(j * CHUNK, (j + 1) * CHUNK)
    spread = spread_heads(first, heads, head_dim)
    x = dot(normed[...], compact(buf.at[j], 0)).astype(BF)
    scaled = (x.astype(F32) * dot(grow, spread)).astype(BF)
    x_ref[:, cols] = x
    xs_ref[:, cols] = scaled
    decay = dot(fall_end, spread)[EXTRA - 1:EXTRA]
    s_ref[0:width, cols] = (dot(b_t, scaled) * decay).astype(BF)
    high = decay.astype(BF).astype(F32)
    row = iota((EXTRA, CHUNK), 0)
    s_ref[width:width + EXTRA, cols] = jnp.where(row == 0, high, jnp.where(row == 1, decay - high, 0.0)).astype(BF)


def encode_kernel(heads, head_dim, half_ref, cell_ref, frames, enc_in, enc_bias, norm_gain, w_keys, w_step, step_bias,
                  rate, enc_out_any, pos_any, w_pair_any, encoded, normed, keys, b_t, grow, fall, x_ref, xs_ref, s_ref,
                  enc_out, pos, buf, sem, wsem):
    half = 1 - half_ref[0]
    count = buf.shape[0]
    cell = cell_ref[0]
    base = pl.multiple_of((cell // EXTRA) * EXTRA, EXTRA)
    out_copy = pltpu.make_async_copy(enc_out_any, enc_out, sem.at[0])
    pos_copy = pltpu.make_async_copy(pos_any.at[pl.ds(base, EXTRA), :], pos, sem.at[1])
    out_copy.start()
    pos_copy.start()
    copies = weight_copies(w_pair_any, buf, wsem, half, count)
    for c in copies:
        c.start()
    rows, depth = encoded.shape
    hidden = []
    for j in range(depth // CHUNK):
        cols = slice(j * CHUNK, (j + 1) * CHUNK)
        h = dot(frames[...], enc_in[:, cols]) + enc_bias[:, cols]
        hidden.append(jax.nn.gelu(h, approximate=True).astype(BF))
    hidden = jnp.concatenate(hidden, axis=1)
    out_copy.wait()
    pos_copy.wait()
    row = jnp.sum(jnp.where(iota(pos.shape, 0) == cell - base, pos[...].astype(F32), 0.0), axis=0, keepdims=True)
    square = jnp.zeros((rows, 1), F32)
    for j in range(depth // CHUNK):
        cols = slice(j * CHUNK, (j + 1) * CHUNK)
        e = (dot(hidden, enc_out[:, cols]) + row[:, cols]).astype(BF)
        encoded[:, cols] = e
        e = e.astype(F32)
        square += jnp.sum(e * e, axis=1, keepdims=True)
    inv = lax.rsqrt(square / depth + 1e-05)
    for j in range(depth // CHUNK):
        cols = slice(j * CHUNK, (j + 1) * CHUNK)
        normed[:, cols] = (encoded[:, cols].astype(F32) * inv * norm_gain[:, cols]).astype(BF)
    k = dot(normed[...], w_keys[...]).astype(BF)
    keys[...] = k
    b_t[...] = k[:, :k.shape[1] // 2].T
    ws = w_step[...]
    twice = lambda v: jnp.concatenate([v, v], axis=1)
    raw = dot_t(normed[...], jnp.concatenate([ws, ws], axis=0)) + twice(step_bias[...])
    step = jax.nn.sigmoid(raw).astype(BF)
    lower = (iota((rows, rows), 0) >= iota((rows, rows), 1)).astype(F32).astype(BF)
    cum = dot(lower, step) * twice(rate[...])
    g = split_two(jnp.exp(-cum), heads)
    f = split_two(jnp.exp(cum), heads)
    grow[...] = g
    fall[...] = f
    for j in range(count):
        copies[j].wait()
        project(j, half, heads, head_dim, count, buf, normed, b_t[...], g, f[rows - EXTRA:], x_ref, xs_ref, s_ref)


def second_kernel(heads, head_dim, half_ref, normed, b_t, grow, fall, w_pair_any, x_ref, xs_ref, s_ref, buf, wsem):
    half = half_ref[0]
    count = buf.shape[0]
    copies = weight_copies(w_pair_any, buf, wsem, half, count)
    for c in copies:
        c.start()
    rows = normed.shape[0]
    for j in range(count):
        copies[j].wait()
        project(j, half, heads, head_dim, count, buf, normed, b_t[...], grow[...], fall[rows - EXTRA:], x_ref, xs_ref, s_ref)


def gate_kernel(half_ref, normed, w_pair_any, mine, other, buf, wsem):
    count = buf.shape[0] // 2
    lists = []
    for k, half in enumerate((half_ref[0], 1 - half_ref[0])):
        lists += weight_copies(w_pair_any, buf.at[pl.ds(k * count, count)], wsem.at[pl.ds(k * count, count)], half, count)
    for c in lists:
        c.start()
    for k, out in enumerate((mine, other)):
        for j in range(count):
            lists[k * count + j].wait()
            z = dot(normed[...], compact(buf.at[k * count + j], 1)).astype(BF).astype(F32)
            out[:, j * CHUNK:(j + 1) * CHUNK] = (z * jax.nn.sigmoid(z)).astype(BF)


def inner_kernel(heads, head_dim, half_ref, keys, fall, skip, x_m, x_o, xs_m, xs_o, sg_m, sg_o, u_m, u_o, v_m, v_o):
    rows = keys.shape[0]
    width = keys.shape[1] // 2
    per = CHUNK // head_dim
    count = x_m.shape[1] // CHUNK
    scores = dot_t(keys[:, width:], keys[:, :width])
    scores = jnp.where(iota((rows, rows), 0) >= iota((rows, rows), 1), scores, 0.0).astype(BF)
    value = jnp.broadcast_to(jnp.concatenate([skip[...], skip[...]], axis=1), (EXTRA, 2 * heads))
    skip_two = split_two(value, heads)
    mid = rows // 2
    groups = ((half_ref[0], x_m, xs_m, sg_m, u_m, v_m), (1 - half_ref[0], x_o, xs_o, sg_o, u_o, v_o))
    for half, x, xs, sg, u, v in groups:
        for j in range(count):
            cols = slice(j * CHUNK, (j + 1) * CHUNK)
            spread = spread_heads((half * count + j) * per, heads, head_dim)
            gain = dot(skip_two, spread)[0:1]
            top = dot(scores[:mid, :mid], xs[:mid, cols])
            low = dot(scores[mid:], xs[:, cols])
            for part, inner in ((slice(0, mid), top), (slice(mid, rows), low)):
                grown = dot(fall[part, :], spread)
                gate = sg[part, cols].astype(F32)
                u[part, cols] = (grown * gate).astype(BF)
                v[part, cols] = ((grown * inner + gain * x[part, cols].astype(F32)) * gate).astype(BF)


def mix(half, head_dim, keys, state, u, v, gain_ref, w_ref, w_copies, acc):
    width = keys.shape[1] // 2
    flat = u.shape[1]
    count = flat // CHUNK
    same = (iota((CHUNK, CHUNK), 0) // head_dim) == (iota((CHUNK, CHUNK), 1) // head_dim)
    mean = jnp.where(same, 1.0 / head_dim, 0.0).astype(BF)
    parts = []
    for j in range(count):
        cols = slice(j * CHUNK, (j + 1) * CHUNK)
        carried = dot(keys[:, width:], state[:, cols])
        g = v[:, cols].astype(F32) + u[:, cols].astype(F32) * carried
        m = dot((g * g).astype(BF), mean)
        gain = gain_ref[:, pl.ds(pl.multiple_of(half * flat + j * CHUNK, CHUNK), CHUNK)]
        parts.append((g * lax.rsqrt(m + 1e-05) * gain).astype(BF))
    mixed = jnp.concatenate(parts, axis=1)
    for c in w_copies:
        c.wait()
    return [acc(n) + dot(mixed, w_ref[:, n * CHUNK:(n + 1) * CHUNK]) for n in range(w_ref.shape[1] // CHUNK)]


def mix_kernel(head_dim, last, half_ref, keys, state, u, v, gain, base, w_any, out, w_ref, wsem):
    half = half_ref[0]
    if last:
        half = 1 - half
    flat = u.shape[1]
    start = pl.multiple_of(half * flat, flat)
    copy = pltpu.make_async_copy(w_any.at[pl.ds(start, flat), :], w_ref, wsem)
    copy.start()
    pieces = mix(half, head_dim, keys, state, u, v, gain, w_ref, [copy],
                 lambda n: base[:, n * CHUNK:(n + 1) * CHUNK].astype(F32))
    for n, piece in enumerate(pieces):
        out[:, n * CHUNK:(n + 1) * CHUNK] = piece.astype(out.dtype)


def body(frames, patch_cell, enc_in, enc_bias, enc_out, pos_table, norm_gain, w_pair, w_keys, w_step,
         step_bias, decay_code, skip_gain, out_gain, w_out):
    rows = frames.shape[0]
    pix = frames.shape[2]
    depth = enc_out.shape[1]
    heads = w_step.shape[1]
    head_dim = w_pair.shape[1] // (2 * heads)
    width = w_keys.shape[1] // 2
    flat = heads * head_dim // 2
    count = flat // CHUNK
    peers = lax.axis_size("tm")
    here = lax.axis_index("tm")
    odd = here % 2 == 1
    half = (here % 2).astype(jnp.int32).reshape(1)
    rate = (-0.0005 - 0.003 * decay_code.astype(F32)).reshape(1, heads)
    row = lambda v: v.reshape(1, -1)
    cost = lambda macs: pl.CostEstimate(flops=2 * macs, bytes_accessed=4 * 2**20, transcendentals=0)

    halves = sds((rows, flat), BF)
    message = sds((width + EXTRA, flat), BF)
    encoded, normed, keys, b_t, grow, fall, x_o, xs_o, s_o = pl.pallas_call(
        functools.partial(encode_kernel, heads, head_dim),
        out_shape=(sds((rows, depth), BF), sds((rows, depth), BF), sds((rows, 2 * width), BF), sds((width, rows), BF),
                   sds((rows, 2 * heads), BF), sds((rows, 2 * heads), BF), halves, halves, message),
        in_specs=[SM, SM] + [VM] * 8 + [ANY] * 3,
        out_specs=(VM,) * 9,
        scratch_shapes=[pltpu.VMEM((depth, depth), BF), pltpu.VMEM((EXTRA, depth), BF),
                        pltpu.VMEM((count, depth, 2 * CHUNK), BF),
                        pltpu.SemaphoreType.DMA((2,)), pltpu.SemaphoreType.DMA((count,))],
        compiler_params=params(40), name="encode",
    )(half, patch_cell, frames.reshape(rows, pix), enc_in, row(enc_bias), row(norm_gain), w_keys, w_step.T,
      row(step_bias), rate, enc_out, pos_table, w_pair)
    pair = lambda by: [(i, i ^ by) for i in range(peers)]
    got = lax.ppermute(s_o, "tm", pair(1))
    x_m, xs_m, s_m = pl.pallas_call(
        functools.partial(second_kernel, heads, head_dim),
        out_shape=(halves, halves, message),
        in_specs=[SM] + [VM] * 4 + [ANY],
        out_specs=(VM,) * 3,
        scratch_shapes=[pltpu.VMEM((count, depth, 2 * CHUNK), BF), pltpu.SemaphoreType.DMA((count,))],
        compiler_params=params(40), name="project", cost_estimate=cost(rows * depth * flat),
    )(half, normed, b_t, grow, fall, w_pair)

    def opened(packed):
        return packed[:width].astype(F32), packed[width].astype(F32)[None] + packed[width + 1].astype(F32)[None]

    def closed(state, decay):
        high = decay.astype(BF)
        low = (decay - high.astype(F32)).astype(BF)
        return jnp.concatenate([state.astype(BF), high, low, jnp.zeros((EXTRA - 2, flat), BF)], axis=0)

    mine, mine_decay = opened(s_m)
    theirs, theirs_decay = opened(got)
    even_state, even_decay = jnp.where(odd, theirs, mine), jnp.where(odd, theirs_decay, mine_decay)
    total = jnp.where(odd, mine_decay, theirs_decay) * even_state + jnp.where(odd, mine, theirs)
    total_decay = mine_decay * theirs_decay
    before, before_decay = jnp.zeros_like(total), jnp.ones_like(total_decay)

    sg_m, sg_o = pl.pallas_call(
        gate_kernel,
        out_shape=(halves, halves),
        in_specs=[SM, VM, ANY],
        out_specs=(VM,) * 2,
        scratch_shapes=[pltpu.VMEM((2 * count, depth, 2 * CHUNK), BF), pltpu.SemaphoreType.DMA((2 * count,))],
        compiler_params=params(40), name="gate", cost_estimate=cost(2 * rows * depth * flat),
    )(half, normed, w_pair)
    u_m, u_o, v_m, v_o = pl.pallas_call(
        functools.partial(inner_kernel, heads, head_dim),
        out_shape=(halves,) * 4,
        in_specs=[SM] + [VM] * 9,
        out_specs=(VM,) * 4,
        compiler_params=params(40), name="inner", cost_estimate=cost(rows * depth * flat),
    )(half, keys, fall, row(skip_gain), x_m, x_o, xs_m, xs_o, sg_m, sg_o)

    reach = 2
    while reach < peers:
        arrived, arrived_decay = opened(lax.ppermute(closed(total, total_decay), "tm", pair(reach)))
        later = (here // reach) % 2 == 1
        before = before + jnp.where(later, before_decay, 0.0) * arrived
        before_decay = before_decay * jnp.where(later, arrived_decay, 1.0)
        total = jnp.where(later, total_decay, arrived_decay) * jnp.where(later, arrived, total) + jnp.where(later, total, arrived)
        total_decay = total_decay * arrived_decay
        reach *= 2

    at_even, at_odd = before.astype(BF), (even_decay * before + even_state).astype(BF)
    state_m = jnp.where(odd, at_odd, at_even)
    state_o = lax.ppermute(jnp.where(odd, at_even, at_odd), "tm", pair(1))

    def mixed(last, state, u, v, base, kind):
        return pl.pallas_call(
            functools.partial(mix_kernel, head_dim, last),
            out_shape=sds((rows, depth), kind),
            in_specs=[SM] + [VM] * 6 + [ANY],
            out_specs=VM,
            scratch_shapes=[pltpu.VMEM((flat, depth), BF), pltpu.SemaphoreType.DMA],
            compiler_params=params(40), name="mix", cost_estimate=cost(rows * depth * flat),
        )(half, keys, state, u, v, row(out_gain), base, w_out)

    partial = mixed(False, state_m, u_m, v_m, encoded, F32)
    return mixed(True, state_o, u_o, v_o, partial, BF).reshape(rows, 1, depth)


def solution(mesh):
    placed = (P("tm", "space", None), P("space")) + (P(),) * 13
    return jax.shard_map(body, mesh=mesh, in_specs=placed, out_specs=P("tm", "space", None), check_vma=False)
```

```python
import functools

import jax
import jax.numpy as jnp
from jax import lax
from jax.experimental import pallas as pl
from jax.experimental.pallas import tpu as pltpu
from jax.sharding import PartitionSpec as P

BF = jnp.bfloat16
F32 = jnp.float32
VM = pl.BlockSpec(memory_space=pltpu.VMEM)
SM = pl.BlockSpec(memory_space=pltpu.SMEM)
ANY = pl.BlockSpec(memory_space=pl.ANY)
LANES = 128
CHUNK = 256
EXTRA = 16


def dot(a, b):
    return jnp.dot(a, b, preferred_element_type=F32)


def dot_t(a, b):
    return lax.dot_general(a, b, (((1,), (1,)), ((), ())), preferred_element_type=F32)


def iota(shape, axis):
    return lax.broadcasted_iota(jnp.int32, shape, axis)


def params(mib):
    return pltpu.CompilerParams(vmem_limit_bytes=mib * 2**20)


def sds(shape, dtype):
    return jax.ShapeDtypeStruct(shape, dtype)


def spread_heads(first_head, heads, head_dim):
    row = iota((2 * heads, CHUNK), 0)
    lane = iota((2 * heads, CHUNK), 1)
    row = jnp.where(row < heads, row, row - heads)
    return (row == first_head + lane // head_dim).astype(F32).astype(BF)


def split_two(value, heads):
    high = value.astype(BF).astype(F32)
    return jnp.where(iota(value.shape, 1) < heads, high, value - high).astype(BF)


def pick_half(tile_a, tile_b, part):
    half = LANES // 2
    low = iota(tile_a.shape, 1) < half
    if part == 0:
        return jnp.where(low, tile_a, pltpu.roll(tile_b, half, 1))
    return jnp.where(low, pltpu.roll(tile_a, half, 1), tile_b)


def compact(ref, part):
    tiles = [ref[:, i * LANES:(i + 1) * LANES] for i in range(2 * CHUNK // LANES)]
    pairs = [pick_half(tiles[i], tiles[i + 1], part) for i in range(0, len(tiles), 2)]
    return jnp.concatenate(pairs, axis=1)


def weight_copies(w_ref, buf, sem, half, count):
    copies = []
    for j in range(count):
        start = pl.multiple_of((half * count + j) * 2 * CHUNK, 2 * CHUNK)
        copies.append(pltpu.make_async_copy(w_ref.at[:, pl.ds(start, 2 * CHUNK)], buf.at[j], sem.at[j]))
    return copies


def project(j, half, heads, head_dim, count, buf, normed, b_t, grow, fall_end, x_ref, xs_ref, s_ref):
    width = b_t.shape[0]
    per = CHUNK // head_dim
    first = (half * count + j) * per
    cols = slice(j * CHUNK, (j + 1) * CHUNK)
    spread = spread_heads(first, heads, head_dim)
    x = dot(normed[...], compact(buf.at[j], 0)).astype(BF)
    scaled = (x.astype(F32) * dot(grow, spread)).astype(BF)
    x_ref[:, cols] = x
    xs_ref[:, cols] = scaled
    decay = dot(fall_end, spread)[EXTRA - 1:EXTRA]
    s_ref[0:width, cols] = (dot(b_t, scaled) * decay).astype(BF)
    high = decay.astype(BF).astype(F32)
    row = iota((EXTRA, CHUNK), 0)
    s_ref[width:width + EXTRA, cols] = jnp.where(row == 0, high, jnp.where(row == 1, decay - high, 0.0)).astype(BF)


def start_all(pairs, sem):
    copies = [pltpu.make_async_copy(src, dst, sem.at[i]) for i, (src, dst) in enumerate(pairs)]
    for c in copies:
        c.start()
    return copies


def encode_kernel(heads, head_dim, here_ref, cell_ref, frames_any, enc_in_any, bias_any, enc_out_any, pos_any, gain_any,
                  w_keys_any, w_step_any, step_bias_any, code_any, w_pair_any,
                  encoded, normed, keys, b_t, grow, fall, x_ref, xs_ref, s_ref,
                  frames, enc_in, bias, enc_out, pos, norm_gain, w_keys, w_step, step_bias, code, buf, sem, wsem):
    half = 1 - here_ref[0] % 2
    count = buf.shape[0]
    cell = cell_ref[0]
    base = pl.multiple_of((cell // EXTRA) * EXTRA, EXTRA)
    small = start_all([(frames_any, frames), (enc_in_any, enc_in), (bias_any, bias), (enc_out_any, enc_out),
                       (pos_any.at[pl.ds(base, EXTRA), :], pos), (gain_any, norm_gain), (w_keys_any, w_keys),
                       (w_step_any, w_step), (step_bias_any, step_bias), (code_any, code)], sem)
    copies = weight_copies(w_pair_any, buf, wsem, half, count)
    for c in copies:
        c.start()
    rows, depth = encoded.shape
    lower = (iota((rows, rows), 0) >= iota((rows, rows), 1)).astype(F32).astype(BF)
    for c in small[:3]:
        c.wait()
    hidden = []
    for j in range(depth // CHUNK):
        cols = slice(j * CHUNK, (j + 1) * CHUNK)
        h = dot(frames[...], enc_in[:, cols]) + bias[:, cols]
        hidden.append(jax.nn.gelu(h, approximate=True).astype(BF))
    hidden = jnp.concatenate(hidden, axis=1)
    for c in small[3:]:
        c.wait()
    row = jnp.sum(jnp.where(iota(pos.shape, 0) == cell - base, pos[...].astype(F32), 0.0), axis=0, keepdims=True)
    square = jnp.zeros((rows, 1), F32)
    for j in range(depth // CHUNK):
        cols = slice(j * CHUNK, (j + 1) * CHUNK)
        e = (dot(hidden, enc_out[:, cols]) + row[:, cols]).astype(BF)
        encoded[:, cols] = e
        e = e.astype(F32)
        square += jnp.sum(e * e, axis=1, keepdims=True)
    inv = lax.rsqrt(square / depth + 1e-05)
    for j in range(depth // CHUNK):
        cols = slice(j * CHUNK, (j + 1) * CHUNK)
        normed[:, cols] = (encoded[:, cols].astype(F32) * inv * norm_gain[:, cols]).astype(BF)
    k = dot(normed[...], w_keys[...]).astype(BF)
    keys[...] = k
    b_t[...] = k[:, :k.shape[1] // 2].T
    ws = w_step[...]
    twice = lambda v: jnp.concatenate([v, v], axis=1)
    raw = dot_t(normed[...], jnp.concatenate([ws, ws], axis=0)) + twice(step_bias[...])
    step = jax.nn.sigmoid(raw).astype(BF)
    cum = dot(lower, step) * twice(-0.0005 - 0.003 * code[...].astype(F32))
    g = split_two(jnp.exp(-cum), heads)
    f = split_two(jnp.exp(cum), heads)
    grow[...] = g
    fall[...] = f
    for j in range(count):
        copies[j].wait()
        project(j, half, heads, head_dim, count, buf, normed, b_t[...], g, f[rows - EXTRA:], x_ref, xs_ref, s_ref)


def second_kernel(heads, head_dim, here_ref, normed, b_t, grow, fall, w_pair_any, x_ref, xs_ref, s_ref, buf, wsem):
    half = here_ref[0] % 2
    count = buf.shape[0]
    copies = weight_copies(w_pair_any, buf, wsem, half, count)
    for c in copies:
        c.start()
    rows = normed.shape[0]
    for j in range(count):
        copies[j].wait()
        project(j, half, heads, head_dim, count, buf, normed, b_t[...], grow[...], fall[rows - EXTRA:], x_ref, xs_ref, s_ref)


def opened(ref):
    width = ref.shape[0] - EXTRA
    tail = ref[width:, :].astype(F32)
    return ref[:width, :].astype(F32), tail[0:1] + tail[1:2]


def close(ref, state, decay):
    width = ref.shape[0] - EXTRA
    ref[:width, :] = state.astype(BF)
    high = decay.astype(BF).astype(F32)
    row = iota((EXTRA, decay.shape[1]), 0)
    ref[width:, :] = jnp.where(row == 0, high, jnp.where(row == 1, decay - high, 0.0)).astype(BF)


def total_kernel(here_ref, mine_ref, got_ref, total_ref):
    mine, mine_decay = opened(mine_ref)
    got, got_decay = opened(got_ref)

    @pl.when(here_ref[0] % 2 == 1)
    def _():
        close(total_ref, mine_decay * got + mine, mine_decay * got_decay)

    @pl.when(here_ref[0] % 2 == 0)
    def _():
        close(total_ref, got_decay * mine + got, mine_decay * got_decay)


def step_kernel(first, reach, here_ref, total_ref, got_ref, before_ref, new_before_ref, new_total_ref):
    later = (here_ref[0] // reach) % 2 == 1
    got, got_decay = opened(got_ref)
    total, total_decay = opened(total_ref)

    @pl.when(later)
    def _():
        if first:
            close(new_before_ref, got, got_decay)
        else:
            before, before_decay = opened(before_ref)
            close(new_before_ref, before + before_decay * got, before_decay * got_decay)
        close(new_total_ref, total_decay * got + total, total_decay * got_decay)

    @pl.when(jnp.logical_not(later))
    def _():
        if first:
            close(new_before_ref, jnp.zeros_like(got), jnp.ones_like(got_decay))
        else:
            new_before_ref[...] = before_ref[...]
        close(new_total_ref, got_decay * total + got, total_decay * got_decay)


def last_kernel(reach, here_ref, got_ref, before_ref, mine_ref, first_ref, keep_ref, send_ref):
    width = keep_ref.shape[0]
    later = (here_ref[0] // reach) % 2 == 1
    got, _ = opened(got_ref)
    before, before_decay = opened(before_ref)
    before = before + jnp.where(later, before_decay, 0.0) * got

    @pl.when(here_ref[0] % 2 == 1)
    def _():
        state, decay = opened(first_ref)
        keep_ref[...] = (decay * before + state).astype(BF)
        send_ref[...] = before.astype(BF)

    @pl.when(here_ref[0] % 2 == 0)
    def _():
        state, decay = opened(mine_ref)
        send_ref[...] = (decay * before + state).astype(BF)
        keep_ref[...] = before.astype(BF)


def gate_kernel(here_ref, normed, w_pair_any, mine, other, buf, wsem):
    count = buf.shape[0] // 2
    lists = []
    for k, half in enumerate((here_ref[0] % 2, 1 - here_ref[0] % 2)):
        lists += weight_copies(w_pair_any, buf.at[pl.ds(k * count, count)], wsem.at[pl.ds(k * count, count)], half, count)
    for c in lists:
        c.start()
    for k, out in enumerate((mine, other)):
        for j in range(count):
            lists[k * count + j].wait()
            z = dot(normed[...], compact(buf.at[k * count + j], 1)).astype(BF).astype(F32)
            out[:, j * CHUNK:(j + 1) * CHUNK] = (z * jax.nn.sigmoid(z)).astype(BF)


def inner_kernel(heads, head_dim, here_ref, keys, fall, skip_any, x_m, x_o, xs_m, xs_o, sg_m, sg_o, u_m, u_o, v_m, v_o, skip, sem):
    copy = pltpu.make_async_copy(skip_any, skip, sem)
    copy.start()
    rows = keys.shape[0]
    width = keys.shape[1] // 2
    per = CHUNK // head_dim
    count = x_m.shape[1] // CHUNK
    scores = dot_t(keys[:, width:], keys[:, :width])
    scores = jnp.where(iota((rows, rows), 0) >= iota((rows, rows), 1), scores, 0.0).astype(BF)
    copy.wait()
    value = jnp.broadcast_to(jnp.concatenate([skip[...], skip[...]], axis=1), (EXTRA, 2 * heads))
    skip_two = split_two(value, heads)
    mid = rows // 2
    groups = ((here_ref[0] % 2, x_m, xs_m, sg_m, u_m, v_m), (1 - here_ref[0] % 2, x_o, xs_o, sg_o, u_o, v_o))
    for half, x, xs, sg, u, v in groups:
        for j in range(count):
            cols = slice(j * CHUNK, (j + 1) * CHUNK)
            spread = spread_heads((half * count + j) * per, heads, head_dim)
            gain = dot(skip_two, spread)[0:1]
            top = dot(scores[:mid, :mid], xs[:mid, cols])
            low = dot(scores[mid:], xs[:, cols])
            for part, inner in ((slice(0, mid), top), (slice(mid, rows), low)):
                grown = dot(fall[part, :], spread)
                gate = sg[part, cols].astype(F32)
                u[part, cols] = (grown * gate).astype(BF)
                v[part, cols] = ((grown * inner + gain * x[part, cols].astype(F32)) * gate).astype(BF)


def mix_kernel(head_dim, last, here_ref, keys, state, u, v, base, gain_any, w_any, out, gain_ref, w_ref, sem):
    half = here_ref[0] % 2
    if last:
        half = 1 - half
    width = keys.shape[1] // 2
    flat = u.shape[1]
    start = pl.multiple_of(half * flat, flat)
    copies = start_all([(gain_any.at[:, pl.ds(start, flat)], gain_ref), (w_any.at[pl.ds(start, flat), :], w_ref)], sem)
    same = (iota((CHUNK, CHUNK), 0) // head_dim) == (iota((CHUNK, CHUNK), 1) // head_dim)
    mean = jnp.where(same, 1.0 / head_dim, 0.0).astype(BF)
    parts = []
    for j in range(flat // CHUNK):
        cols = slice(j * CHUNK, (j + 1) * CHUNK)
        carried = dot(keys[:, width:], state[:, cols])
        g = v[:, cols].astype(F32) + u[:, cols].astype(F32) * carried
        m = dot((g * g).astype(BF), mean)
        if j == 0:
            copies[0].wait()
        parts.append((g * lax.rsqrt(m + 1e-05) * gain_ref[:, cols]).astype(BF))
    mixed = jnp.concatenate(parts, axis=1)
    copies[1].wait()
    for n in range(w_ref.shape[1] // CHUNK):
        cols = slice(n * CHUNK, (n + 1) * CHUNK)
        out[:, cols] = (base[:, cols].astype(F32) + dot(mixed, w_ref[:, cols])).astype(out.dtype)


def body(frames, patch_cell, enc_in, enc_bias, enc_out, pos_table, norm_gain, w_pair, w_keys, w_step,
         step_bias, decay_code, skip_gain, out_gain, w_out):
    rows = frames.shape[0]
    pix = frames.shape[2]
    depth = enc_out.shape[1]
    heads = w_step.shape[1]
    head_dim = w_pair.shape[1] // (2 * heads)
    width = w_keys.shape[1] // 2
    flat = heads * head_dim // 2
    count = flat // CHUNK
    peers = lax.axis_size("tm")
    here = lax.axis_index("tm").astype(jnp.int32).reshape(1)
    row = lambda v: v.reshape(1, -1)
    cost = lambda macs: pl.CostEstimate(flops=2 * macs, bytes_accessed=4 * 2**20, transcendentals=0)
    far = lambda v: pltpu.with_memory_space_constraint(v, pltpu.HBM)
    near = lambda shape, dtype=BF: pltpu.VMEM(shape, dtype)
    sems = lambda n: pltpu.SemaphoreType.DMA((n,))
    pair = lambda by: [(i, i ^ by) for i in range(peers)]

    def call(kernel, name, outs, ins, scratch=(), macs=0):
        specs = [spec for spec, _ in ins]
        return pl.pallas_call(kernel, out_shape=tuple(outs), in_specs=specs, out_specs=(VM,) * len(outs),
                              scratch_shapes=list(scratch), compiler_params=params(24), name=name,
                              cost_estimate=cost(macs))(*[v for _, v in ins])

    vm = lambda *vs: [(VM, v) for v in vs]
    hbm = lambda *vs: [(pl.BlockSpec(memory_space=pltpu.HBM), far(v)) for v in vs]
    where = [(SM, here)]
    w_pair, w_out, gain_row = far(w_pair), far(w_out), row(out_gain)

    halves, message = near((rows, flat)), near((width + EXTRA, flat))
    encoded, normed, keys, b_t, grow, fall, x_o, xs_o, s_o = call(
        functools.partial(encode_kernel, heads, head_dim), "encode",
        (near((rows, depth)), near((rows, depth)), near((rows, 2 * width)), near((width, rows)),
         near((rows, 2 * heads)), near((rows, 2 * heads)), halves, halves, message),
        where + [(SM, patch_cell)] + hbm(frames.reshape(rows, pix), enc_in, row(enc_bias), enc_out, pos_table, row(norm_gain),
                                         w_keys, w_step.T, row(step_bias), row(decay_code), w_pair),
        [near((rows, pix)), near((pix, depth)), near((1, depth), F32), near((depth, depth)), near((EXTRA, depth)),
         near((1, depth), F32), near((depth, 2 * width)), near((heads, depth)), near((1, heads), F32),
         near((1, heads), jnp.int32), near((count, depth, 2 * CHUNK)), sems(10), sems(count)],
        rows * depth * depth)
    got_first = lax.ppermute(s_o, "tm", pair(1))
    x_m, xs_m, s_m = call(
        functools.partial(second_kernel, heads, head_dim), "project", (halves, halves, message),
        where + vm(normed, b_t, grow, fall) + hbm(w_pair),
        [near((count, depth, 2 * CHUNK)), sems(count)], rows * depth * flat)
    total, = call(total_kernel, "total", (message,), where + vm(s_m, got_first))

    sg_m, sg_o = call(gate_kernel, "gate", (halves, halves), where + vm(normed) + hbm(w_pair),
                      [near((2 * count, depth, 2 * CHUNK)), sems(2 * count)], 2 * rows * depth * flat)
    u_m, u_o, v_m, v_o = call(
        functools.partial(inner_kernel, heads, head_dim), "inner", (halves,) * 4,
        where + vm(keys, fall) + hbm(row(skip_gain)) + vm(x_m, x_o, xs_m, xs_o, sg_m, sg_o),
        [near((1, heads), F32), pltpu.SemaphoreType.DMA], rows * rows * flat * 2)

    before = total
    ready = [sg_m, u_m]
    reach = 2
    while reach * 2 < peers:
        got = lax.ppermute(total, "tm", pair(reach))
        if ready:
            got, _ = lax.optimization_barrier((got, ready.pop(0)))
        before, total = call(functools.partial(step_kernel, reach == 2, reach), "step", (message, message),
                             where + vm(total, got, before))
        reach *= 2
    got = lax.ppermute(total, "tm", pair(reach))
    for value in ready:
        got, _ = lax.optimization_barrier((got, value))
    state_m, send = call(functools.partial(last_kernel, reach), "last", (near((width, flat)),) * 2,
                         where + vm(got, before, s_m, got_first))
    state_o = lax.ppermute(send, "tm", pair(1))

    def mixed(last, state, u, v, base, kind):
        return call(functools.partial(mix_kernel, head_dim, last), "mix",
                    (sds((rows, depth), kind) if last else near((rows, depth), kind),),
                    where + vm(keys, state, u, v, base) + hbm(gain_row, w_out),
                    [near((1, flat), F32), near((flat, depth)), sems(2)], rows * depth * flat)[0]

    partial = mixed(False, state_m, u_m, v_m, encoded, F32)
    return mixed(True, state_o, u_o, v_o, partial, BF).reshape(rows, 1, depth)


def solution(mesh):
    placed = (P("tm", "space", None), P("space")) + (P(),) * 13
    return jax.shard_map(body, mesh=mesh, in_specs=placed, out_specs=P("tm", "space", None), check_vma=False)
```

```python
import functools

import jax
import jax.numpy as jnp
from jax import lax
from jax.experimental import pallas as pl
from jax.experimental.pallas import tpu as pltpu
from jax.sharding import PartitionSpec as P

BF = jnp.bfloat16
F32 = jnp.float32
VM = pl.BlockSpec(memory_space=pltpu.VMEM)
SM = pl.BlockSpec(memory_space=pltpu.SMEM)
ANY = pl.BlockSpec(memory_space=pl.ANY)
LANES = 128
CHUNK = 256
EXTRA = 16


def dot(a, b):
    return jnp.dot(a, b, preferred_element_type=F32)


def dot_t(a, b):
    return lax.dot_general(a, b, (((1,), (1,)), ((), ())), preferred_element_type=F32)


def iota(shape, axis):
    return lax.broadcasted_iota(jnp.int32, shape, axis)


def params(mib):
    return pltpu.CompilerParams(vmem_limit_bytes=mib * 2**20)


def sds(shape, dtype):
    return jax.ShapeDtypeStruct(shape, dtype)


def spread_heads(first_head, heads, head_dim):
    row = iota((2 * heads, CHUNK), 0)
    lane = iota((2 * heads, CHUNK), 1)
    row = jnp.where(row < heads, row, row - heads)
    return (row == first_head + lane // head_dim).astype(F32).astype(BF)


def split_two(value, heads):
    high = value.astype(BF).astype(F32)
    return jnp.where(iota(value.shape, 1) < heads, high, value - high).astype(BF)


def pick_half(tile_a, tile_b, part):
    half = LANES // 2
    low = iota(tile_a.shape, 1) < half
    if part == 0:
        return jnp.where(low, tile_a, pltpu.roll(tile_b, half, 1))
    return jnp.where(low, pltpu.roll(tile_a, half, 1), tile_b)


def compact(ref, j, part):
    start = j * 2 * CHUNK
    tiles = [ref[:, start + i:start + i + LANES] for i in range(0, 2 * CHUNK, LANES)]
    pairs = [pick_half(tiles[i], tiles[i + 1], part) for i in range(0, len(tiles), 2)]
    return jnp.concatenate(pairs, axis=1)


def project(half, group, heads, head_dim, w, normed, b_t, grow, fall_end, x_ref, xs_ref, s_ref):
    width = b_t.shape[0]
    size = x_ref.shape[1]
    first = (half * 2 + group) * (size // head_dim)
    for j in range(size // CHUNK):
        cols = slice(j * CHUNK, (j + 1) * CHUNK)
        spread = spread_heads(first + j * (CHUNK // head_dim), heads, head_dim)
        x = dot(normed[...], compact(w, j, 0)).astype(BF)
        scaled = (x.astype(F32) * dot(grow, spread)).astype(BF)
        x_ref[:, cols] = x
        xs_ref[:, cols] = scaled
        decay = dot(fall_end, spread)[EXTRA - 1:EXTRA]
        s_ref[0:width, cols] = (dot(b_t, scaled) * decay).astype(BF)
        s_ref[width:width + EXTRA, cols] = decay_rows(decay)


def decay_rows(decay):
    high = decay.astype(BF).astype(F32)
    row = iota((EXTRA, decay.shape[1]), 0)
    return jnp.where(row == 0, high, jnp.where(row == 1, decay - high, 0.0)).astype(BF)


def start_all(pairs, sem):
    copies = [pltpu.make_async_copy(src, dst, sem.at[i]) for i, (src, dst) in enumerate(pairs)]
    for c in copies:
        c.start()
    return copies


def encode_kernel(heads, head_dim, here_ref, cell_ref, frames_any, enc_in_any, bias_any, enc_out_any, pos_any, gain_any,
                  w_keys_any, w_step_any, step_bias_any, code_any, w_pair_any,
                  encoded, normed, keys, b_t, grow, fall, x_ref, xs_ref, s_ref, w_o1, w_o2, w_m1, w_m2,
                  frames, enc_in, bias, enc_out, pos, norm_gain, w_keys, w_step, step_bias, code, sem, wsem):
    half = 1 - here_ref[0] % 2
    cell = cell_ref[0]
    base = pl.multiple_of((cell // EXTRA) * EXTRA, EXTRA)
    small = start_all([(frames_any, frames), (enc_in_any, enc_in), (bias_any, bias), (enc_out_any, enc_out),
                       (pos_any.at[pl.ds(base, EXTRA), :], pos), (gain_any, norm_gain), (w_keys_any, w_keys),
                       (w_step_any, w_step), (step_bias_any, step_bias), (code_any, code)], sem)
    size = w_o1.shape[1]
    columns = lambda which, group: w_pair_any.at[:, pl.ds(pl.multiple_of((which * 2 + group) * size, size), size)]
    rows, depth = encoded.shape
    lower = (iota((rows, rows), 0) >= iota((rows, rows), 1)).astype(F32).astype(BF)
    for c in small[:3]:
        c.wait()
    big = start_all([(columns(half, 0), w_o1), (columns(1 - half, 0), w_m1), (columns(half, 1), w_o2),
                     (columns(1 - half, 1), w_m2)], wsem)
    hidden = []
    for j in range(depth // CHUNK):
        cols = slice(j * CHUNK, (j + 1) * CHUNK)
        h = dot(frames[...], enc_in[:, cols]) + bias[:, cols]
        hidden.append(jax.nn.gelu(h, approximate=True).astype(BF))
    hidden = jnp.concatenate(hidden, axis=1)
    for c in small[3:]:
        c.wait()
    row = jnp.sum(jnp.where(iota(pos.shape, 0) == cell - base, pos[...].astype(F32), 0.0), axis=0, keepdims=True)
    square = jnp.zeros((rows, 1), F32)
    for j in range(depth // CHUNK):
        cols = slice(j * CHUNK, (j + 1) * CHUNK)
        e = (dot(hidden, enc_out[:, cols]) + row[:, cols]).astype(BF)
        encoded[:, cols] = e
        e = e.astype(F32)
        square += jnp.sum(e * e, axis=1, keepdims=True)
    inv = lax.rsqrt(square / depth + 1e-05)
    for j in range(depth // CHUNK):
        cols = slice(j * CHUNK, (j + 1) * CHUNK)
        normed[:, cols] = (encoded[:, cols].astype(F32) * inv * norm_gain[:, cols]).astype(BF)
    k = dot(normed[...], w_keys[...]).astype(BF)
    keys[...] = k
    b_t[...] = k[:, :k.shape[1] // 2].T
    ws = w_step[...]
    twice = lambda v: jnp.concatenate([v, v], axis=1)
    raw = dot_t(normed[...], jnp.concatenate([ws, ws], axis=0)) + twice(step_bias[...])
    step = jax.nn.sigmoid(raw).astype(BF)
    cum = dot(lower, step) * twice(-0.0005 - 0.003 * code[...].astype(F32))
    g = split_two(jnp.exp(-cum), heads)
    f = split_two(jnp.exp(cum), heads)
    grow[...] = g
    fall[...] = f
    big[0].wait()
    project(half, 0, heads, head_dim, w_o1, normed, b_t[...], g, f[rows - EXTRA:], x_ref, xs_ref, s_ref)
    for c in big[1:]:
        c.wait()


def project_kernel(heads, head_dim, own, group, here_ref, normed, b_t, grow, fall, w, x_ref, xs_ref, s_ref):
    half = (here_ref[0] + 1 - own) % 2
    rows = normed.shape[0]
    project(half, group, heads, head_dim, w, normed, b_t[...], grow[...], fall[rows - EXTRA:], x_ref, xs_ref, s_ref)


def opened(ref):
    width = ref.shape[0] - EXTRA
    tail = ref[width:, :].astype(F32)
    return ref[:width, :].astype(F32), tail[0:1] + tail[1:2]


def close(ref, state, decay):
    width = ref.shape[0] - EXTRA
    ref[:width, :] = state.astype(BF)
    ref[width:, :] = decay_rows(decay)


def total_kernel(here_ref, mine_ref, got_ref, total_ref):
    mine, mine_decay = opened(mine_ref)
    got, got_decay = opened(got_ref)

    @pl.when(here_ref[0] % 2 == 1)
    def _():
        close(total_ref, mine_decay * got + mine, mine_decay * got_decay)

    @pl.when(here_ref[0] % 2 == 0)
    def _():
        close(total_ref, got_decay * mine + got, mine_decay * got_decay)


def step_kernel(first, reach, here_ref, total_ref, got_ref, before_ref, new_before_ref, new_total_ref):
    later = (here_ref[0] // reach) % 2 == 1
    got, got_decay = opened(got_ref)
    total, total_decay = opened(total_ref)

    @pl.when(later)
    def _():
        if first:
            close(new_before_ref, got, got_decay)
        else:
            before, before_decay = opened(before_ref)
            close(new_before_ref, before + before_decay * got, before_decay * got_decay)
        close(new_total_ref, total_decay * got + total, total_decay * got_decay)

    @pl.when(jnp.logical_not(later))
    def _():
        if first:
            close(new_before_ref, jnp.zeros_like(got), jnp.ones_like(got_decay))
        else:
            new_before_ref[...] = before_ref[...]
        close(new_total_ref, got_decay * total + got, total_decay * got_decay)


def last_kernel(reach, here_ref, got_ref, before_ref, mine_ref, first_ref, keep_ref, send_ref):
    width = keep_ref.shape[0]
    later = (here_ref[0] // reach) % 2 == 1
    got, _ = opened(got_ref)
    before, before_decay = opened(before_ref)
    before = before + jnp.where(later, before_decay, 0.0) * got

    @pl.when(here_ref[0] % 2 == 1)
    def _():
        state, decay = opened(first_ref)
        keep_ref[...] = (decay * before + state).astype(BF)
        send_ref[...] = before.astype(BF)

    @pl.when(here_ref[0] % 2 == 0)
    def _():
        state, decay = opened(mine_ref)
        send_ref[...] = (decay * before + state).astype(BF)
        keep_ref[...] = before.astype(BF)


def inner_kernel(heads, head_dim, own, group, here_ref, normed, keys, fall, skip_any, w_out_any, w, x, xs,
                 u, v, w_rows, skip, sem):
    half = (here_ref[0] + 1 - own) % 2
    rows = keys.shape[0]
    width = keys.shape[1] // 2
    size = x.shape[1]
    start = pl.multiple_of((half * 2 + group) * size, size)
    copies = start_all([(skip_any, skip), (w_out_any.at[pl.ds(start, size), :], w_rows)], sem)
    scores = dot_t(keys[:, width:], keys[:, :width])
    scores = jnp.where(iota((rows, rows), 0) >= iota((rows, rows), 1), scores, 0.0).astype(BF)
    mid = rows // 2
    copies[0].wait()
    both = jnp.broadcast_to(jnp.concatenate([skip[...], skip[...]], axis=1), (EXTRA, 2 * heads))
    skip_two = split_two(both, heads)
    first = (half * 2 + group) * (size // head_dim)
    for j in range(size // CHUNK):
        cols = slice(j * CHUNK, (j + 1) * CHUNK)
        z = dot(normed[...], compact(w, j, 1)).astype(BF).astype(F32)
        gate = z * jax.nn.sigmoid(z)
        spread = spread_heads(first + j * (CHUNK // head_dim), heads, head_dim)
        gain = dot(skip_two, spread)[0:1]
        grown = dot(fall[...], spread)
        u[:, cols] = (grown * gate).astype(BF)
        top = dot(scores[:mid, :mid], xs[:mid, cols])
        low = dot(scores[mid:], xs[:, cols])
        for part, inner in ((slice(0, mid), top), (slice(mid, rows), low)):
            v[part, cols] = ((grown[part] * inner + gain * x[part, cols].astype(F32)) * gate[part]).astype(BF)
    copies[1].wait()


def mix_kernel(head_dim, places, here_ref, keys, base, gain_any, *refs):
    many = len(places)
    states, us, vs, ws = (refs[i * many:(i + 1) * many] for i in range(4))
    out, gain_ref, sem = refs[4 * many:]
    width = keys.shape[1] // 2
    size = us[0].shape[1]
    starts = [((here_ref[0] + 1 - own) % 2 * 2 + group) * size for own, group in places]
    copies = start_all([(gain_any.at[:, pl.ds(pl.multiple_of(s, size), size)], gain_ref.at[pl.ds(i, 1), :])
                        for i, s in enumerate(starts)], sem)
    same = (iota((CHUNK, CHUNK), 0) // head_dim) == (iota((CHUNK, CHUNK), 1) // head_dim)
    mean = jnp.where(same, 1.0 / head_dim, 0.0).astype(BF)
    work = []
    for state, u, v in zip(states, us, vs):
        for j in range(size // CHUNK):
            cols = slice(j * CHUNK, (j + 1) * CHUNK)
            carried = dot(keys[:, width:], state[:, cols])
            g = v[:, cols].astype(F32) + u[:, cols].astype(F32) * carried
            work.append((g, dot((g * g).astype(BF), mean)))
    for c in copies:
        c.wait()
    mixed = []
    for i in range(many):
        row = gain_ref[i:i + 1, :]
        parts = []
        for j in range(size // CHUNK):
            g, m = work[i * (size // CHUNK) + j]
            parts.append((g * lax.rsqrt(m + 1e-05) * row[:, j * CHUNK:(j + 1) * CHUNK]).astype(BF))
        mixed.append(jnp.concatenate(parts, axis=1))
    for n in range(out.shape[1] // CHUNK):
        cols = slice(n * CHUNK, (n + 1) * CHUNK)
        total = base[:, cols].astype(F32)
        for part, w in zip(mixed, ws):
            total = total + dot(part, w[:, cols])
        out[:, cols] = total.astype(out.dtype)


def body(frames, patch_cell, enc_in, enc_bias, enc_out, pos_table, norm_gain, w_pair, w_keys, w_step,
         step_bias, decay_code, skip_gain, out_gain, w_out):
    rows = frames.shape[0]
    pix = frames.shape[2]
    depth = enc_out.shape[1]
    heads = w_step.shape[1]
    head_dim = w_pair.shape[1] // (2 * heads)
    width = w_keys.shape[1] // 2
    size = heads * head_dim // 4
    peers = lax.axis_size("tm")
    here = lax.axis_index("tm").astype(jnp.int32).reshape(1)
    row = lambda v: v.reshape(1, -1)
    far = lambda v: pltpu.with_memory_space_constraint(v, pltpu.HBM)
    near = lambda shape, dtype=BF: pltpu.VMEM(shape, dtype)
    sems = lambda n: pltpu.SemaphoreType.DMA((n,))
    pair = lambda by: [(i, i ^ by) for i in range(peers)]
    after = lambda value, *first: lax.optimization_barrier((value,) + first)[0]

    def call(kernel, name, outs, ins, scratch=(), macs=0):
        specs = [spec for spec, _ in ins]
        cost = pl.CostEstimate(flops=2 * macs, bytes_accessed=4 * 2**20, transcendentals=0)
        return pl.pallas_call(kernel, out_shape=tuple(outs), in_specs=specs, out_specs=(VM,) * len(outs),
                              scratch_shapes=list(scratch), compiler_params=params(24), name=name,
                              cost_estimate=cost)(*[v for _, v in ins])

    vm = lambda *vs: [(VM, v) for v in vs]
    hbm = lambda *vs: [(pl.BlockSpec(memory_space=pltpu.HBM), far(v)) for v in vs]
    where = [(SM, here)]

    part, message, weight = near((rows, size)), near((width + EXTRA, size)), near((depth, 2 * size))
    encoded, normed, keys, b_t, grow, fall, x_o1, xs_o1, s_o1, w_o1, w_o2, w_m1, w_m2 = call(
        functools.partial(encode_kernel, heads, head_dim), "encode",
        (near((rows, depth)), near((rows, depth)), near((rows, 2 * width)), near((width, rows)),
         near((rows, 2 * heads)), near((rows, 2 * heads)), part, part, message) + (weight,) * 4,
        where + [(SM, patch_cell)] + hbm(frames.reshape(rows, pix), enc_in, row(enc_bias), enc_out, pos_table, row(norm_gain),
                                         w_keys, w_step.T, row(step_bias), row(decay_code), w_pair),
        [near((rows, pix)), near((pix, depth)), near((1, depth), F32), near((depth, depth)), near((EXTRA, depth)),
         near((1, depth), F32), near((depth, 2 * width)), near((heads, depth)), near((1, heads), F32),
         near((1, heads), jnp.int32), sems(10), sems(4)],
        rows * depth * depth)

    def projected(own, group, w):
        return call(functools.partial(project_kernel, heads, head_dim, own, group), "project", (part, part, message),
                    where + vm(normed, b_t, grow, fall, w), (), rows * depth * size)

    def inner(own, group, w, x, xs):
        return call(functools.partial(inner_kernel, heads, head_dim, own, group), "inner",
                    (part, part, near((size, depth))),
                    where + vm(normed, keys, fall) + hbm(skip_row, w_out) + vm(w, x, xs),
                    [near((1, heads), F32), sems(2)], rows * depth * size)

    def mixed(places, base, kind, *groups):
        states, us, vs, ws = zip(*groups)
        last = kind == BF
        return call(functools.partial(mix_kernel, head_dim, places), "mix",
                    (sds((rows, depth), kind) if last else near((rows, depth), kind),),
                    where + vm(keys, base) + hbm(gain_row) + vm(*states, *us, *vs, *ws),
                    [near((len(places), size), F32), sems(len(places))], len(places) * rows * depth * size)[0]

    skip_row, gain_row = row(skip_gain), row(out_gain)
    got_1 = lax.ppermute(s_o1, "tm", pair(1))
    x_m1, xs_m1, s_m1 = projected(1, 0, w_m1)
    total_1, = call(total_kernel, "total", (message,), where + vm(s_m1, got_1))
    x_o2, xs_o2, s_o2 = projected(0, 1, after(w_o2, total_1))
    got_2 = lax.ppermute(s_o2, "tm", pair(1))
    x_m2, xs_m2, s_m2 = projected(1, 1, w_m2)
    total_2, = call(total_kernel, "total", (message,), where + vm(s_m2, got_2))

    todo = [(0, 0, w_o1, x_o1, xs_o1), (1, 0, w_m1, x_m1, xs_m1), (1, 1, w_m2, x_m2, xs_m2), (0, 1, w_o2, x_o2, xs_o2)]
    done = {}
    totals, befores = [total_1, total_2], [total_1, total_2]
    gots = [lax.ppermute(total_1, "tm", pair(2)), lax.ppermute(total_2, "tm", pair(2))]
    stamp = total_2
    reach = 2
    while reach * 2 < peers:
        for i in range(2):
            if todo:
                own, group, w, x, xs = todo.pop(0)
                done[own, group] = inner(own, group, w, after(x, stamp), xs)
                gots[i] = after(gots[i], done[own, group][0])
            befores[i], totals[i] = call(functools.partial(step_kernel, reach == 2, reach), "step", (message, message),
                                         where + vm(totals[i], gots[i], befores[i]))
            stamp = totals[i]
            gots[i] = lax.ppermute(totals[i], "tm", pair(2 * reach))
        reach *= 2
    for own, group, w, x, xs in todo:
        done[own, group] = inner(own, group, w, after(x, stamp), xs)
        stamp = done[own, group][0]

    def last(i, got, mine, first):
        keep, send = call(functools.partial(last_kernel, reach), "last", (near((width, size)),) * 2,
                          where + vm(got, befores[i], mine, first))
        return keep, lax.ppermute(send, "tm", pair(1))

    keep_1, sent_1 = last(0, after(gots[0], stamp), s_m1, got_1)
    mix_1 = mixed(((1, 0),), encoded, F32, (keep_1, *done[1, 0]))
    keep_2, sent_2 = last(1, after(gots[1], mix_1), s_m2, got_2)
    mix_2 = mixed(((0, 0), (1, 1)), mix_1, F32, (sent_1, *done[0, 0]), (keep_2, *done[1, 1]))
    return mixed(((0, 1),), mix_2, BF, (sent_2, *done[0, 1])).reshape(rows, 1, depth)


def solution(mesh):
    placed = (P("tm", "space", None), P("space")) + (P(),) * 13
    return jax.shard_map(body, mesh=mesh, in_specs=placed, out_specs=P("tm", "space", None), check_vma=False)
```

```python
import functools

import jax
import jax.numpy as jnp
from jax import lax
from jax.experimental import pallas as pl
from jax.experimental.pallas import tpu as pltpu
from jax.sharding import PartitionSpec as P

BF = jnp.bfloat16
F32 = jnp.float32
VM = pl.BlockSpec(memory_space=pltpu.VMEM)
SM = pl.BlockSpec(memory_space=pltpu.SMEM)
ANY = pl.BlockSpec(memory_space=pl.ANY)
LANES = 128
CHUNK = 256
EXTRA = 16


def dot(a, b):
    return jnp.dot(a, b, preferred_element_type=F32)


def dot_t(a, b):
    return lax.dot_general(a, b, (((1,), (1,)), ((), ())), preferred_element_type=F32)


def iota(shape, axis):
    return lax.broadcasted_iota(jnp.int32, shape, axis)


def params(mib):
    return pltpu.CompilerParams(vmem_limit_bytes=mib * 2**20)


def sds(shape, dtype):
    return jax.ShapeDtypeStruct(shape, dtype)


def spread_heads(first_head, heads, head_dim):
    row = iota((2 * heads, CHUNK), 0)
    lane = iota((2 * heads, CHUNK), 1)
    row = jnp.where(row < heads, row, row - heads)
    return (row == first_head + lane // head_dim).astype(F32).astype(BF)


def split_two(value, heads):
    high = value.astype(BF).astype(F32)
    return jnp.where(iota(value.shape, 1) < heads, high, value - high).astype(BF)


def pick_half(tile_a, tile_b, part):
    half = LANES // 2
    low = iota(tile_a.shape, 1) < half
    if part == 0:
        return jnp.where(low, tile_a, pltpu.roll(tile_b, half, 1))
    return jnp.where(low, pltpu.roll(tile_a, half, 1), tile_b)


def compact(ref, j, part):
    start = j * 2 * CHUNK
    tiles = [ref[:, start + i:start + i + LANES] for i in range(0, 2 * CHUNK, LANES)]
    pairs = [pick_half(tiles[i], tiles[i + 1], part) for i in range(0, len(tiles), 2)]
    return jnp.concatenate(pairs, axis=1)


def project(half, group, heads, head_dim, w, normed, b_t, grow, fall_end, x_ref, xs_ref, s_ref):
    width = b_t.shape[0]
    size = x_ref.shape[1]
    first = (half * 2 + group) * (size // head_dim)
    later = []
    for j in range(size // CHUNK):
        cols = slice(j * CHUNK, (j + 1) * CHUNK)
        spread = spread_heads(first + j * (CHUNK // head_dim), heads, head_dim)
        x = dot(normed[...], compact(w, j, 0)).astype(BF)
        scaled = (x.astype(F32) * dot(grow, spread)).astype(BF)
        x_ref[:, cols] = x
        xs_ref[:, cols] = scaled
        decay = dot(fall_end, spread)[EXTRA - 1:EXTRA]
        s_ref[width:width + EXTRA, cols] = decay_rows(decay)
        later.append((cols, scaled, decay))
    for cols, scaled, decay in later:
        s_ref[0:width, cols] = (dot(b_t, scaled) * decay).astype(BF)


def decay_rows(decay):
    high = decay.astype(BF).astype(F32)
    row = iota((EXTRA, decay.shape[1]), 0)
    return jnp.where(row == 0, high, jnp.where(row == 1, decay - high, 0.0)).astype(BF)


def in_pieces(src, dst, sem, slot):
    block = dst.shape[0] // 2

    def piece(i):
        part = pl.ds(pl.multiple_of(i * block, block), block)
        return pltpu.make_async_copy(src.at[part, :], dst.at[part, :], sem.at[slot, i])

    return piece


def start_pieces(pieces):
    def go(i, carry):
        for piece in pieces:
            piece(i).start()
        return carry

    lax.fori_loop(0, 2, go, 0)


def wait_pieces(pieces):
    def go(i, carry):
        for piece in pieces:
            piece(i).wait()
        return carry

    lax.fori_loop(0, 2, go, 0)


def encode_kernel(heads, head_dim, here_ref, cell_ref, frames_any, enc_in_any, bias_any, enc_out_any, pos_any, gain_any,
                  w_keys_any, w_step_any, step_bias_any, code_any, skip_any, out_gain_any, w_pair_any,
                  encoded, normed, keys, b_t, grow, fall, skip, out_gain, x_ref, xs_ref, s_ref, w_o1, w_m1, w_o2, w_m2,
                  frames, enc_in, bias, enc_out, pos, norm_gain, w_keys, w_step, step_bias, code, sem, wsem):
    half = 1 - here_ref[0] % 2
    cell = cell_ref[0]
    base = pl.multiple_of((cell // EXTRA) * EXTRA, EXTRA)
    small = [pltpu.make_async_copy(src, dst, sem.at[i]) for i, (src, dst) in enumerate((
        (bias_any, bias), (pos_any.at[pl.ds(base, EXTRA), :], pos), (gain_any, norm_gain), (step_bias_any, step_bias),
        (code_any, code), (skip_any, skip), (out_gain_any, out_gain)))]
    first = [in_pieces(src, dst, wsem, i) for i, (src, dst) in enumerate((
        (frames_any, frames), (enc_in_any, enc_in), (enc_out_any, enc_out), (w_keys_any, w_keys), (w_step_any, w_step)))]
    big = [in_pieces(group_columns(w_pair_any, dst, which, group), dst, wsem, 5 + i) for i, (which, group, dst) in enumerate((
        (half, 0, w_o1), (1 - half, 0, w_m1), (half, 1, w_o2), (1 - half, 1, w_m2)))]
    start_pieces(first[:2])
    for c in small:
        c.start()
    start_pieces(first[2:])
    rows, depth = encoded.shape
    block = rows // 2
    lower = (iota((rows, rows), 0) >= iota((rows, rows), 1)).astype(F32).astype(BF)
    small[0].wait()
    wait_pieces(first[:2])
    start_pieces(big)
    twice = lambda v: jnp.concatenate([v, v], axis=1)
    columns = [slice(j, j + CHUNK) for j in range(0, depth, CHUNK)]

    def hide(part):
        pieces = []
        for cols in columns:
            h = dot(frames[part, :], enc_in[:, cols]) + bias[:, cols]
            pieces.append(jax.nn.gelu(h, approximate=True).astype(BF))
        return jnp.concatenate(pieces, axis=1)

    def encode(part, hidden, row):
        square = jnp.zeros((block, 1), F32)
        for cols in columns:
            e = (dot(hidden, enc_out[:, cols]) + row[:, cols]).astype(BF)
            encoded[part, cols] = e
            e = e.astype(F32)
            square += jnp.sum(e * e, axis=1, keepdims=True)
        inv = lax.rsqrt(square / depth + 1e-05)
        pieces = []
        for cols in columns:
            piece = (encoded[part, cols].astype(F32) * inv * norm_gain[:, cols]).astype(BF)
            normed[part, cols] = piece
            pieces.append(piece)
        return jnp.concatenate(pieces, axis=1)

    def read_out(part, wide):
        k = dot(wide, w_keys[...]).astype(BF)
        keys[part, :] = k
        b_t[:, part] = k[:, :k.shape[1] // 2].T
        ws = w_step[...]
        raw = dot_t(wide, jnp.concatenate([ws, ws], axis=0)) + twice(step_bias[...])
        return jax.nn.sigmoid(raw).astype(BF)

    top, low = slice(0, block), slice(block, rows)
    hidden_top = hide(top)
    hidden_low = hide(low)
    for c in small[1:]:
        c.wait()
    wait_pieces(first[2:])
    row = jnp.sum(jnp.where(iota(pos.shape, 0) == cell - base, pos[...].astype(F32), 0.0), axis=0, keepdims=True)
    wide_top = encode(top, hidden_top, row)
    wide_low = encode(low, hidden_low, row)
    step = jnp.concatenate([read_out(top, wide_top), read_out(low, wide_low)], axis=0)
    cum = dot(lower, step) * twice(-0.0005 - 0.003 * code[...].astype(F32))
    g = split_two(jnp.exp(-cum), heads)
    f = split_two(jnp.exp(cum), heads)
    grow[...] = g
    fall[...] = f
    wait_pieces(big[:1])
    project(half, 0, heads, head_dim, w_o1, normed, b_t[...], g, f[rows - EXTRA:], x_ref, xs_ref, s_ref)
    wait_pieces(big[1:])


def group_columns(w_any, like, half, group):
    size = like.shape[1]
    return w_any.at[:, pl.ds(pl.multiple_of((half * 2 + group) * size, size), size)]


def project_kernel(heads, head_dim, own, group, here_ref, normed, b_t, grow, fall, w, x_ref, xs_ref, s_ref):
    half = (here_ref[0] + 1 - own) % 2
    rows = normed.shape[0]
    project(half, group, heads, head_dim, w, normed, b_t[...], grow[...], fall[rows - EXTRA:], x_ref, xs_ref, s_ref)


def opened(ref):
    width = ref.shape[0] - EXTRA
    tail = ref[width:, :].astype(F32)
    return ref[:width, :].astype(F32), tail[0:1] + tail[1:2]


def close(ref, state, decay):
    width = ref.shape[0] - EXTRA
    ref[:width, :] = state.astype(BF)
    ref[width:, :] = decay_rows(decay)


def total_kernel(here_ref, mine_ref, got_ref, total_ref):
    mine, mine_decay = opened(mine_ref)
    got, got_decay = opened(got_ref)

    @pl.when(here_ref[0] % 2 == 1)
    def _():
        close(total_ref, mine_decay * got + mine, mine_decay * got_decay)

    @pl.when(here_ref[0] % 2 == 0)
    def _():
        close(total_ref, got_decay * mine + got, mine_decay * got_decay)


def step_kernel(first, reach, here_ref, total_ref, got_ref, before_ref, new_before_ref, new_total_ref):
    later = (here_ref[0] // reach) % 2 == 1
    got, got_decay = opened(got_ref)
    total, total_decay = opened(total_ref)

    @pl.when(later)
    def _():
        if first:
            close(new_before_ref, got, got_decay)
        else:
            before, before_decay = opened(before_ref)
            close(new_before_ref, before + before_decay * got, before_decay * got_decay)
        close(new_total_ref, total_decay * got + total, total_decay * got_decay)

    @pl.when(jnp.logical_not(later))
    def _():
        if first:
            close(new_before_ref, jnp.zeros_like(got), jnp.ones_like(got_decay))
        else:
            new_before_ref[...] = before_ref[...]
        close(new_total_ref, got_decay * total + got, total_decay * got_decay)


def last_kernel(reach, here_ref, got_ref, before_ref, mine_ref, first_ref, keep_ref, send_ref):
    width = keep_ref.shape[0]
    later = (here_ref[0] // reach) % 2 == 1
    got, _ = opened(got_ref)
    before, before_decay = opened(before_ref)
    before = before + jnp.where(later, before_decay, 0.0) * got

    @pl.when(here_ref[0] % 2 == 1)
    def _():
        state, decay = opened(first_ref)
        keep_ref[...] = (decay * before + state).astype(BF)
        send_ref[...] = before.astype(BF)

    @pl.when(here_ref[0] % 2 == 0)
    def _():
        state, decay = opened(mine_ref)
        send_ref[...] = (decay * before + state).astype(BF)
        keep_ref[...] = before.astype(BF)


def inner_kernel(heads, head_dim, own, group, fresh, here_ref, normed, keys, fall, skip, w_out_any, w, x, xs, *refs):
    half = (here_ref[0] + 1 - own) % 2
    rows = keys.shape[0]
    width = keys.shape[1] // 2
    size = x.shape[1]
    if fresh:
        u, v, w_rows, scores_ref, sem = refs
    else:
        scores_ref, u, v, w_rows, sem = refs
    start = pl.multiple_of((half * 2 + group) * size, size)
    copies = [in_pieces(w_out_any.at[pl.ds(start, size), :], w_rows, sem, 0)]
    start_pieces(copies)
    if fresh:
        scores = dot_t(keys[:, width:], keys[:, :width])
        scores_ref[...] = jnp.where(iota((rows, rows), 0) >= iota((rows, rows), 1), scores, 0.0).astype(BF)
    scores = scores_ref[...]
    mid = rows // 2
    both = jnp.broadcast_to(jnp.concatenate([skip[...], skip[...]], axis=1), (EXTRA, 2 * heads))
    skip_two = split_two(both, heads)
    first = (half * 2 + group) * (size // head_dim)
    for j in range(size // CHUNK):
        cols = slice(j * CHUNK, (j + 1) * CHUNK)
        z = dot(normed[...], compact(w, j, 1)).astype(BF).astype(F32)
        gate = z * jax.nn.sigmoid(z)
        spread = spread_heads(first + j * (CHUNK // head_dim), heads, head_dim)
        gain = dot(skip_two, spread)[0:1]
        grown = dot(fall[...], spread)
        u[:, cols] = (grown * gate).astype(BF)
        top = dot(scores[:mid, :mid], xs[:mid, cols])
        low = dot(scores[mid:], xs[:, cols])
        for part, inner in ((slice(0, mid), top), (slice(mid, rows), low)):
            v[part, cols] = ((grown[part] * inner + gain * x[part, cols].astype(F32)) * gate[part]).astype(BF)
    wait_pieces(copies)


def mix_kernel(head_dim, places, last, here_ref, keys, base, gain, *refs):
    many = len(places)
    states, us, vs, ws = (refs[i * many:(i + 1) * many] for i in range(4))
    out = refs[4 * many]
    width = keys.shape[1] // 2
    size = us[0].shape[1]
    starts = [((here_ref[0] + 1 - own) % 2 * 2 + group) * size for own, group in places]
    same = (iota((CHUNK, CHUNK), 0) // head_dim) == (iota((CHUNK, CHUNK), 1) // head_dim)
    mean = jnp.where(same, 1.0 / head_dim, 0.0).astype(BF)
    work = []
    for state, u, v in zip(states, us, vs):
        for j in range(size // CHUNK):
            cols = slice(j * CHUNK, (j + 1) * CHUNK)
            carried = dot(keys[:, width:], state[:, cols])
            g = v[:, cols].astype(F32) + u[:, cols].astype(F32) * carried
            work.append((g, dot((g * g).astype(BF), mean)))
    mixed = []
    for i in range(many):
        parts = []
        for j in range(size // CHUNK):
            g, m = work[i * (size // CHUNK) + j]
            row = gain[:, pl.ds(pl.multiple_of(starts[i] + j * CHUNK, CHUNK), CHUNK)]
            parts.append((g * lax.rsqrt(m + 1e-05) * row).astype(BF))
        mixed.append(jnp.concatenate(parts, axis=1))
    copies = []
    for n in range(base.shape[1] // CHUNK):
        cols = slice(n * CHUNK, (n + 1) * CHUNK)
        total = base[:, cols].astype(F32)
        for part, w in zip(mixed, ws):
            total = total + dot(part, w[:, cols])
        if last:
            buf, sem = refs[4 * many + 1:]
            buf[:, cols] = total.astype(buf.dtype)
            copies.append(pltpu.make_async_copy(buf.at[:, cols], out.at[:, cols], sem.at[n]))
            copies[-1].start()
        else:
            out[:, cols] = total.astype(out.dtype)
    for c in copies:
        c.wait()


def body(frames, patch_cell, enc_in, enc_bias, enc_out, pos_table, norm_gain, w_pair, w_keys, w_step,
         step_bias, decay_code, skip_gain, out_gain, w_out):
    rows = frames.shape[0]
    pix = frames.shape[2]
    depth = enc_out.shape[1]
    heads = w_step.shape[1]
    head_dim = w_pair.shape[1] // (2 * heads)
    width = w_keys.shape[1] // 2
    size = heads * head_dim // 4
    peers = lax.axis_size("tm")
    here = lax.axis_index("tm").astype(jnp.int32).reshape(1)
    row = lambda v: v.reshape(1, -1)
    far = lambda v: pltpu.with_memory_space_constraint(v, pltpu.HBM)
    near = lambda shape, dtype=BF: pltpu.VMEM(shape, dtype)
    sems = lambda n: pltpu.SemaphoreType.DMA((n,))
    pair = lambda by: [(i, i ^ by) for i in range(peers)]
    after = lambda value, *first: lax.optimization_barrier((value,) + first)[0]

    def call(kernel, name, outs, ins, scratch=(), macs=0, out_spec=VM):
        specs = [spec for spec, _ in ins]
        cost = pl.CostEstimate(flops=macs // 4, bytes_accessed=2**20, transcendentals=0)
        return pl.pallas_call(kernel, out_shape=tuple(outs), in_specs=specs, out_specs=(out_spec,) * len(outs),
                              scratch_shapes=list(scratch), compiler_params=params(24), name=name,
                              cost_estimate=cost)(*[v for _, v in ins])

    vm = lambda *vs: [(VM, v) for v in vs]
    hbm = lambda *vs: [(pl.BlockSpec(memory_space=pltpu.HBM), far(v)) for v in vs]
    where = [(SM, here)]

    part, message, weight = near((rows, size)), near((width + EXTRA, size)), near((depth, 2 * size))
    encoded, normed, keys, b_t, grow, fall, skip, gain, x_o1, xs_o1, s_o1, w_o1, w_m1, w_o2, w_m2 = call(
        functools.partial(encode_kernel, heads, head_dim), "encode",
        (near((rows, depth)), near((rows, depth)), near((rows, 2 * width)), near((width, rows)),
         near((rows, 2 * heads)), near((rows, 2 * heads)), near((1, heads), F32), near((1, heads * head_dim), F32),
         part, part, message) + (weight,) * 4,
        where + [(SM, patch_cell)] + hbm(frames.reshape(rows, pix), enc_in, row(enc_bias), enc_out, pos_table, row(norm_gain),
                                         w_keys, w_step.T, row(step_bias), row(decay_code), row(skip_gain), row(out_gain),
                                         w_pair),
        [near((rows, pix)), near((pix, depth)), near((1, depth), F32), near((depth, depth)), near((EXTRA, depth)),
         near((1, depth), F32), near((depth, 2 * width)), near((heads, depth)), near((1, heads), F32),
         near((1, heads), jnp.int32), sems(7), pltpu.SemaphoreType.DMA((9, 2))],
        rows * depth * depth)

    def projected(own, group, w):
        return call(functools.partial(project_kernel, heads, head_dim, own, group), "project",
                    (part, part, message), where + vm(normed, b_t, grow, fall, w), (), rows * depth * size)

    scores = []

    def inner(own, group, w, x, xs):
        outs = call(functools.partial(inner_kernel, heads, head_dim, own, group, not scores), "inner",
                    (part, part, near((size, depth))) + (() if scores else (near((rows, rows)),)),
                    where + vm(normed, keys, fall, skip) + hbm(w_out) + vm(w, x, xs, *scores),
                    [pltpu.SemaphoreType.DMA((1, 2))], rows * depth * size)
        scores.extend(outs[3:])
        return outs[:3]

    def mixed(places, base, last, *groups):
        states, us, vs, ws = zip(*groups)
        shape = sds((rows, depth), BF) if last else near((rows, depth), F32)
        return call(functools.partial(mix_kernel, head_dim, places, last), "mix", (shape,),
                    where + vm(keys, base, gain, *states, *us, *vs, *ws),
                    [near((rows, depth)), sems(depth // CHUNK)] if last else [], len(places) * rows * depth * size,
                    ANY if last else VM)[0]

    got_1 = lax.ppermute(s_o1, "tm", pair(1))
    x_m1, xs_m1, s_m1 = projected(1, 0, w_m1)
    total_1, = call(total_kernel, "total", (message,), where + vm(s_m1, got_1))
    x_o2, xs_o2, s_o2 = projected(0, 1, after(w_o2, total_1))
    got_2 = lax.ppermute(s_o2, "tm", pair(1))
    x_m2, xs_m2, s_m2 = projected(1, 1, w_m2)
    total_2, = call(total_kernel, "total", (message,), where + vm(s_m2, got_2))

    todo = [(0, 0, w_o1, x_o1, xs_o1), (1, 0, w_m1, x_m1, xs_m1), (1, 1, w_m2, x_m2, xs_m2), (0, 1, w_o2, x_o2, xs_o2)]
    done = {}
    totals, befores = [total_1, total_2], [total_1, total_2]
    gots = [lax.ppermute(total_1, "tm", pair(2)), lax.ppermute(total_2, "tm", pair(2))]
    stamp = total_2
    reach = 2
    while reach * 2 < peers:
        for i in range(2):
            if todo:
                own, group, w, x, xs = todo.pop(0)
                done[own, group] = inner(own, group, w, after(x, stamp), xs)
                gots[i] = after(gots[i], done[own, group][0])
            befores[i], totals[i] = call(functools.partial(step_kernel, reach == 2, reach), "step", (message, message),
                                         where + vm(totals[i], gots[i], befores[i]))
            stamp = totals[i]
            gots[i] = lax.ppermute(totals[i], "tm", pair(2 * reach))
        reach *= 2
    for own, group, w, x, xs in todo:
        done[own, group] = inner(own, group, w, after(x, stamp), xs)
        stamp = done[own, group][0]

    def last(i, got, mine, first):
        keep, send = call(functools.partial(last_kernel, reach), "last", (near((width, size)),) * 2,
                          where + vm(got, befores[i], mine, first))
        return keep, lax.ppermute(send, "tm", pair(1))

    keep_1, sent_1 = last(0, after(gots[0], stamp), s_m1, got_1)
    mix_1 = mixed(((1, 0),), encoded, False, (keep_1, *done[1, 0]))
    keep_2, sent_2 = last(1, after(gots[1], mix_1), s_m2, got_2)
    mix_2 = mixed(((0, 0), (1, 1)), mix_1, False, (sent_1, *done[0, 0]), (keep_2, *done[1, 1]))
    return mixed(((0, 1),), mix_2, True, (sent_2, *done[0, 1])).reshape(rows, 1, depth)


def solution(mesh):
    placed = (P("tm", "space", None), P("space")) + (P(),) * 13
    return jax.shard_map(body, mesh=mesh, in_specs=placed, out_specs=P("tm", "space", None), check_vma=False)
```

```python
import functools

import jax
import jax.numpy as jnp
from jax import lax
from jax.experimental import pallas as pl
from jax.experimental.pallas import tpu as pltpu
from jax.sharding import PartitionSpec as P

BF = jnp.bfloat16
F32 = jnp.float32
VM = pl.BlockSpec(memory_space=pltpu.VMEM)
SM = pl.BlockSpec(memory_space=pltpu.SMEM)
ANY = pl.BlockSpec(memory_space=pl.ANY)
LANES = 128
CHUNK = 256
EXTRA = 16


def dot(a, b):
    return jnp.dot(a, b, preferred_element_type=F32)


def dot_t(a, b):
    return lax.dot_general(a, b, (((1,), (1,)), ((), ())), preferred_element_type=F32)


def iota(shape, axis):
    return lax.broadcasted_iota(jnp.int32, shape, axis)


def params(mib):
    return pltpu.CompilerParams(vmem_limit_bytes=mib * 2**20)


def sds(shape, dtype):
    return jax.ShapeDtypeStruct(shape, dtype)


def spread_heads(first_head, heads, head_dim):
    row = iota((2 * heads, CHUNK), 0)
    lane = iota((2 * heads, CHUNK), 1)
    row = jnp.where(row < heads, row, row - heads)
    return (row == first_head + lane // head_dim).astype(F32).astype(BF)


def split_two(value, heads):
    high = value.astype(BF).astype(F32)
    return jnp.where(iota(value.shape, 1) < heads, high, value - high).astype(BF)


def pick_half(tile_a, tile_b, part):
    half = LANES // 2
    low = iota(tile_a.shape, 1) < half
    if part == 0:
        return jnp.where(low, tile_a, pltpu.roll(tile_b, half, 1))
    return jnp.where(low, pltpu.roll(tile_a, half, 1), tile_b)


def compact(ref, j, part):
    start = j * 2 * CHUNK
    tiles = [ref[:, start + i:start + i + LANES] for i in range(0, 2 * CHUNK, LANES)]
    pairs = [pick_half(tiles[i], tiles[i + 1], part) for i in range(0, len(tiles), 2)]
    return jnp.concatenate(pairs, axis=1)


def project(jobs, heads, head_dim, normed, b_t, grow, fall_end):
    width = b_t.shape[0]
    later = []
    for first, w, x_ref, xs_ref, s_ref in jobs:
        for j in range(x_ref.shape[1] // CHUNK):
            cols = slice(j * CHUNK, (j + 1) * CHUNK)
            spread = spread_heads(first + j * (CHUNK // head_dim), heads, head_dim)
            x = dot(normed[...], compact(w, j, 0)).astype(BF)
            scaled = (x.astype(F32) * dot(grow, spread)).astype(BF)
            x_ref[:, cols] = x
            xs_ref[:, cols] = scaled
            decay = dot(fall_end, spread)[EXTRA - 1:EXTRA]
            s_ref[width:width + EXTRA, cols] = decay_rows(decay)
            later.append((s_ref, cols, scaled, decay))
    for s_ref, cols, scaled, decay in later:
        s_ref[0:width, cols] = (dot(b_t, scaled) * decay).astype(BF)


def decay_rows(decay):
    high = decay.astype(BF).astype(F32)
    row = iota((EXTRA, decay.shape[1]), 0)
    return jnp.where(row == 0, high, jnp.where(row == 1, decay - high, 0.0)).astype(BF)


def in_pieces(src, dst, sem, slot):
    block = dst.shape[0] // 2

    def piece(i):
        part = pl.ds(pl.multiple_of(i * block, block), block)
        return pltpu.make_async_copy(src.at[part, :], dst.at[part, :], sem.at[slot, i])

    return piece


def start_pieces(pieces):
    def go(i, carry):
        for piece in pieces:
            piece(i).start()
        return carry

    lax.fori_loop(0, 2, go, 0)


def wait_pieces(pieces):
    def go(i, carry):
        for piece in pieces:
            piece(i).wait()
        return carry

    lax.fori_loop(0, 2, go, 0)


def encode_kernel(heads, head_dim, here_ref, cell_ref, frames_any, enc_in_any, bias_any, enc_out_any, pos_any, gain_any,
                  w_keys_any, w_step_any, step_bias_any, code_any, skip_any, out_gain_any, w_pair_any,
                  encoded, normed, keys, b_t, grow, fall, skip, out_gain, x_o1, xs_o1, x_o2, xs_o2, s_o, w_o1, w_m1, w_o2, w_m2,
                  frames, enc_in, bias, enc_out, pos, norm_gain, w_keys, w_step, step_bias, code, sem, wsem):
    half = 1 - here_ref[0] % 2
    cell = cell_ref[0]
    base = pl.multiple_of((cell // EXTRA) * EXTRA, EXTRA)
    small = [pltpu.make_async_copy(src, dst, sem.at[i]) for i, (src, dst) in enumerate((
        (bias_any, bias), (pos_any.at[pl.ds(base, EXTRA), :], pos), (gain_any, norm_gain), (step_bias_any, step_bias),
        (code_any, code), (skip_any, skip), (out_gain_any, out_gain)))]
    first = [in_pieces(src, dst, wsem, i) for i, (src, dst) in enumerate((
        (frames_any, frames), (enc_in_any, enc_in), (enc_out_any, enc_out), (w_keys_any, w_keys), (w_step_any, w_step)))]
    big = [in_pieces(group_columns(w_pair_any, dst, which, group), dst, wsem, 5 + i) for i, (which, group, dst) in enumerate((
        (half, 0, w_o1), (half, 1, w_o2), (1 - half, 0, w_m1), (1 - half, 1, w_m2)))]
    start_pieces(first[:2])
    for c in small:
        c.start()
    start_pieces(first[2:])
    rows, depth = encoded.shape
    block = rows // 2
    lower = (iota((rows, rows), 0) >= iota((rows, rows), 1)).astype(F32).astype(BF)
    small[0].wait()
    wait_pieces(first[:2])
    start_pieces(big)
    twice = lambda v: jnp.concatenate([v, v], axis=1)
    columns = [slice(j, j + CHUNK) for j in range(0, depth, CHUNK)]

    def hide(part):
        pieces = []
        for cols in columns:
            h = dot(frames[part, :], enc_in[:, cols]) + bias[:, cols]
            pieces.append(jax.nn.gelu(h, approximate=True).astype(BF))
        return jnp.concatenate(pieces, axis=1)

    def encode(part, hidden, row):
        square = jnp.zeros((block, 1), F32)
        for cols in columns:
            e = (dot(hidden, enc_out[:, cols]) + row[:, cols]).astype(BF)
            encoded[part, cols] = e
            e = e.astype(F32)
            square += jnp.sum(e * e, axis=1, keepdims=True)
        inv = lax.rsqrt(square / depth + 1e-05)
        pieces = []
        for cols in columns:
            piece = (encoded[part, cols].astype(F32) * inv * norm_gain[:, cols]).astype(BF)
            normed[part, cols] = piece
            pieces.append(piece)
        return jnp.concatenate(pieces, axis=1)

    def read_out(part, wide):
        k = dot(wide, w_keys[...]).astype(BF)
        keys[part, :] = k
        b_t[:, part] = k[:, :k.shape[1] // 2].T
        ws = w_step[...]
        raw = dot_t(wide, jnp.concatenate([ws, ws], axis=0)) + twice(step_bias[...])
        return jax.nn.sigmoid(raw).astype(BF)

    top, low = slice(0, block), slice(block, rows)
    hidden_top = hide(top)
    hidden_low = hide(low)
    for c in small[1:]:
        c.wait()
    wait_pieces(first[2:])
    row = jnp.sum(jnp.where(iota(pos.shape, 0) == cell - base, pos[...].astype(F32), 0.0), axis=0, keepdims=True)
    wide_top = encode(top, hidden_top, row)
    wide_low = encode(low, hidden_low, row)
    step = jnp.concatenate([read_out(top, wide_top), read_out(low, wide_low)], axis=0)
    cum = dot(lower, step) * twice(-0.0005 - 0.003 * code[...].astype(F32))
    g = split_two(jnp.exp(-cum), heads)
    f = split_two(jnp.exp(cum), heads)
    grow[...] = g
    fall[...] = f
    wait_pieces(big[:2])
    size = x_o1.shape[1]
    per = size // head_dim
    project([(half * 2 * per, w_o1, x_o1, xs_o1, s_o.at[:, :size]), (half * 2 * per + per, w_o2, x_o2, xs_o2, s_o.at[:, size:])],
            heads, head_dim, normed, b_t[...], g, f[rows - EXTRA:])
    wait_pieces(big[2:])


def group_columns(w_any, like, half, group):
    size = like.shape[1]
    return w_any.at[:, pl.ds(pl.multiple_of((half * 2 + group) * size, size), size)]


def project_kernel(heads, head_dim, own, group, here_ref, normed, b_t, grow, fall, w, x_ref, xs_ref, s_ref):
    half = (here_ref[0] + 1 - own) % 2
    rows = normed.shape[0]
    first = (half * 2 + group) * (x_ref.shape[1] // head_dim)
    project([(first, w, x_ref, xs_ref, s_ref)], heads, head_dim, normed, b_t[...], grow[...], fall[rows - EXTRA:])


def opened(ref):
    width = ref.shape[0] - EXTRA
    tail = ref[width:, :].astype(F32)
    return ref[:width, :].astype(F32), tail[0:1] + tail[1:2]


def close(ref, state, decay):
    width = ref.shape[0] - EXTRA
    ref[:width, :] = state.astype(BF)
    ref[width:, :] = decay_rows(decay)


def total_kernel(group, here_ref, mine_ref, got_ref, total_ref):
    size = mine_ref.shape[1]
    mine, mine_decay = opened(mine_ref)
    got, got_decay = opened(got_ref.at[:, group * size:(group + 1) * size])

    @pl.when(here_ref[0] % 2 == 1)
    def _():
        close(total_ref, mine_decay * got + mine, mine_decay * got_decay)

    @pl.when(here_ref[0] % 2 == 0)
    def _():
        close(total_ref, got_decay * mine + got, mine_decay * got_decay)


def step_kernel(first, final, reach, here_ref, total_ref, got_ref, before_ref, new_before_ref, new_total_ref):
    later = (here_ref[0] // reach) % 2 == 1
    got, got_decay = opened(got_ref)
    total, total_decay = opened(total_ref)

    def put_total(value):
        if final:
            new_total_ref[...] = value.astype(BF)
        else:
            close(new_total_ref, value, total_decay * got_decay)

    @pl.when(later)
    def _():
        if first:
            close(new_before_ref, got, got_decay)
        else:
            before, before_decay = opened(before_ref)
            close(new_before_ref, before + before_decay * got, before_decay * got_decay)
        put_total(total_decay * got + total)

    @pl.when(jnp.logical_not(later))
    def _():
        if first:
            close(new_before_ref, jnp.zeros_like(got), jnp.ones_like(got_decay))
        else:
            new_before_ref[...] = before_ref[...]
        put_total(got_decay * total + got)


def last_kernel(reach, group, here_ref, got_ref, before_ref, mine_ref, first_ref, keep_ref, send_ref):
    state_size = keep_ref.shape[1]
    later = (here_ref[0] // reach) % 2 == 1
    got = got_ref[:keep_ref.shape[0], :].astype(F32)
    before, before_decay = opened(before_ref)
    before = before + jnp.where(later, before_decay, 0.0) * got

    @pl.when(here_ref[0] % 2 == 1)
    def _():
        state, decay = opened(first_ref.at[:, group * state_size:(group + 1) * state_size])
        keep_ref[...] = (decay * before + state).astype(BF)
        send_ref[...] = before.astype(BF)

    @pl.when(here_ref[0] % 2 == 0)
    def _():
        state, decay = opened(mine_ref)
        send_ref[...] = (decay * before + state).astype(BF)
        keep_ref[...] = before.astype(BF)


def inner_kernel(heads, head_dim, own, group, fresh, here_ref, normed, keys, fall, skip, w_out_any, w, x, xs, *refs):
    half = (here_ref[0] + 1 - own) % 2
    rows = keys.shape[0]
    width = keys.shape[1] // 2
    size = x.shape[1]
    if fresh:
        u, v, w_rows, scores_ref, sem = refs
    else:
        scores_ref, u, v, w_rows, sem = refs
    start = pl.multiple_of((half * 2 + group) * size, size)
    copies = [in_pieces(w_out_any.at[pl.ds(start, size), :], w_rows, sem, 0)]
    start_pieces(copies)
    if fresh:
        scores = dot_t(keys[:, width:], keys[:, :width])
        scores_ref[...] = jnp.where(iota((rows, rows), 0) >= iota((rows, rows), 1), scores, 0.0).astype(BF)
    scores = scores_ref[...]
    mid = rows // 2
    both = jnp.broadcast_to(jnp.concatenate([skip[...], skip[...]], axis=1), (EXTRA, 2 * heads))
    skip_two = split_two(both, heads)
    first = (half * 2 + group) * (size // head_dim)
    for j in range(size // CHUNK):
        cols = slice(j * CHUNK, (j + 1) * CHUNK)
        z = dot(normed[...], compact(w, j, 1)).astype(BF).astype(F32)
        gate = z * jax.nn.sigmoid(z)
        spread = spread_heads(first + j * (CHUNK // head_dim), heads, head_dim)
        gain = dot(skip_two, spread)[0:1]
        grown = dot(fall[...], spread)
        u[:, cols] = (grown * gate).astype(BF)
        top = dot(scores[:mid, :mid], xs[:mid, cols])
        low = dot(scores[mid:], xs[:, cols])
        for part, inner in ((slice(0, mid), top), (slice(mid, rows), low)):
            v[part, cols] = ((grown[part] * inner + gain * x[part, cols].astype(F32)) * gate[part]).astype(BF)
    wait_pieces(copies)


def mix_kernel(head_dim, places, last, here_ref, keys, base, gain, *refs):
    many = len(places)
    states, us, vs, ws = (refs[i * many:(i + 1) * many] for i in range(4))
    out = refs[4 * many]
    width = keys.shape[1] // 2
    size = us[0].shape[1]
    starts = [((here_ref[0] + 1 - own) % 2 * 2 + group) * size for own, group in places]
    same = (iota((CHUNK, CHUNK), 0) // head_dim) == (iota((CHUNK, CHUNK), 1) // head_dim)
    mean = jnp.where(same, 1.0 / head_dim, 0.0).astype(BF)
    work = []
    for state, u, v in zip(states, us, vs):
        for j in range(size // CHUNK):
            cols = slice(j * CHUNK, (j + 1) * CHUNK)
            carried = dot(keys[:, width:], state[:, cols])
            g = v[:, cols].astype(F32) + u[:, cols].astype(F32) * carried
            work.append((g, dot((g * g).astype(BF), mean)))
    mixed = []
    for i in range(many):
        parts = []
        for j in range(size // CHUNK):
            g, m = work[i * (size // CHUNK) + j]
            row = gain[:, pl.ds(pl.multiple_of(starts[i] + j * CHUNK, CHUNK), CHUNK)]
            parts.append((g * lax.rsqrt(m + 1e-05) * row).astype(BF))
        mixed.append(jnp.concatenate(parts, axis=1))
    copies = []
    for n in range(base.shape[1] // CHUNK):
        cols = slice(n * CHUNK, (n + 1) * CHUNK)
        total = base[:, cols].astype(F32)
        for part, w in zip(mixed, ws):
            total = total + dot(part, w[:, cols])
        if last:
            buf, sem = refs[4 * many + 1:]
            buf[:, cols] = total.astype(buf.dtype)
            copies.append(pltpu.make_async_copy(buf.at[:, cols], out.at[:, cols], sem.at[n]))
            copies[-1].start()
        else:
            out[:, cols] = total.astype(out.dtype)
    for c in copies:
        c.wait()


def body(frames, patch_cell, enc_in, enc_bias, enc_out, pos_table, norm_gain, w_pair, w_keys, w_step,
         step_bias, decay_code, skip_gain, out_gain, w_out):
    rows = frames.shape[0]
    pix = frames.shape[2]
    depth = enc_out.shape[1]
    heads = w_step.shape[1]
    head_dim = w_pair.shape[1] // (2 * heads)
    width = w_keys.shape[1] // 2
    size = heads * head_dim // 4
    peers = lax.axis_size("tm")
    here = lax.axis_index("tm").astype(jnp.int32).reshape(1)
    row = lambda v: v.reshape(1, -1)
    far = lambda v: pltpu.with_memory_space_constraint(v, pltpu.HBM)
    near = lambda shape, dtype=BF: pltpu.VMEM(shape, dtype)
    sems = lambda n: pltpu.SemaphoreType.DMA((n,))
    pair = lambda by: [(i, i ^ by) for i in range(peers)]
    after = lambda value, *first: lax.optimization_barrier((value,) + first)[0]

    def call(kernel, name, outs, ins, scratch=(), macs=0, out_spec=VM):
        specs = [spec for spec, _ in ins]
        cost = pl.CostEstimate(flops=macs // 4, bytes_accessed=2**20, transcendentals=0)
        return pl.pallas_call(kernel, out_shape=tuple(outs), in_specs=specs, out_specs=(out_spec,) * len(outs),
                              scratch_shapes=list(scratch), compiler_params=params(24), name=name,
                              cost_estimate=cost)(*[v for _, v in ins])

    vm = lambda *vs: [(VM, v) for v in vs]
    hbm = lambda *vs: [(pl.BlockSpec(memory_space=pltpu.HBM), far(v)) for v in vs]
    where = [(SM, here)]

    part, message, weight = near((rows, size)), near((width + EXTRA, size)), near((depth, 2 * size))
    encoded, normed, keys, b_t, grow, fall, skip, gain, x_o1, xs_o1, x_o2, xs_o2, s_o, w_o1, w_m1, w_o2, w_m2 = call(
        functools.partial(encode_kernel, heads, head_dim), "encode",
        (near((rows, depth)), near((rows, depth)), near((rows, 2 * width)), near((width, rows)),
         near((rows, 2 * heads)), near((rows, 2 * heads)), near((1, heads), F32), near((1, heads * head_dim), F32),
         part, part, part, part, near((width + EXTRA, 2 * size))) + (weight,) * 4,
        where + [(SM, patch_cell)] + hbm(frames.reshape(rows, pix), enc_in, row(enc_bias), enc_out, pos_table, row(norm_gain),
                                         w_keys, w_step.T, row(step_bias), row(decay_code), row(skip_gain), row(out_gain),
                                         w_pair),
        [near((rows, pix)), near((pix, depth)), near((1, depth), F32), near((depth, depth)), near((EXTRA, depth)),
         near((1, depth), F32), near((depth, 2 * width)), near((heads, depth)), near((1, heads), F32),
         near((1, heads), jnp.int32), sems(7), pltpu.SemaphoreType.DMA((9, 2))],
        rows * depth * depth)

    def projected(own, group, w):
        return call(functools.partial(project_kernel, heads, head_dim, own, group), "project",
                    (part, part, message), where + vm(normed, b_t, grow, fall, w), (), rows * depth * size)

    scores = []

    def inner(own, group, w, x, xs):
        outs = call(functools.partial(inner_kernel, heads, head_dim, own, group, not scores), "inner",
                    (part, part, near((size, depth))) + (() if scores else (near((rows, rows)),)),
                    where + vm(normed, keys, fall, skip) + hbm(w_out) + vm(w, x, xs, *scores),
                    [pltpu.SemaphoreType.DMA((1, 2))], rows * depth * size)
        scores.extend(outs[3:])
        return outs[:3]

    def mixed(places, base, last, *groups):
        states, us, vs, ws = zip(*groups)
        shape = sds((rows, depth), BF) if last else near((rows, depth), F32)
        return call(functools.partial(mix_kernel, head_dim, places, last), "mix", (shape,),
                    where + vm(keys, base, gain, *states, *us, *vs, *ws),
                    [near((rows, depth)), sems(depth // CHUNK)] if last else [], len(places) * rows * depth * size,
                    ANY if last else VM)[0]

    totals, befores, arriving = [None, None], [None, None], [None, None]
    done = {}

    def work(own, group, w, x, xs, stamp):
        done[own, group] = inner(own, group, w, after(x, stamp), xs)
        return done[own, group][0]

    def start_total(i, mine):
        totals[i], = call(functools.partial(total_kernel, i), "total", (message,), where + vm(mine, got))
        befores[i] = totals[i]
        arriving[i] = lax.ppermute(totals[i], "tm", pair(2))

    def advance(i, reach, arrived):
        final = reach * 4 >= peers
        befores[i], totals[i] = call(
            functools.partial(step_kernel, reach == 2, final, reach), "step",
            (message, near((width, size)) if final else message), where + vm(totals[i], arrived, befores[i]))
        arriving[i] = lax.ppermute(totals[i], "tm", pair(2 * reach))

    def finish(i, arrived, mine):
        keep, send = call(functools.partial(last_kernel, peers // 2, i), "last", (near((width, size)),) * 2,
                          where + vm(arrived, befores[i], mine, got))
        return keep, lax.ppermute(send, "tm", pair(1))

    got = lax.ppermute(s_o, "tm", pair(1))
    x_m1, xs_m1, s_m1 = projected(1, 0, w_m1)
    start_total(0, s_m1)
    x_m2, xs_m2, s_m2 = projected(1, 1, after(w_m2, totals[0]))
    stamp = work(0, 0, w_o1, x_o1, xs_o1, s_m2)
    start_total(1, after(s_m2, stamp))
    advance(0, 2, after(arriving[0], totals[1]))
    stamp = work(1, 0, w_m1, x_m1, xs_m1, befores[0])
    stamp = work(1, 1, w_m2, x_m2, xs_m2, stamp)
    advance(1, 2, after(arriving[1], stamp))
    reach = 4
    while reach * 2 < peers:
        for i in range(2):
            advance(i, reach, arriving[i])
        reach *= 2
    keep_1, sent_1 = finish(0, after(arriving[0], befores[1]), s_m1)
    stamp = work(0, 1, w_o2, x_o2, xs_o2, keep_1)
    mixing = mixed(((1, 0),), after(encoded, stamp), False, (keep_1, *done[1, 0]))
    keep_2, sent_2 = finish(1, after(arriving[1], mixing), s_m2)
    mixing = mixed(((0, 0), (1, 1)), after(mixing, keep_2), False, (sent_1, *done[0, 0]), (keep_2, *done[1, 1]))
    return mixed(((0, 1),), mixing, True, (sent_2, *done[0, 1])).reshape(rows, 1, depth)


def solution(mesh):
    placed = (P("tm", "space", None), P("space")) + (P(),) * 13
    return jax.shard_map(body, mesh=mesh, in_specs=placed, out_specs=P("tm", "space", None), check_vma=False)
```

```python
import functools

import jax
import jax.numpy as jnp
from jax import lax
from jax.experimental import pallas as pl
from jax.experimental.pallas import tpu as pltpu
from jax.sharding import PartitionSpec as P

BF = jnp.bfloat16
F32 = jnp.float32
VM = pl.BlockSpec(memory_space=pltpu.VMEM)
SM = pl.BlockSpec(memory_space=pltpu.SMEM)
ANY = pl.BlockSpec(memory_space=pl.ANY)
LANES = 128
CHUNK = 256
EXTRA = 16


def dot(a, b):
    return jnp.dot(a, b, preferred_element_type=F32)


def dot_t(a, b):
    return lax.dot_general(a, b, (((1,), (1,)), ((), ())), preferred_element_type=F32)


def iota(shape, axis):
    return lax.broadcasted_iota(jnp.int32, shape, axis)


def params(mib):
    return pltpu.CompilerParams(vmem_limit_bytes=mib * 2**20)


def sds(shape, dtype):
    return jax.ShapeDtypeStruct(shape, dtype)


def spread_heads(first_head, heads, head_dim):
    row = iota((2 * heads, CHUNK), 0)
    lane = iota((2 * heads, CHUNK), 1)
    row = jnp.where(row < heads, row, row - heads)
    return (row == first_head + lane // head_dim).astype(F32).astype(BF)


def split_two(value, heads):
    high = value.astype(BF).astype(F32)
    return jnp.where(iota(value.shape, 1) < heads, high, value - high).astype(BF)


def pick_half(tile_a, tile_b, part):
    half = LANES // 2
    low = iota(tile_a.shape, 1) < half
    if part == 0:
        return jnp.where(low, tile_a, pltpu.roll(tile_b, half, 1))
    return jnp.where(low, pltpu.roll(tile_a, half, 1), tile_b)


def compact(ref, j, part):
    start = j * 2 * CHUNK
    tiles = [ref[:, start + i:start + i + LANES] for i in range(0, 2 * CHUNK, LANES)]
    pairs = [pick_half(tiles[i], tiles[i + 1], part) for i in range(0, len(tiles), 2)]
    return jnp.concatenate(pairs, axis=1)


def project(first, w, xs_ref, s_ref, heads, head_dim, normed, b_t, grow, fall_end):
    width = b_t.shape[0]
    later = []
    for j in range(xs_ref.shape[1] // CHUNK):
        cols = slice(j * CHUNK, (j + 1) * CHUNK)
        spread = spread_heads(first + j * (CHUNK // head_dim), heads, head_dim)
        x = dot(normed[...], compact(w, j, 0)).astype(BF)
        scaled = (x.astype(F32) * dot(grow, spread)).astype(BF)
        xs_ref[:, cols] = scaled
        decay = dot(fall_end, spread)[EXTRA - 1:EXTRA]
        s_ref[width:width + EXTRA, cols] = decay_rows(decay)
        later.append((cols, scaled, decay))
    for cols, scaled, decay in later:
        s_ref[0:width, cols] = (dot(b_t, scaled) * decay).astype(BF)


def decay_rows(decay):
    high = decay.astype(BF).astype(F32)
    row = iota((EXTRA, decay.shape[1]), 0)
    return jnp.where(row == 0, high, jnp.where(row == 1, decay - high, 0.0)).astype(BF)


def in_pieces(src, dst, sem, slot):
    block = dst.shape[0] // 2

    def piece(i):
        part = pl.ds(pl.multiple_of(i * block, block), block)
        return pltpu.make_async_copy(src.at[part, :], dst.at[part, :], sem.at[slot, i])

    return piece


def start_pieces(pieces):
    def go(i, carry):
        for piece in pieces:
            piece(i).start()
        return carry

    lax.fori_loop(0, 2, go, 0)


def wait_pieces(pieces):
    def go(i, carry):
        for piece in pieces:
            piece(i).wait()
        return carry

    lax.fori_loop(0, 2, go, 0)


def encode_kernel(heads, head_dim, here_ref, cell_ref, frames_any, enc_in_any, bias_any, enc_out_any, pos_any, gain_any,
                  w_keys_any, w_step_any, step_bias_any, code_any, skip_any, out_gain_any, w_pair_any,
                  encoded, normed, keys, b_t, grow, fall, skip, out_gain, xs_o1, s_o1, w_o1, w_m1, w_o2, w_m2,
                  frames, enc_in, bias, enc_out, pos, norm_gain, w_keys, w_step, step_bias, code, sem, wsem):
    half = 1 - here_ref[0] % 2
    cell = cell_ref[0]
    base = pl.multiple_of((cell // EXTRA) * EXTRA, EXTRA)
    small = [pltpu.make_async_copy(src, dst, sem.at[i]) for i, (src, dst) in enumerate((
        (bias_any, bias), (pos_any.at[pl.ds(base, EXTRA), :], pos), (gain_any, norm_gain), (step_bias_any, step_bias),
        (code_any, code), (skip_any, skip), (out_gain_any, out_gain)))]
    first = [in_pieces(src, dst, wsem, i) for i, (src, dst) in enumerate((
        (frames_any, frames), (enc_in_any, enc_in), (enc_out_any, enc_out), (w_keys_any, w_keys), (w_step_any, w_step)))]
    big = [in_pieces(group_columns(w_pair_any, dst, which, group), dst, wsem, 5 + i) for i, (which, group, dst) in enumerate((
        (half, 0, w_o1), (1 - half, 0, w_m1), (half, 1, w_o2), (1 - half, 1, w_m2)))]
    start_pieces(first[:2])
    for c in small:
        c.start()
    start_pieces(first[2:])
    rows, depth = encoded.shape
    block = rows // 2
    lower = (iota((rows, rows), 0) >= iota((rows, rows), 1)).astype(F32).astype(BF)
    small[0].wait()
    wait_pieces(first[:2])
    start_pieces(big)
    twice = lambda v: jnp.concatenate([v, v], axis=1)
    columns = [slice(j, j + CHUNK) for j in range(0, depth, CHUNK)]

    def hide(part):
        pieces = []
        for cols in columns:
            h = dot(frames[part, :], enc_in[:, cols]) + bias[:, cols]
            pieces.append(jax.nn.gelu(h, approximate=True).astype(BF))
        return jnp.concatenate(pieces, axis=1)

    def encode(part, hidden, row):
        square = jnp.zeros((block, 1), F32)
        for cols in columns:
            e = (dot(hidden, enc_out[:, cols]) + row[:, cols]).astype(BF)
            encoded[part, cols] = e
            e = e.astype(F32)
            square += jnp.sum(e * e, axis=1, keepdims=True)
        inv = lax.rsqrt(square / depth + 1e-05)
        pieces = []
        for cols in columns:
            piece = (encoded[part, cols].astype(F32) * inv * norm_gain[:, cols]).astype(BF)
            normed[part, cols] = piece
            pieces.append(piece)
        return jnp.concatenate(pieces, axis=1)

    def read_out(part, wide):
        k = dot(wide, w_keys[...]).astype(BF)
        keys[part, :] = k
        b_t[:, part] = k[:, :k.shape[1] // 2].T
        ws = w_step[...]
        raw = dot_t(wide, jnp.concatenate([ws, ws], axis=0)) + twice(step_bias[...])
        return jax.nn.sigmoid(raw).astype(BF)

    top, low = slice(0, block), slice(block, rows)
    hidden_top = hide(top)
    hidden_low = hide(low)
    for c in small[1:]:
        c.wait()
    wait_pieces(first[2:])
    row = jnp.sum(jnp.where(iota(pos.shape, 0) == cell - base, pos[...].astype(F32), 0.0), axis=0, keepdims=True)
    wide_top = encode(top, hidden_top, row)
    wide_low = encode(low, hidden_low, row)
    step = jnp.concatenate([read_out(top, wide_top), read_out(low, wide_low)], axis=0)
    cum = dot(lower, step) * twice(-0.0005 - 0.003 * code[...].astype(F32))
    g = split_two(jnp.exp(-cum), heads)
    f = split_two(jnp.exp(cum), heads)
    grow[...] = g
    fall[...] = f
    wait_pieces(big[:1])
    project(half * (heads // 2), w_o1, xs_o1, s_o1, heads, head_dim, normed, b_t[...], g, f[rows - EXTRA:])
    wait_pieces(big[1:])


def group_columns(w_any, like, half, group):
    size = like.shape[1]
    return w_any.at[:, pl.ds(pl.multiple_of((half * 2 + group) * size, size), size)]


def project_kernel(heads, head_dim, own, group, here_ref, normed, b_t, grow, fall, w, xs_ref, s_ref):
    half = (here_ref[0] + 1 - own) % 2
    rows = normed.shape[0]
    first = (half * 2 + group) * (xs_ref.shape[1] // head_dim)
    project(first, w, xs_ref, s_ref, heads, head_dim, normed, b_t[...], grow[...], fall[rows - EXTRA:])


def opened(ref):
    width = ref.shape[0] - EXTRA
    tail = ref[width:, :].astype(F32)
    return ref[:width, :].astype(F32), tail[0:1] + tail[1:2]


def close(ref, state, decay):
    width = ref.shape[0] - EXTRA
    ref[:width, :] = state.astype(BF)
    ref[width:, :] = decay_rows(decay)


def total_kernel(here_ref, mine_ref, got_ref, total_ref):
    mine, mine_decay = opened(mine_ref)
    got, got_decay = opened(got_ref)

    @pl.when(here_ref[0] % 2 == 1)
    def _():
        close(total_ref, mine_decay * got + mine, mine_decay * got_decay)

    @pl.when(here_ref[0] % 2 == 0)
    def _():
        close(total_ref, got_decay * mine + got, mine_decay * got_decay)


def step_kernel(first, final, reach, here_ref, total_ref, got_ref, before_ref, new_before_ref, new_total_ref):
    later = (here_ref[0] // reach) % 2 == 1
    got, got_decay = opened(got_ref)
    total, total_decay = opened(total_ref)

    def put_total(value):
        if final:
            new_total_ref[...] = value.astype(BF)
        else:
            close(new_total_ref, value, total_decay * got_decay)

    @pl.when(later)
    def _():
        if first:
            close(new_before_ref, got, got_decay)
        else:
            before, before_decay = opened(before_ref)
            close(new_before_ref, before + before_decay * got, before_decay * got_decay)
        put_total(total_decay * got + total)

    @pl.when(jnp.logical_not(later))
    def _():
        if first:
            close(new_before_ref, jnp.zeros_like(got), jnp.ones_like(got_decay))
        else:
            new_before_ref[...] = before_ref[...]
        put_total(got_decay * total + got)


def last_kernel(reach, here_ref, got_ref, before_ref, mine_ref, first_ref, keep_ref, send_ref):
    later = (here_ref[0] // reach) % 2 == 1
    got = got_ref[:keep_ref.shape[0], :].astype(F32)
    before, before_decay = opened(before_ref)
    before = before + jnp.where(later, before_decay, 0.0) * got

    @pl.when(here_ref[0] % 2 == 1)
    def _():
        state, decay = opened(first_ref)
        keep_ref[...] = (decay * before + state).astype(BF)
        send_ref[...] = before.astype(BF)

    @pl.when(here_ref[0] % 2 == 0)
    def _():
        state, decay = opened(mine_ref)
        send_ref[...] = (decay * before + state).astype(BF)
        keep_ref[...] = before.astype(BF)


def inner_kernel(heads, head_dim, own, group, fresh, here_ref, normed, keys, fall, skip, w_out_any, w, xs, *refs):
    half = (here_ref[0] + 1 - own) % 2
    rows = keys.shape[0]
    width = keys.shape[1] // 2
    size = xs.shape[1]
    if fresh:
        u, v, w_rows, scores_ref, sem = refs
    else:
        scores_ref, u, v, w_rows, sem = refs
    start = pl.multiple_of((half * 2 + group) * size, size)
    copies = [in_pieces(w_out_any.at[pl.ds(start, size), :], w_rows, sem, 0)]
    start_pieces(copies)
    if fresh:
        scores = dot_t(keys[:, width:], keys[:, :width])
        scores_ref[...] = jnp.where(iota((rows, rows), 0) >= iota((rows, rows), 1), scores, 0.0).astype(BF)
    scores = scores_ref[...]
    mid = rows // 2
    both = jnp.broadcast_to(jnp.concatenate([skip[...], skip[...]], axis=1), (EXTRA, 2 * heads))
    skip_two = split_two(both, heads)
    first = (half * 2 + group) * (size // head_dim)
    for j in range(size // CHUNK):
        cols = slice(j * CHUNK, (j + 1) * CHUNK)
        z = dot(normed[...], compact(w, j, 1)).astype(BF).astype(F32)
        gate = z * jax.nn.sigmoid(z)
        spread = spread_heads(first + j * (CHUNK // head_dim), heads, head_dim)
        gain = dot(skip_two, spread)[0:1]
        grown = dot(fall[...], spread)
        grown = grown * gate
        u[:, cols] = grown.astype(BF)
        top = dot(scores[:mid, :mid], xs[:mid, cols])
        low = dot(scores[mid:], xs[:, cols])
        for part, inner in ((slice(0, mid), top), (slice(mid, rows), low)):
            v[part, cols] = (grown[part] * (inner + gain * xs[part, cols].astype(F32))).astype(BF)
    wait_pieces(copies)


def mix_kernel(head_dim, places, last, here_ref, keys, base, gain, *refs):
    many = len(places)
    states, us, vs, ws = (refs[i * many:(i + 1) * many] for i in range(4))
    out = refs[4 * many]
    width = keys.shape[1] // 2
    size = us[0].shape[1]
    starts = [((here_ref[0] + 1 - own) % 2 * 2 + group) * size for own, group in places]
    same = (iota((CHUNK, CHUNK), 0) // head_dim) == (iota((CHUNK, CHUNK), 1) // head_dim)
    mean = jnp.where(same, 1.0 / head_dim, 0.0).astype(BF)
    work = []
    for state, u, v in zip(states, us, vs):
        for j in range(size // CHUNK):
            cols = slice(j * CHUNK, (j + 1) * CHUNK)
            carried = dot(keys[:, width:], state[:, cols])
            g = v[:, cols].astype(F32) + u[:, cols].astype(F32) * carried
            work.append((g, dot((g * g).astype(BF), mean)))
    mixed = []
    for i in range(many):
        parts = []
        for j in range(size // CHUNK):
            g, m = work[i * (size // CHUNK) + j]
            row = gain[:, pl.ds(pl.multiple_of(starts[i] + j * CHUNK, CHUNK), CHUNK)]
            parts.append((g * lax.rsqrt(m + 1e-05) * row).astype(BF))
        mixed.append(jnp.concatenate(parts, axis=1))
    copies = []
    for n in range(base.shape[1] // CHUNK):
        cols = slice(n * CHUNK, (n + 1) * CHUNK)
        total = base[:, cols].astype(F32)
        for part, w in zip(mixed, ws):
            total = total + dot(part, w[:, cols])
        if last:
            buf, sem = refs[4 * many + 1:]
            buf[:, cols] = total.astype(buf.dtype)
            copies.append(pltpu.make_async_copy(buf.at[:, cols], out.at[:, cols], sem.at[n]))
            copies[-1].start()
        else:
            out[:, cols] = total.astype(out.dtype)
    for c in copies:
        c.wait()


def body(frames, patch_cell, enc_in, enc_bias, enc_out, pos_table, norm_gain, w_pair, w_keys, w_step,
         step_bias, decay_code, skip_gain, out_gain, w_out):
    rows = frames.shape[0]
    pix = frames.shape[2]
    depth = enc_out.shape[1]
    heads = w_step.shape[1]
    head_dim = w_pair.shape[1] // (2 * heads)
    width = w_keys.shape[1] // 2
    size = heads * head_dim // 4
    peers = lax.axis_size("tm")
    here = lax.axis_index("tm").astype(jnp.int32).reshape(1)
    row = lambda v: v.reshape(1, -1)
    far = lambda v: pltpu.with_memory_space_constraint(v, pltpu.HBM)
    near = lambda shape, dtype=BF: pltpu.VMEM(shape, dtype)
    sems = lambda n: pltpu.SemaphoreType.DMA((n,))
    pair = lambda by: [(i, i ^ by) for i in range(peers)]
    after = lambda value, *first: lax.optimization_barrier((value,) + first)[0]

    def call(kernel, name, outs, ins, scratch=(), flops=0, out_spec=VM):
        specs = [spec for spec, _ in ins]
        cost = pl.CostEstimate(flops=flops, bytes_accessed=2**20, transcendentals=0)
        return pl.pallas_call(kernel, out_shape=tuple(outs), in_specs=specs, out_specs=(out_spec,) * len(outs),
                              scratch_shapes=list(scratch), compiler_params=params(24), name=name,
                              cost_estimate=cost)(*[v for _, v in ins])

    vm = lambda *vs: [(VM, v) for v in vs]
    hbm = lambda *vs: [(pl.BlockSpec(memory_space=pltpu.HBM), far(v)) for v in vs]
    where = [(SM, here)]

    part, message, weight = near((rows, size)), near((width + EXTRA, size)), near((depth, 2 * size))
    encoded, normed, keys, b_t, grow, fall, skip, gain, xs_o1, s_o1, w_o1, w_m1, w_o2, w_m2 = call(
        functools.partial(encode_kernel, heads, head_dim), "encode",
        (near((rows, depth)), near((rows, depth)), near((rows, 2 * width)), near((width, rows)),
         near((rows, 2 * heads)), near((rows, 2 * heads)), near((1, heads), F32), near((1, heads * head_dim), F32),
         part, message) + (weight,) * 4,
        where + [(SM, patch_cell)] + hbm(frames.reshape(rows, pix), enc_in, row(enc_bias), enc_out, pos_table, row(norm_gain),
                                         w_keys, w_step.T, row(step_bias), row(decay_code), row(skip_gain), row(out_gain),
                                         w_pair),
        [near((rows, pix)), near((pix, depth)), near((1, depth), F32), near((depth, depth)), near((EXTRA, depth)),
         near((1, depth), F32), near((depth, 2 * width)), near((heads, depth)), near((1, heads), F32),
         near((1, heads), jnp.int32), sems(7), pltpu.SemaphoreType.DMA((9, 2))],
        rows * depth * depth)

    long, short = 8 * rows * depth * size, rows * depth * size // 4

    def projected(own, group, w):
        return call(functools.partial(project_kernel, heads, head_dim, own, group), "project",
                    (part, message), where + vm(normed, b_t, grow, fall, w), (), long)

    scores = []

    def inner(own, group, w, xs, flops):
        outs = call(functools.partial(inner_kernel, heads, head_dim, own, group, not scores), "inner",
                    (part, part, near((size, depth))) + (() if scores else (near((rows, rows)),)),
                    where + vm(normed, keys, fall, skip) + hbm(w_out) + vm(w, xs, *scores),
                    [pltpu.SemaphoreType.DMA((1, 2))], flops)
        scores.extend(outs[3:])
        return outs[:3]

    def mixed(places, base, last, *groups):
        states, us, vs, ws = zip(*groups)
        shape = sds((rows, depth), BF) if last else near((rows, depth), F32)
        return call(functools.partial(mix_kernel, head_dim, places, last), "mix", (shape,),
                    where + vm(keys, base, gain, *states, *us, *vs, *ws),
                    [near((rows, depth)), sems(depth // CHUNK)] if last else [], short,
                    ANY if last else VM)[0]

    totals, befores, arriving = [None, None], [None, None], [None, None]
    done = {}

    def work(own, group, w, xs, stamp, flops):
        done[own, group] = inner(own, group, w, after(xs, stamp), flops)
        return done[own, group][0]

    def start_total(i, mine, theirs):
        totals[i], = call(total_kernel, "total", (message,), where + vm(mine, theirs))
        befores[i] = totals[i]
        arriving[i] = lax.ppermute(totals[i], "tm", pair(2))

    def advance(i, reach, arrived):
        final = reach * 4 >= peers
        befores[i], totals[i] = call(
            functools.partial(step_kernel, reach == 2, final, reach), "step",
            (message, near((width, size)) if final else message), where + vm(totals[i], arrived, befores[i]))
        arriving[i] = lax.ppermute(totals[i], "tm", pair(2 * reach))

    def finish(i, arrived, mine, theirs):
        keep, send = call(functools.partial(last_kernel, peers // 2), "last", (near((width, size)),) * 2,
                          where + vm(arrived, befores[i], mine, theirs))
        return keep, lax.ppermute(send, "tm", pair(1))

    got_1 = lax.ppermute(s_o1, "tm", pair(1))
    xs_m1, s_m1 = projected(1, 0, w_m1)
    start_total(0, s_m1, got_1)
    xs_o2, s_o2 = projected(0, 1, after(w_o2, totals[0]))
    got_2 = lax.ppermute(s_o2, "tm", pair(1))
    xs_m2, s_m2 = projected(1, 1, after(w_m2, s_o2))
    start_total(1, s_m2, got_2)
    stamp = work(0, 0, w_o1, xs_o1, totals[1], long)
    advance(0, 2, after(arriving[0], stamp))
    stamp = work(1, 0, w_m1, xs_m1, befores[0], short)
    stamp = work(1, 1, w_m2, xs_m2, stamp, short)
    advance(1, 2, after(arriving[1], stamp))
    reach = 4
    while reach * 2 < peers:
        for i in range(2):
            advance(i, reach, arriving[i])
        reach *= 2
    keep_1, sent_1 = finish(0, after(arriving[0], befores[1]), s_m1, got_1)
    stamp = work(0, 1, w_o2, xs_o2, keep_1, short)
    mixing = mixed(((1, 0),), after(encoded, stamp), False, (keep_1, *done[1, 0]))
    keep_2, sent_2 = finish(1, after(arriving[1], mixing), s_m2, got_2)
    mixing = mixed(((0, 0), (1, 1)), after(mixing, keep_2), False, (sent_1, *done[0, 0]), (keep_2, *done[1, 1]))
    return mixed(((0, 1),), mixing, True, (sent_2, *done[0, 1])).reshape(rows, 1, depth)


def solution(mesh):
    placed = (P("tm", "space", None), P("space")) + (P(),) * 13
    return jax.shard_map(body, mesh=mesh, in_specs=placed, out_specs=P("tm", "space", None), check_vma=False)
```

```python
import functools

import jax
import jax.numpy as jnp
from jax import lax
from jax.experimental import pallas as pl
from jax.experimental.pallas import tpu as pltpu
from jax.sharding import PartitionSpec as P

BF = jnp.bfloat16
F32 = jnp.float32
VM = pl.BlockSpec(memory_space=pltpu.VMEM)
SM = pl.BlockSpec(memory_space=pltpu.SMEM)
ANY = pl.BlockSpec(memory_space=pl.ANY)
LANES = 128
CHUNK = 256
EXTRA = 16


def dot(a, b):
    return jnp.dot(a, b, preferred_element_type=F32)


def dot_t(a, b):
    return lax.dot_general(a, b, (((1,), (1,)), ((), ())), preferred_element_type=F32)


def iota(shape, axis):
    return lax.broadcasted_iota(jnp.int32, shape, axis)


def params(mib):
    return pltpu.CompilerParams(vmem_limit_bytes=mib * 2**20)


def sds(shape, dtype):
    return jax.ShapeDtypeStruct(shape, dtype)


def spread_heads(first_head, heads, head_dim):
    row = iota((2 * heads, CHUNK), 0)
    lane = iota((2 * heads, CHUNK), 1)
    row = jnp.where(row < heads, row, row - heads)
    return (row == first_head + lane // head_dim).astype(F32).astype(BF)


def split_two(value, heads):
    high = value.astype(BF).astype(F32)
    return jnp.where(iota(value.shape, 1) < heads, high, value - high).astype(BF)


def pick_half(tile_a, tile_b, part):
    half = LANES // 2
    low = iota(tile_a.shape, 1) < half
    if part == 0:
        return jnp.where(low, tile_a, pltpu.roll(tile_b, half, 1))
    return jnp.where(low, pltpu.roll(tile_a, half, 1), tile_b)


def compact(ref, j, part):
    start = j * 2 * CHUNK
    tiles = [ref[:, start + i:start + i + LANES] for i in range(0, 2 * CHUNK, LANES)]
    pairs = [pick_half(tiles[i], tiles[i + 1], part) for i in range(0, len(tiles), 2)]
    return jnp.concatenate(pairs, axis=1)


def project(first, w, xs_ref, s_ref, heads, head_dim, normed, b_t, grow, fall_end):
    width = b_t.shape[0]
    later = []
    for j in range(xs_ref.shape[1] // CHUNK):
        cols = slice(j * CHUNK, (j + 1) * CHUNK)
        spread = spread_heads(first + j * (CHUNK // head_dim), heads, head_dim)
        x = dot(normed[...], compact(w, j, 0)).astype(BF)
        scaled = (x.astype(F32) * dot(grow, spread)).astype(BF)
        xs_ref[:, cols] = scaled
        decay = dot(fall_end, spread)[EXTRA - 1:EXTRA]
        if s_ref.shape[0] > width:
            next_first = first + (xs_ref.shape[1] + j * CHUNK) // head_dim
            next_decay = dot(fall_end, spread_heads(next_first, heads, head_dim))[EXTRA - 1:EXTRA]
            s_ref[width:width + EXTRA, cols] = decay_rows((decay, next_decay))
        later.append((cols, scaled, decay))
    for cols, scaled, decay in later:
        s_ref[0:width, cols] = (dot(b_t, scaled) * decay).astype(BF)


def decay_rows(values):
    row = iota((EXTRA, values[0].shape[1]), 0)
    out = jnp.zeros(row.shape, F32)
    for k, value in enumerate(values):
        high = value.astype(BF).astype(F32)
        out = jnp.where(row == 2 * k, high, jnp.where(row == 2 * k + 1, value - high, out))
    return out.astype(BF)


def in_pieces(src, dst, sem, slot):
    block = dst.shape[0] // 2

    def piece(i):
        part = pl.ds(pl.multiple_of(i * block, block), block)
        return pltpu.make_async_copy(src.at[part, :], dst.at[part, :], sem.at[slot, i])

    return piece


def start_pieces(pieces):
    def go(i, carry):
        for piece in pieces:
            piece(i).start()
        return carry

    lax.fori_loop(0, 2, go, 0)


def wait_pieces(pieces):
    def go(i, carry):
        for piece in pieces:
            piece(i).wait()
        return carry

    lax.fori_loop(0, 2, go, 0)


def encode_kernel(heads, head_dim, here_ref, cell_ref, frames_any, enc_in_any, bias_any, enc_out_any, pos_any, gain_any,
                  w_keys_any, w_step_any, step_bias_any, code_any, skip_any, out_gain_any, w_pair_any,
                  encoded, normed, keys, b_t, grow, fall, skip, out_gain, xs_o1, s_o1, w_o1, w_m1, w_o2, w_m2,
                  frames, enc_in, bias, enc_out, pos, norm_gain, w_keys, w_step, step_bias, code, sem, wsem):
    half = 1 - here_ref[0] % 2
    cell = cell_ref[0]
    base = pl.multiple_of((cell // EXTRA) * EXTRA, EXTRA)
    small = [pltpu.make_async_copy(src, dst, sem.at[i]) for i, (src, dst) in enumerate((
        (bias_any, bias), (pos_any.at[pl.ds(base, EXTRA), :], pos), (gain_any, norm_gain), (step_bias_any, step_bias),
        (code_any, code), (skip_any, skip), (out_gain_any, out_gain)))]
    first = [in_pieces(src, dst, wsem, i) for i, (src, dst) in enumerate((
        (frames_any, frames), (enc_in_any, enc_in), (enc_out_any, enc_out), (w_keys_any, w_keys), (w_step_any, w_step)))]
    big = [in_pieces(group_columns(w_pair_any, dst, which, group), dst, wsem, 5 + i) for i, (which, group, dst) in enumerate((
        (half, 0, w_o1), (1 - half, 0, w_m1), (half, 1, w_o2), (1 - half, 1, w_m2)))]
    start_pieces(first[:2])
    for c in small:
        c.start()
    start_pieces(first[2:])
    rows, depth = encoded.shape
    block = rows // 2
    lower = (iota((rows, rows), 0) >= iota((rows, rows), 1)).astype(F32).astype(BF)
    small[0].wait()
    wait_pieces(first[:2])
    start_pieces(big)
    twice = lambda v: jnp.concatenate([v, v], axis=1)
    columns = [slice(j, j + CHUNK) for j in range(0, depth, CHUNK)]

    def hide(part):
        pieces = []
        for cols in columns:
            h = dot(frames[part, :], enc_in[:, cols]) + bias[:, cols]
            pieces.append(jax.nn.gelu(h, approximate=True).astype(BF))
        return jnp.concatenate(pieces, axis=1)

    def encode(part, hidden, row):
        square = jnp.zeros((block, 1), F32)
        for cols in columns:
            e = (dot(hidden, enc_out[:, cols]) + row[:, cols]).astype(BF)
            encoded[part, cols] = e
            e = e.astype(F32)
            square += jnp.sum(e * e, axis=1, keepdims=True)
        inv = lax.rsqrt(square / depth + 1e-05)
        pieces = []
        for cols in columns:
            piece = (encoded[part, cols].astype(F32) * inv * norm_gain[:, cols]).astype(BF)
            normed[part, cols] = piece
            pieces.append(piece)
        return jnp.concatenate(pieces, axis=1)

    def read_out(part, wide):
        k = dot(wide, w_keys[...]).astype(BF)
        keys[part, :] = k
        b_t[:, part] = k[:, :k.shape[1] // 2].T
        ws = w_step[...]
        raw = dot_t(wide, jnp.concatenate([ws, ws], axis=0)) + twice(step_bias[...])
        return jax.nn.sigmoid(raw).astype(BF)

    top, low = slice(0, block), slice(block, rows)
    hidden_top = hide(top)
    hidden_low = hide(low)
    for c in small[1:]:
        c.wait()
    wait_pieces(first[2:])
    row = jnp.sum(jnp.where(iota(pos.shape, 0) == cell - base, pos[...].astype(F32), 0.0), axis=0, keepdims=True)
    wide_top = encode(top, hidden_top, row)
    wide_low = encode(low, hidden_low, row)
    step = jnp.concatenate([read_out(top, wide_top), read_out(low, wide_low)], axis=0)
    cum = dot(lower, step) * twice(-0.0005 - 0.003 * code[...].astype(F32))
    g = split_two(jnp.exp(-cum), heads)
    f = split_two(jnp.exp(cum), heads)
    grow[...] = g
    fall[...] = f
    wait_pieces(big[:1])
    project(half * (heads // 2), w_o1, xs_o1, s_o1, heads, head_dim, normed, b_t[...], g, f[rows - EXTRA:])
    wait_pieces(big[1:])


def group_columns(w_any, like, half, group):
    size = like.shape[1]
    return w_any.at[:, pl.ds(pl.multiple_of((half * 2 + group) * size, size), size)]


def project_kernel(heads, head_dim, own, group, here_ref, normed, b_t, grow, fall, w, xs_ref, s_ref):
    half = (here_ref[0] + 1 - own) % 2
    rows = normed.shape[0]
    first = (half * 2 + group) * (xs_ref.shape[1] // head_dim)
    project(first, w, xs_ref, s_ref, heads, head_dim, normed, b_t[...], grow[...], fall[rows - EXTRA:])


def state_of(ref, width):
    return ref[:width, :].astype(F32)


def decays_of(ref):
    tail = ref[ref.shape[0] - EXTRA:, :].astype(F32)
    return tail[0:1] + tail[1:2], tail[2:3] + tail[3:4]


def put(ref, width, state, decays):
    ref[:width, :] = state.astype(BF)
    if ref.shape[0] > width:
        ref[width:, :] = decay_rows(decays)


def times(one, other):
    return one[0] * other[0], one[1] * other[1]


def total_kernel(group, width, here_ref, mine_ref, got_ref, mine_first, got_first, total_ref):
    mine, got = state_of(mine_ref, width), state_of(got_ref, width)
    mine_decays, got_decays = decays_of(mine_first), decays_of(got_first)
    both = times(mine_decays, got_decays)

    @pl.when(here_ref[0] % 2 == 1)
    def _():
        put(total_ref, width, mine_decays[group] * got + mine, both)

    @pl.when(here_ref[0] % 2 == 0)
    def _():
        put(total_ref, width, got_decays[group] * mine + got, both)


def step_kernel(group, width, reach, here_ref, total_ref, got_ref, total_first, got_first, *refs):
    begin = len(refs) == 2
    new_before_ref, new_total_ref = refs[-2:]
    later = (here_ref[0] // reach) % 2 == 1
    got, total = state_of(got_ref, width), state_of(total_ref, width)
    got_decays, total_decays = decays_of(got_first), decays_of(total_first)
    both = times(total_decays, got_decays)

    @pl.when(later)
    def _():
        if begin:
            put(new_before_ref, width, got, got_decays)
        else:
            before_decays = decays_of(refs[1])
            put(new_before_ref, width, state_of(refs[0], width) + before_decays[group] * got,
                times(before_decays, got_decays))
        put(new_total_ref, width, total_decays[group] * got + total, both)

    @pl.when(jnp.logical_not(later))
    def _():
        if begin:
            one = jnp.ones_like(got_decays[0])
            put(new_before_ref, width, jnp.zeros_like(got), (one, one))
        else:
            put(new_before_ref, width, state_of(refs[0], width), decays_of(refs[1]))
        put(new_total_ref, width, got_decays[group] * total + got, both)


def last_kernel(group, reach, here_ref, got_ref, before_ref, before_first, mine_ref, theirs_ref, mine_first, theirs_first,
                keep_ref, send_ref):
    width = keep_ref.shape[0]
    later = (here_ref[0] // reach) % 2 == 1
    before_decay = jnp.where(later, decays_of(before_first)[group], 0.0)
    before = state_of(before_ref, width) + before_decay * state_of(got_ref, width)

    @pl.when(here_ref[0] % 2 == 1)
    def _():
        keep_ref[...] = (decays_of(theirs_first)[group] * before + state_of(theirs_ref, width)).astype(BF)
        send_ref[...] = before.astype(BF)

    @pl.when(here_ref[0] % 2 == 0)
    def _():
        send_ref[...] = (decays_of(mine_first)[group] * before + state_of(mine_ref, width)).astype(BF)
        keep_ref[...] = before.astype(BF)


def inner_kernel(heads, head_dim, own, group, fresh, here_ref, normed, keys, fall, skip, w_out_any, w, xs, *refs):
    half = (here_ref[0] + 1 - own) % 2
    rows = keys.shape[0]
    width = keys.shape[1] // 2
    size = xs.shape[1]
    if fresh:
        u, v, w_rows, scores_ref, sem = refs
    else:
        scores_ref, u, v, w_rows, sem = refs
    start = pl.multiple_of((half * 2 + group) * size, size)
    copies = [in_pieces(w_out_any.at[pl.ds(start, size), :], w_rows, sem, 0)]
    start_pieces(copies)
    if fresh:
        scores = dot_t(keys[:, width:], keys[:, :width])
        scores_ref[...] = jnp.where(iota((rows, rows), 0) >= iota((rows, rows), 1), scores, 0.0).astype(BF)
    scores = scores_ref[...]
    mid = rows // 2
    both = jnp.broadcast_to(jnp.concatenate([skip[...], skip[...]], axis=1), (EXTRA, 2 * heads))
    skip_two = split_two(both, heads)
    first = (half * 2 + group) * (size // head_dim)
    for j in range(size // CHUNK):
        cols = slice(j * CHUNK, (j + 1) * CHUNK)
        z = dot(normed[...], compact(w, j, 1)).astype(BF).astype(F32)
        gate = z * jax.nn.sigmoid(z)
        spread = spread_heads(first + j * (CHUNK // head_dim), heads, head_dim)
        gain = dot(skip_two, spread)[0:1]
        grown = dot(fall[...], spread)
        grown = grown * gate
        u[:, cols] = grown.astype(BF)
        top = dot(scores[:mid, :mid], xs[:mid, cols])
        low = dot(scores[mid:], xs[:, cols])
        for part, inner in ((slice(0, mid), top), (slice(mid, rows), low)):
            v[part, cols] = (grown[part] * (inner + gain * xs[part, cols].astype(F32))).astype(BF)
    wait_pieces(copies)


def mix_kernel(head_dim, places, last, here_ref, keys, base, gain, *refs):
    many = len(places)
    states, us, vs, ws = (refs[i * many:(i + 1) * many] for i in range(4))
    out = refs[4 * many]
    width = keys.shape[1] // 2
    size = us[0].shape[1]
    starts = [((here_ref[0] + 1 - own) % 2 * 2 + group) * size for own, group in places]
    same = (iota((CHUNK, CHUNK), 0) // head_dim) == (iota((CHUNK, CHUNK), 1) // head_dim)
    mean = jnp.where(same, 1.0 / head_dim, 0.0).astype(BF)
    work = []
    for state, u, v in zip(states, us, vs):
        for j in range(size // CHUNK):
            cols = slice(j * CHUNK, (j + 1) * CHUNK)
            carried = dot(keys[:, width:], state[:, cols])
            g = v[:, cols].astype(F32) + u[:, cols].astype(F32) * carried
            work.append((g, dot((g * g).astype(BF), mean)))
    mixed = []
    for i in range(many):
        parts = []
        for j in range(size // CHUNK):
            g, m = work[i * (size // CHUNK) + j]
            row = gain[:, pl.ds(pl.multiple_of(starts[i] + j * CHUNK, CHUNK), CHUNK)]
            parts.append((g * lax.rsqrt(m + 1e-05) * row).astype(BF))
        mixed.append(jnp.concatenate(parts, axis=1))
    copies = []
    for n in range(base.shape[1] // CHUNK):
        cols = slice(n * CHUNK, (n + 1) * CHUNK)
        total = base[:, cols].astype(F32)
        for part, w in zip(mixed, ws):
            total = total + dot(part, w[:, cols])
        if last:
            buf, sem = refs[4 * many + 1:]
            buf[:, cols] = total.astype(buf.dtype)
            copies.append(pltpu.make_async_copy(buf.at[:, cols], out.at[:, cols], sem.at[n]))
            copies[-1].start()
        else:
            out[:, cols] = total.astype(out.dtype)
    for c in copies:
        c.wait()


def body(frames, patch_cell, enc_in, enc_bias, enc_out, pos_table, norm_gain, w_pair, w_keys, w_step,
         step_bias, decay_code, skip_gain, out_gain, w_out):
    rows = frames.shape[0]
    pix = frames.shape[2]
    depth = enc_out.shape[1]
    heads = w_step.shape[1]
    head_dim = w_pair.shape[1] // (2 * heads)
    width = w_keys.shape[1] // 2
    size = heads * head_dim // 4
    peers = lax.axis_size("tm")
    here = lax.axis_index("tm").astype(jnp.int32).reshape(1)
    row = lambda v: v.reshape(1, -1)
    far = lambda v: pltpu.with_memory_space_constraint(v, pltpu.HBM)
    near = lambda shape, dtype=BF: pltpu.VMEM(shape, dtype)
    sems = lambda n: pltpu.SemaphoreType.DMA((n,))
    pair = lambda by: [(i, i ^ by) for i in range(peers)]
    after = lambda value, *first: lax.optimization_barrier((value,) + first)[0]

    def call(kernel, name, outs, ins, scratch=(), flops=0, out_spec=VM):
        specs = [spec for spec, _ in ins]
        cost = pl.CostEstimate(flops=flops, bytes_accessed=2**20, transcendentals=0)
        return pl.pallas_call(kernel, out_shape=tuple(outs), in_specs=specs, out_specs=(out_spec,) * len(outs),
                              scratch_shapes=list(scratch), compiler_params=params(24), name=name,
                              cost_estimate=cost)(*[v for _, v in ins])

    vm = lambda *vs: [(VM, v) for v in vs]
    hbm = lambda *vs: [(pl.BlockSpec(memory_space=pltpu.HBM), far(v)) for v in vs]
    where = [(SM, here)]

    part, message, weight = near((rows, size)), near((width + EXTRA, size)), near((depth, 2 * size))
    kinds = (message, near((width, size)))
    encoded, normed, keys, b_t, grow, fall, skip, gain, xs_o1, s_o1, w_o1, w_m1, w_o2, w_m2 = call(
        functools.partial(encode_kernel, heads, head_dim), "encode",
        (near((rows, depth)), near((rows, depth)), near((rows, 2 * width)), near((width, rows)),
         near((rows, 2 * heads)), near((rows, 2 * heads)), near((1, heads), F32), near((1, heads * head_dim), F32),
         part, message) + (weight,) * 4,
        where + [(SM, patch_cell)] + hbm(frames.reshape(rows, pix), enc_in, row(enc_bias), enc_out, pos_table, row(norm_gain),
                                         w_keys, w_step.T, row(step_bias), row(decay_code), row(skip_gain), row(out_gain),
                                         w_pair),
        [near((rows, pix)), near((pix, depth)), near((1, depth), F32), near((depth, depth)), near((EXTRA, depth)),
         near((1, depth), F32), near((depth, 2 * width)), near((heads, depth)), near((1, heads), F32),
         near((1, heads), jnp.int32), sems(7), pltpu.SemaphoreType.DMA((9, 2))],
        rows * depth * depth)

    long, short = 8 * rows * depth * size, rows * depth * size // 4

    def projected(own, group, w):
        return call(functools.partial(project_kernel, heads, head_dim, own, group), "project",
                    (part, kinds[group]), where + vm(normed, b_t, grow, fall, w), (), long)

    scores = []

    def inner(own, group, w, xs, flops):
        outs = call(functools.partial(inner_kernel, heads, head_dim, own, group, not scores), "inner",
                    (part, part, near((size, depth))) + (() if scores else (near((rows, rows)),)),
                    where + vm(normed, keys, fall, skip) + hbm(w_out) + vm(w, xs, *scores),
                    [pltpu.SemaphoreType.DMA((1, 2))], flops)
        scores.extend(outs[3:])
        return outs[:3]

    def mixed(places, base, last, *groups):
        states, us, vs, ws = zip(*groups)
        shape = sds((rows, depth), BF) if last else near((rows, depth), F32)
        return call(functools.partial(mix_kernel, head_dim, places, last), "mix", (shape,),
                    where + vm(keys, base, gain, *states, *us, *vs, *ws),
                    [near((rows, depth)), sems(depth // CHUNK)] if last else [], short,
                    ANY if last else VM)[0]

    totals, befores, arriving, firsts = [None, None], [None, None], [None, None], {}
    done = {}

    def work(own, group, w, xs, stamp, flops):
        done[own, group] = inner(own, group, w, after(xs, stamp), flops)
        return done[own, group][0]

    def start_total(i, mine, theirs):
        totals[i], = call(functools.partial(total_kernel, i, width), "total", (kinds[i],),
                          where + vm(mine, theirs, s_m1, got_1))
        arriving[i] = lax.ppermute(totals[i], "tm", pair(2))

    def advance(i, reach, arrived):
        if i == 0:
            firsts[reach] = totals[0], arrived, befores[0]
        own, theirs, before = firsts[reach]
        carried = [] if reach == 2 else [befores[i], before]
        final = reach * 4 >= peers
        befores[i], totals[i] = call(
            functools.partial(step_kernel, i, width, reach), "step", (kinds[i], kinds[1] if final else kinds[i]),
            where + vm(totals[i], arrived, own, theirs, *carried))
        arriving[i] = lax.ppermute(totals[i], "tm", pair(2 * reach))

    def finish(i, arrived, mine, theirs):
        keep, send = call(functools.partial(last_kernel, i, peers // 2), "last", (kinds[1],) * 2,
                          where + vm(arrived, befores[i], befores[0], mine, theirs, s_m1, got_1))
        return keep, lax.ppermute(send, "tm", pair(1))

    got_1 = lax.ppermute(s_o1, "tm", pair(1))
    xs_m1, s_m1 = projected(1, 0, w_m1)
    start_total(0, s_m1, got_1)
    xs_o2, s_o2 = projected(0, 1, after(w_o2, totals[0]))
    got_2 = lax.ppermute(s_o2, "tm", pair(1))
    xs_m2, s_m2 = projected(1, 1, after(w_m2, s_o2))
    start_total(1, s_m2, got_2)
    stamp = work(0, 0, w_o1, xs_o1, totals[1], long)
    advance(0, 2, after(arriving[0], stamp))
    stamp = work(1, 0, w_m1, xs_m1, befores[0], short)
    stamp = work(1, 1, w_m2, xs_m2, stamp, short)
    advance(1, 2, after(arriving[1], stamp))
    reach = 4
    while reach * 2 < peers:
        for i in range(2):
            advance(i, reach, arriving[i])
        reach *= 2
    keep_1, sent_1 = finish(0, after(arriving[0], befores[1]), s_m1, got_1)
    stamp = work(0, 1, w_o2, xs_o2, keep_1, short)
    mixing = mixed(((1, 0),), after(encoded, stamp), False, (keep_1, *done[1, 0]))
    keep_2, sent_2 = finish(1, after(arriving[1], mixing), s_m2, got_2)
    mixing = mixed(((0, 0), (1, 1)), after(mixing, keep_2), False, (sent_1, *done[0, 0]), (keep_2, *done[1, 1]))
    return mixed(((0, 1),), mixing, True, (sent_2, *done[0, 1])).reshape(rows, 1, depth)


def solution(mesh):
    placed = (P("tm", "space", None), P("space")) + (P(),) * 13
    return jax.shard_map(body, mesh=mesh, in_specs=placed, out_specs=P("tm", "space", None), check_vma=False)
```

```python
import functools

import jax
import jax.numpy as jnp
from jax import lax
from jax.experimental import pallas as pl
from jax.experimental.pallas import tpu as pltpu
from jax.sharding import PartitionSpec as P

BF = jnp.bfloat16
F32 = jnp.float32
VM = pl.BlockSpec(memory_space=pltpu.VMEM)
SM = pl.BlockSpec(memory_space=pltpu.SMEM)
ANY = pl.BlockSpec(memory_space=pl.ANY)
LANES = 128
CHUNK = 256
EXTRA = 16


def dot(a, b):
    return jnp.dot(a, b, preferred_element_type=F32)


def dot_t(a, b):
    return lax.dot_general(a, b, (((1,), (1,)), ((), ())), preferred_element_type=F32)


def iota(shape, axis):
    return lax.broadcasted_iota(jnp.int32, shape, axis)


def params(mib):
    return pltpu.CompilerParams(vmem_limit_bytes=mib * 2**20)


def sds(shape, dtype):
    return jax.ShapeDtypeStruct(shape, dtype)


def spread_heads(first_head, heads, head_dim):
    row = iota((2 * heads, CHUNK), 0)
    lane = iota((2 * heads, CHUNK), 1)
    row = jnp.where(row < heads, row, row - heads)
    return (row == first_head + lane // head_dim).astype(F32).astype(BF)


def split_two(value, heads):
    high = value.astype(BF).astype(F32)
    return jnp.where(iota(value.shape, 1) < heads, high, value - high).astype(BF)


def pick_half(tile_a, tile_b, part):
    half = LANES // 2
    low = iota(tile_a.shape, 1) < half
    if part == 0:
        return jnp.where(low, tile_a, pltpu.roll(tile_b, half, 1))
    return jnp.where(low, pltpu.roll(tile_a, half, 1), tile_b)


def compact(ref, j, part):
    start = j * 2 * CHUNK
    tiles = [ref[:, start + i:start + i + LANES] for i in range(0, 2 * CHUNK, LANES)]
    pairs = [pick_half(tiles[i], tiles[i + 1], part) for i in range(0, len(tiles), 2)]
    return jnp.concatenate(pairs, axis=1)


def project(first, w, xs_ref, s_ref, heads, head_dim, normed, b_t, grow, fall_end):
    width = b_t.shape[0]
    later = []
    for j in range(xs_ref.shape[1] // CHUNK):
        cols = slice(j * CHUNK, (j + 1) * CHUNK)
        spread = spread_heads(first + j * (CHUNK // head_dim), heads, head_dim)
        x = dot(normed[...], compact(w, j, 0)).astype(BF)
        scaled = (x.astype(F32) * dot(grow, spread)).astype(BF)
        xs_ref[:, cols] = scaled
        decay = dot(fall_end, spread)[EXTRA - 1:EXTRA]
        if s_ref.shape[0] > width:
            next_first = first + (xs_ref.shape[1] + j * CHUNK) // head_dim
            next_decay = dot(fall_end, spread_heads(next_first, heads, head_dim))[EXTRA - 1:EXTRA]
            s_ref[width:width + EXTRA, cols] = decay_rows((decay, next_decay))
        later.append((cols, scaled, decay))
    for cols, scaled, decay in later:
        s_ref[0:width, cols] = (dot(b_t, scaled) * decay).astype(BF)


def decay_rows(values):
    row = iota((EXTRA, values[0].shape[1]), 0)
    out = jnp.zeros(row.shape, F32)
    for k, value in enumerate(values):
        high = value.astype(BF).astype(F32)
        out = jnp.where(row == 2 * k, high, jnp.where(row == 2 * k + 1, value - high, out))
    return out.astype(BF)


def in_pieces(src, dst, sem, slot):
    block = dst.shape[0] // 2

    def piece(i):
        part = pl.ds(pl.multiple_of(i * block, block), block)
        return pltpu.make_async_copy(src.at[part, :], dst.at[part, :], sem.at[slot, i])

    return piece


def start_pieces(pieces):
    def go(i, carry):
        for piece in pieces:
            piece(i).start()
        return carry

    lax.fori_loop(0, 2, go, 0)


def wait_pieces(pieces):
    def go(i, carry):
        for piece in pieces:
            piece(i).wait()
        return carry

    lax.fori_loop(0, 2, go, 0)


def encode_kernel(heads, head_dim, here_ref, cell_ref, frames_any, enc_in_any, bias_any, enc_out_any, pos_any, gain_any,
                  w_keys_any, w_step_any, step_bias_any, code_any, skip_any, out_gain_any, w_pair_any,
                  encoded, normed, keys, b_t, grow, fall, skip, out_gain, xs_o1, s_o1, w_o1, w_m1, w_o2, w_m2,
                  frames, enc_in, bias, enc_out, pos, norm_gain, w_keys, w_step, step_bias, code, sem, wsem):
    half = 1 - here_ref[0] % 2
    cell = cell_ref[0]
    base = pl.multiple_of((cell // EXTRA) * EXTRA, EXTRA)
    small = [pltpu.make_async_copy(src, dst, sem.at[i]) for i, (src, dst) in enumerate((
        (bias_any, bias), (pos_any.at[pl.ds(base, EXTRA), :], pos), (gain_any, norm_gain), (step_bias_any, step_bias),
        (code_any, code), (skip_any, skip), (out_gain_any, out_gain)))]
    first = [in_pieces(src, dst, wsem, i) for i, (src, dst) in enumerate((
        (frames_any, frames), (enc_in_any, enc_in), (enc_out_any, enc_out), (w_keys_any, w_keys), (w_step_any, w_step)))]
    big = [in_pieces(group_columns(w_pair_any, dst, which, group), dst, wsem, 5 + i) for i, (which, group, dst) in enumerate((
        (half, 0, w_o1), (1 - half, 0, w_m1), (half, 1, w_o2), (1 - half, 1, w_m2)))]
    start_pieces(first[:2])
    for c in small:
        c.start()
    start_pieces(first[2:])
    rows, depth = encoded.shape
    block = rows // 2
    lower = (iota((rows, rows), 0) >= iota((rows, rows), 1)).astype(F32).astype(BF)
    small[0].wait()
    wait_pieces(first[:2])
    start_pieces(big)
    twice = lambda v: jnp.concatenate([v, v], axis=1)
    columns = [slice(j, j + CHUNK) for j in range(0, depth, CHUNK)]

    def hide(part):
        pieces = []
        for cols in columns:
            h = dot(frames[part, :], enc_in[:, cols]) + bias[:, cols]
            pieces.append(jax.nn.gelu(h, approximate=True).astype(BF))
        return jnp.concatenate(pieces, axis=1)

    def encode(part, hidden, row):
        square = jnp.zeros((block, 1), F32)
        for cols in columns:
            e = (dot(hidden, enc_out[:, cols]) + row[:, cols]).astype(BF)
            encoded[part, cols] = e
            e = e.astype(F32)
            square += jnp.sum(e * e, axis=1, keepdims=True)
        inv = lax.rsqrt(square / depth + 1e-05)
        pieces = []
        for cols in columns:
            piece = (encoded[part, cols].astype(F32) * inv * norm_gain[:, cols]).astype(BF)
            normed[part, cols] = piece
            pieces.append(piece)
        return jnp.concatenate(pieces, axis=1)

    def read_out(part, wide):
        k = dot(wide, w_keys[...]).astype(BF)
        keys[part, :] = k
        b_t[:, part] = k[:, :k.shape[1] // 2].T
        ws = w_step[...]
        raw = dot_t(wide, jnp.concatenate([ws, ws], axis=0)) + twice(step_bias[...])
        return jax.nn.sigmoid(raw).astype(BF)

    top, low = slice(0, block), slice(block, rows)
    hidden_top = hide(top)
    hidden_low = hide(low)
    for c in small[1:]:
        c.wait()
    wait_pieces(first[2:])
    row = jnp.sum(jnp.where(iota(pos.shape, 0) == cell - base, pos[...].astype(F32), 0.0), axis=0, keepdims=True)
    wide_top = encode(top, hidden_top, row)
    wide_low = encode(low, hidden_low, row)
    step = jnp.concatenate([read_out(top, wide_top), read_out(low, wide_low)], axis=0)
    cum = dot(lower, step) * twice(-0.0005 - 0.003 * code[...].astype(F32))
    g = split_two(jnp.exp(-cum), heads)
    f = split_two(jnp.exp(cum), heads)
    grow[...] = g
    fall[...] = f
    wait_pieces(big[:1])
    project(half * (heads // 2), w_o1, xs_o1, s_o1, heads, head_dim, normed, b_t[...], g, f[rows - EXTRA:])
    wait_pieces(big[1:])


def group_columns(w_any, like, half, group):
    size = like.shape[1]
    return w_any.at[:, pl.ds(pl.multiple_of((half * 2 + group) * size, size), size)]


def project_kernel(heads, head_dim, own, group, here_ref, normed, b_t, grow, fall, w, xs_ref, s_ref):
    half = (here_ref[0] + 1 - own) % 2
    rows = normed.shape[0]
    first = (half * 2 + group) * (xs_ref.shape[1] // head_dim)
    project(first, w, xs_ref, s_ref, heads, head_dim, normed, b_t[...], grow[...], fall[rows - EXTRA:])


def state_of(ref, width):
    return ref[:width, :].astype(F32)


def decays_of(ref):
    tail = ref[ref.shape[0] - EXTRA:, :].astype(F32)
    return tail[0:1] + tail[1:2], tail[2:3] + tail[3:4]


def put(ref, width, state, decays):
    ref[:width, :] = state.astype(BF)
    if ref.shape[0] > width:
        ref[width:, :] = decay_rows(decays)


def times(one, other):
    return one[0] * other[0], one[1] * other[1]


def total_kernel(group, width, here_ref, mine_ref, got_ref, mine_first, got_first, total_ref):
    mine, got = state_of(mine_ref, width), state_of(got_ref, width)
    mine_decays, got_decays = decays_of(mine_first), decays_of(got_first)
    both = times(mine_decays, got_decays)

    @pl.when(here_ref[0] % 2 == 1)
    def _():
        put(total_ref, width, mine_decays[group] * got + mine, both)

    @pl.when(here_ref[0] % 2 == 0)
    def _():
        put(total_ref, width, got_decays[group] * mine + got, both)


def step_kernel(group, width, reach, here_ref, total_ref, got_ref, total_first, got_first, *refs):
    begin = len(refs) == 2
    new_before_ref, new_total_ref = refs[-2:]
    later = (here_ref[0] // reach) % 2 == 1
    got, total = state_of(got_ref, width), state_of(total_ref, width)
    got_decays, total_decays = decays_of(got_first), decays_of(total_first)
    both = times(total_decays, got_decays)

    @pl.when(later)
    def _():
        if begin:
            put(new_before_ref, width, got, got_decays)
        else:
            before_decays = decays_of(refs[1])
            put(new_before_ref, width, state_of(refs[0], width) + before_decays[group] * got,
                times(before_decays, got_decays))
        put(new_total_ref, width, total_decays[group] * got + total, both)

    @pl.when(jnp.logical_not(later))
    def _():
        if begin:
            one = jnp.ones_like(got_decays[0])
            put(new_before_ref, width, jnp.zeros_like(got), (one, one))
        else:
            put(new_before_ref, width, state_of(refs[0], width), decays_of(refs[1]))
        put(new_total_ref, width, got_decays[group] * total + got, both)


def last_kernel(group, reach, here_ref, got_ref, before_ref, before_first, mine_ref, theirs_ref, mine_first, theirs_first,
                keep_ref, send_ref):
    width = keep_ref.shape[0]
    later = (here_ref[0] // reach) % 2 == 1
    before_decay = jnp.where(later, decays_of(before_first)[group], 0.0)
    before = state_of(before_ref, width) + before_decay * state_of(got_ref, width)

    @pl.when(here_ref[0] % 2 == 1)
    def _():
        keep_ref[...] = (decays_of(theirs_first)[group] * before + state_of(theirs_ref, width)).astype(BF)
        send_ref[...] = before.astype(BF)

    @pl.when(here_ref[0] % 2 == 0)
    def _():
        send_ref[...] = (decays_of(mine_first)[group] * before + state_of(mine_ref, width)).astype(BF)
        keep_ref[...] = before.astype(BF)


def inner_kernel(heads, head_dim, own, group, fresh, here_ref, normed, keys, fall, skip, w_out_any, w, xs, *refs):
    half = (here_ref[0] + 1 - own) % 2
    rows = keys.shape[0]
    width = keys.shape[1] // 2
    size = xs.shape[1]
    if fresh:
        u, v, w_rows, scores_ref, sem = refs
    else:
        scores_ref, u, v, w_rows, sem = refs
    start = pl.multiple_of((half * 2 + group) * size, size)
    copies = [in_pieces(w_out_any.at[pl.ds(start, size), :], w_rows, sem, 0)]
    start_pieces(copies)
    if fresh:
        scores = dot_t(keys[:, width:], keys[:, :width])
        scores_ref[...] = jnp.where(iota((rows, rows), 0) >= iota((rows, rows), 1), scores, 0.0).astype(BF)
    scores = scores_ref[...]
    mid = rows // 2
    both = jnp.broadcast_to(jnp.concatenate([skip[...], skip[...]], axis=1), (EXTRA, 2 * heads))
    skip_two = split_two(both, heads)
    first = (half * 2 + group) * (size // head_dim)
    for j in range(size // CHUNK):
        cols = slice(j * CHUNK, (j + 1) * CHUNK)
        z = dot(normed[...], compact(w, j, 1)).astype(BF).astype(F32)
        gate = z * jax.nn.sigmoid(z)
        spread = spread_heads(first + j * (CHUNK // head_dim), heads, head_dim)
        gain = dot(skip_two, spread)[0:1]
        grown = dot(fall[...], spread)
        grown = grown * gate
        u[:, cols] = grown.astype(BF)
        top = dot(scores[:mid, :mid], xs[:mid, cols])
        low = dot(scores[mid:], xs[:, cols])
        for part, inner in ((slice(0, mid), top), (slice(mid, rows), low)):
            v[part, cols] = (grown[part] * (inner + gain * xs[part, cols].astype(F32))).astype(BF)
    wait_pieces(copies)


def mix_kernel(head_dim, places, last, here_ref, keys, base, gain, *refs):
    many = len(places)
    states, us, vs, ws = (refs[i * many:(i + 1) * many] for i in range(4))
    out = refs[4 * many]
    width = keys.shape[1] // 2
    size = us[0].shape[1]
    starts = [((here_ref[0] + 1 - own) % 2 * 2 + group) * size for own, group in places]
    same = (iota((CHUNK, CHUNK), 0) // head_dim) == (iota((CHUNK, CHUNK), 1) // head_dim)
    mean = jnp.where(same, 1.0 / head_dim, 0.0).astype(BF)
    work = []
    for state, u, v in zip(states, us, vs):
        for j in range(size // CHUNK):
            cols = slice(j * CHUNK, (j + 1) * CHUNK)
            carried = dot(keys[:, width:], state[:, cols])
            g = v[:, cols].astype(F32) + u[:, cols].astype(F32) * carried
            work.append((g, dot((g * g).astype(BF), mean)))
    steps = base.shape[1] // CHUNK
    totals = [base[:, n * CHUNK:(n + 1) * CHUNK].astype(F32) for n in range(steps)]
    for i in range(many):
        parts = []
        for j in range(size // CHUNK):
            g, m = work[i * (size // CHUNK) + j]
            row = gain[:, pl.ds(pl.multiple_of(starts[i] + j * CHUNK, CHUNK), CHUNK)]
            parts.append((g * lax.rsqrt(m + 1e-05) * row).astype(BF))
        mixed = jnp.concatenate(parts, axis=1)
        totals = [totals[n] + dot(mixed, ws[i][:, n * CHUNK:(n + 1) * CHUNK]) for n in range(steps)]
    copies = []
    for n, total in enumerate(totals):
        cols = slice(n * CHUNK, (n + 1) * CHUNK)
        if last:
            buf, sem = refs[4 * many + 1:]
            buf[:, cols] = total.astype(buf.dtype)
            copies.append(pltpu.make_async_copy(buf.at[:, cols], out.at[:, cols], sem.at[n]))
            copies[-1].start()
        else:
            out[:, cols] = total.astype(out.dtype)
    for c in copies:
        c.wait()


def body(frames, patch_cell, enc_in, enc_bias, enc_out, pos_table, norm_gain, w_pair, w_keys, w_step,
         step_bias, decay_code, skip_gain, out_gain, w_out):
    rows = frames.shape[0]
    pix = frames.shape[2]
    depth = enc_out.shape[1]
    heads = w_step.shape[1]
    head_dim = w_pair.shape[1] // (2 * heads)
    width = w_keys.shape[1] // 2
    size = heads * head_dim // 4
    peers = lax.axis_size("tm")
    here = lax.axis_index("tm").astype(jnp.int32).reshape(1)
    row = lambda v: v.reshape(1, -1)
    far = lambda v: pltpu.with_memory_space_constraint(v, pltpu.HBM)
    near = lambda shape, dtype=BF: pltpu.VMEM(shape, dtype)
    sems = lambda n: pltpu.SemaphoreType.DMA((n,))
    pair = lambda by: [(i, i ^ by) for i in range(peers)]
    after = lambda value, *first: lax.optimization_barrier((value,) + first)[0]

    def call(kernel, name, outs, ins, scratch=(), flops=0, out_spec=VM):
        specs = [spec for spec, _ in ins]
        cost = pl.CostEstimate(flops=flops, bytes_accessed=2**20, transcendentals=0)
        return pl.pallas_call(kernel, out_shape=tuple(outs), in_specs=specs, out_specs=(out_spec,) * len(outs),
                              scratch_shapes=list(scratch), compiler_params=params(24), name=name,
                              cost_estimate=cost)(*[v for _, v in ins])

    vm = lambda *vs: [(VM, v) for v in vs]
    hbm = lambda *vs: [(pl.BlockSpec(memory_space=pltpu.HBM), far(v)) for v in vs]
    where = [(SM, here)]

    part, message, weight = near((rows, size)), near((width + EXTRA, size)), near((depth, 2 * size))
    kinds = (message, near((width, size)))
    encoded, normed, keys, b_t, grow, fall, skip, gain, xs_o1, s_o1, w_o1, w_m1, w_o2, w_m2 = call(
        functools.partial(encode_kernel, heads, head_dim), "encode",
        (near((rows, depth)), near((rows, depth)), near((rows, 2 * width)), near((width, rows)),
         near((rows, 2 * heads)), near((rows, 2 * heads)), near((1, heads), F32), near((1, heads * head_dim), F32),
         part, message) + (weight,) * 4,
        where + [(SM, patch_cell)] + hbm(frames.reshape(rows, pix), enc_in, row(enc_bias), enc_out, pos_table, row(norm_gain),
                                         w_keys, w_step.T, row(step_bias), row(decay_code), row(skip_gain), row(out_gain),
                                         w_pair),
        [near((rows, pix)), near((pix, depth)), near((1, depth), F32), near((depth, depth)), near((EXTRA, depth)),
         near((1, depth), F32), near((depth, 2 * width)), near((heads, depth)), near((1, heads), F32),
         near((1, heads), jnp.int32), sems(7), pltpu.SemaphoreType.DMA((9, 2))],
        rows * depth * depth)

    long, short = 8 * rows * depth * size, rows * depth * size // 4

    def projected(own, group, w):
        return call(functools.partial(project_kernel, heads, head_dim, own, group), "project",
                    (part, kinds[group]), where + vm(normed, b_t, grow, fall, w), (), long)

    scores = []

    def inner(own, group, w, xs, flops):
        outs = call(functools.partial(inner_kernel, heads, head_dim, own, group, not scores), "inner",
                    (part, part, near((size, depth))) + (() if scores else (near((rows, rows)),)),
                    where + vm(normed, keys, fall, skip) + hbm(w_out) + vm(w, xs, *scores),
                    [pltpu.SemaphoreType.DMA((1, 2))], flops)
        scores.extend(outs[3:])
        return outs[:3]

    def mixed(places, base, last, *groups):
        states, us, vs, ws = zip(*groups)
        shape = sds((rows, depth), BF) if last else near((rows, depth), F32)
        return call(functools.partial(mix_kernel, head_dim, places, last), "mix", (shape,),
                    where + vm(keys, base, gain, *states, *us, *vs, *ws),
                    [near((rows, depth)), sems(depth // CHUNK)] if last else [], short,
                    ANY if last else VM)[0]

    totals, befores, arriving, firsts = [None, None], [None, None], [None, None], {}
    done = {}

    def work(own, group, w, xs, stamp, flops):
        done[own, group] = inner(own, group, w, after(xs, stamp), flops)
        return done[own, group][0]

    def start_total(i, mine, theirs):
        totals[i], = call(functools.partial(total_kernel, i, width), "total", (kinds[i],),
                          where + vm(mine, theirs, s_m1, got_1))
        arriving[i] = lax.ppermute(totals[i], "tm", pair(2))

    def advance(i, reach, arrived):
        if i == 0:
            firsts[reach] = totals[0], arrived, befores[0]
        own, theirs, before = firsts[reach]
        carried = [] if reach == 2 else [befores[i], before]
        final = reach * 4 >= peers
        befores[i], totals[i] = call(
            functools.partial(step_kernel, i, width, reach), "step", (kinds[i], kinds[1] if final else kinds[i]),
            where + vm(totals[i], arrived, own, theirs, *carried))
        arriving[i] = lax.ppermute(totals[i], "tm", pair(2 * reach))

    def finish(i, arrived, mine, theirs):
        keep, send = call(functools.partial(last_kernel, i, peers // 2), "last", (kinds[1],) * 2,
                          where + vm(arrived, befores[i], befores[0], mine, theirs, s_m1, got_1))
        return keep, lax.ppermute(send, "tm", pair(1))

    got_1 = lax.ppermute(s_o1, "tm", pair(1))
    xs_m1, s_m1 = projected(1, 0, w_m1)
    start_total(0, s_m1, got_1)
    xs_o2, s_o2 = projected(0, 1, after(w_o2, totals[0]))
    got_2 = lax.ppermute(s_o2, "tm", pair(1))
    xs_m2, s_m2 = projected(1, 1, after(w_m2, s_o2))
    start_total(1, s_m2, got_2)
    stamp = work(0, 0, w_o1, xs_o1, totals[1], long)
    advance(0, 2, after(arriving[0], stamp))
    stamp = work(1, 0, w_m1, xs_m1, befores[0], short)
    stamp = work(1, 1, w_m2, xs_m2, stamp, short)
    advance(1, 2, after(arriving[1], stamp))
    reach = 4
    while reach * 2 < peers:
        for i in range(2):
            advance(i, reach, arriving[i])
        reach *= 2
    keep_1, sent_1 = finish(0, after(arriving[0], befores[1]), s_m1, got_1)
    stamp = work(0, 1, w_o2, xs_o2, keep_1, short)
    mixing = mixed(((1, 0),), after(encoded, stamp), False, (keep_1, *done[1, 0]))
    keep_2, sent_2 = finish(1, after(arriving[1], mixing), s_m2, got_2)
    mixing = mixed(((0, 0), (1, 1)), after(mixing, keep_2), False, (sent_1, *done[0, 0]), (keep_2, *done[1, 1]))
    return mixed(((0, 1),), mixing, True, (sent_2, *done[0, 1])).reshape(rows, 1, depth)


def solution(mesh):
    placed = (P("tm", "space", None), P("space")) + (P(),) * 13
    return jax.shard_map(body, mesh=mesh, in_specs=placed, out_specs=P("tm", "space", None), check_vma=False)
```

```python
import functools

import jax
import jax.numpy as jnp
from jax import lax
from jax.experimental import pallas as pl
from jax.experimental.pallas import tpu as pltpu
from jax.sharding import PartitionSpec as P

BF = jnp.bfloat16
F32 = jnp.float32
VM = pl.BlockSpec(memory_space=pltpu.VMEM)
SM = pl.BlockSpec(memory_space=pltpu.SMEM)
ANY = pl.BlockSpec(memory_space=pl.ANY)
LANES = 128
CHUNK = 256
EXTRA = 16


def dot(a, b):
    return jnp.dot(a, b, preferred_element_type=F32)


def dot_t(a, b):
    return lax.dot_general(a, b, (((1,), (1,)), ((), ())), preferred_element_type=F32)


def iota(shape, axis):
    return lax.broadcasted_iota(jnp.int32, shape, axis)


def params(mib):
    return pltpu.CompilerParams(vmem_limit_bytes=mib * 2**20)


def sds(shape, dtype):
    return jax.ShapeDtypeStruct(shape, dtype)


def spread_heads(first_head, heads, head_dim):
    row = iota((2 * heads, CHUNK), 0)
    lane = iota((2 * heads, CHUNK), 1)
    row = jnp.where(row < heads, row, row - heads)
    return (row == first_head + lane // head_dim).astype(F32).astype(BF)


def split_two(value, heads):
    high = value.astype(BF).astype(F32)
    return jnp.where(iota(value.shape, 1) < heads, high, value - high).astype(BF)


def pick_half(tile_a, tile_b, part):
    half = LANES // 2
    low = iota(tile_a.shape, 1) < half
    if part == 0:
        return jnp.where(low, tile_a, pltpu.roll(tile_b, half, 1))
    return jnp.where(low, pltpu.roll(tile_a, half, 1), tile_b)


def compact(ref, j, part):
    start = j * 2 * CHUNK
    tiles = [ref[:, start + i:start + i + LANES] for i in range(0, 2 * CHUNK, LANES)]
    pairs = [pick_half(tiles[i], tiles[i + 1], part) for i in range(0, len(tiles), 2)]
    return jnp.concatenate(pairs, axis=1)


def project(first, w, xs_ref, s_ref, heads, head_dim, normed, b_t, grow, fall_end):
    width = b_t.shape[0]
    later = []
    for j in range(xs_ref.shape[1] // CHUNK):
        cols = slice(j * CHUNK, (j + 1) * CHUNK)
        spread = spread_heads(first + j * (CHUNK // head_dim), heads, head_dim)
        x = dot(normed[...], compact(w, j, 0)).astype(BF)
        scaled = (x.astype(F32) * dot(grow, spread)).astype(BF)
        xs_ref[:, cols] = scaled
        decay = dot(fall_end, spread)[EXTRA - 1:EXTRA]
        if s_ref.shape[0] > width:
            next_first = first + (xs_ref.shape[1] + j * CHUNK) // head_dim
            next_decay = dot(fall_end, spread_heads(next_first, heads, head_dim))[EXTRA - 1:EXTRA]
            s_ref[width:width + EXTRA, cols] = decay_rows((decay, next_decay))
        later.append((cols, scaled, decay))
    for cols, scaled, decay in later:
        s_ref[0:width, cols] = (dot(b_t, scaled) * decay).astype(BF)


def decay_rows(values):
    row = iota((EXTRA, values[0].shape[1]), 0)
    out = jnp.zeros(row.shape, F32)
    for k, value in enumerate(values):
        high = value.astype(BF).astype(F32)
        out = jnp.where(row == 2 * k, high, jnp.where(row == 2 * k + 1, value - high, out))
    return out.astype(BF)


def in_pieces(src, dst, sem, slot):
    block = dst.shape[0] // 2

    def piece(i):
        part = pl.ds(pl.multiple_of(i * block, block), block)
        return pltpu.make_async_copy(src.at[part, :], dst.at[part, :], sem.at[slot, i])

    return piece


def start_pieces(pieces):
    def go(i, carry):
        for piece in pieces:
            piece(i).start()
        return carry

    lax.fori_loop(0, 2, go, 0)


def wait_pieces(pieces):
    def go(i, carry):
        for piece in pieces:
            piece(i).wait()
        return carry

    lax.fori_loop(0, 2, go, 0)


def encode_kernel(heads, head_dim, here_ref, cell_ref, frames_any, enc_in_any, bias_any, enc_out_any, pos_any, gain_any,
                  w_keys_any, w_step_any, step_bias_any, code_any, skip_any, out_gain_any, w_pair_any,
                  encoded, normed, keys, b_t, grow, fall, skip, out_gain, xs_o1, s_o1, w_o1, w_m1, w_o2, w_m2,
                  frames, enc_in, bias, enc_out, pos, norm_gain, w_keys, w_step, step_bias, code, sem, wsem):
    half = 1 - here_ref[0] % 2
    cell = cell_ref[0]
    base = pl.multiple_of((cell // EXTRA) * EXTRA, EXTRA)
    small = [pltpu.make_async_copy(src, dst, sem.at[i]) for i, (src, dst) in enumerate((
        (bias_any, bias), (pos_any.at[pl.ds(base, EXTRA), :], pos), (gain_any, norm_gain), (step_bias_any, step_bias),
        (code_any, code), (skip_any, skip), (out_gain_any, out_gain)))]
    first = [in_pieces(src, dst, wsem, i) for i, (src, dst) in enumerate((
        (frames_any, frames), (enc_in_any, enc_in), (enc_out_any, enc_out), (w_keys_any, w_keys), (w_step_any, w_step)))]
    big = [in_pieces(group_columns(w_pair_any, dst, which, group), dst, wsem, 5 + i) for i, (which, group, dst) in enumerate((
        (half, 0, w_o1), (1 - half, 0, w_m1), (half, 1, w_o2), (1 - half, 1, w_m2)))]
    start_pieces(first[:2])
    for c in small:
        c.start()
    start_pieces(first[2:])
    rows, depth = encoded.shape
    block = rows // 2
    lower = (iota((rows, rows), 0) >= iota((rows, rows), 1)).astype(F32).astype(BF)
    small[0].wait()
    wait_pieces(first[:2])
    start_pieces(big)
    twice = lambda v: jnp.concatenate([v, v], axis=1)
    columns = [slice(j, j + CHUNK) for j in range(0, depth, CHUNK)]

    def hide(part):
        pieces = []
        for cols in columns:
            h = dot(frames[part, :], enc_in[:, cols]) + bias[:, cols]
            pieces.append(jax.nn.gelu(h, approximate=True).astype(BF))
        return jnp.concatenate(pieces, axis=1)

    def encode(part, hidden, row):
        square = jnp.zeros((block, 1), F32)
        for cols in columns:
            e = (dot(hidden, enc_out[:, cols]) + row[:, cols]).astype(BF)
            encoded[part, cols] = e
            e = e.astype(F32)
            square += jnp.sum(e * e, axis=1, keepdims=True)
        inv = lax.rsqrt(square / depth + 1e-05)
        pieces = []
        for cols in columns:
            piece = (encoded[part, cols].astype(F32) * inv * norm_gain[:, cols]).astype(BF)
            normed[part, cols] = piece
            pieces.append(piece)
        return jnp.concatenate(pieces, axis=1)

    def read_out(part, wide):
        k = dot(wide, w_keys[...]).astype(BF)
        keys[part, :] = k
        b_t[:, part] = k[:, :k.shape[1] // 2].T
        ws = w_step[...]
        raw = dot_t(wide, jnp.concatenate([ws, ws], axis=0)) + twice(step_bias[...])
        return jax.nn.sigmoid(raw).astype(BF)

    top, low = slice(0, block), slice(block, rows)
    hidden_top = hide(top)
    hidden_low = hide(low)
    for c in small[1:]:
        c.wait()
    wait_pieces(first[2:])
    row = jnp.sum(jnp.where(iota(pos.shape, 0) == cell - base, pos[...].astype(F32), 0.0), axis=0, keepdims=True)
    wide_top = encode(top, hidden_top, row)
    wide_low = encode(low, hidden_low, row)
    step = jnp.concatenate([read_out(top, wide_top), read_out(low, wide_low)], axis=0)
    cum = dot(lower, step) * twice(-0.0005 - 0.003 * code[...].astype(F32))
    g = split_two(jnp.exp(-cum), heads)
    f = split_two(jnp.exp(cum), heads)
    grow[...] = g
    fall[...] = f
    wait_pieces(big[:1])
    project(half * (heads // 2), w_o1, xs_o1, s_o1, heads, head_dim, normed, b_t[...], g, f[rows - EXTRA:])
    wait_pieces(big[1:])


def group_columns(w_any, like, half, group):
    size = like.shape[1]
    return w_any.at[:, pl.ds(pl.multiple_of((half * 2 + group) * size, size), size)]


def project_kernel(heads, head_dim, own, group, here_ref, normed, b_t, grow, fall, w, *refs):
    half = (here_ref[0] + 1 - own) % 2
    rows = normed.shape[0]
    if len(refs) == 2:
        xs_ref, s_ref = refs
    else:
        keys, xs_ref, s_ref, scores_ref = refs
        width = keys.shape[1] // 2
        scores = dot_t(keys[:, width:], keys[:, :width])
        scores_ref[...] = jnp.where(iota((rows, rows), 0) >= iota((rows, rows), 1), scores, 0.0).astype(BF)
    first = (half * 2 + group) * (xs_ref.shape[1] // head_dim)
    project(first, w, xs_ref, s_ref, heads, head_dim, normed, b_t[...], grow[...], fall[rows - EXTRA:])


def state_of(ref, width):
    return ref[:width, :].astype(F32)


def decays_of(ref):
    tail = ref[ref.shape[0] - EXTRA:, :].astype(F32)
    return tail[0:1] + tail[1:2], tail[2:3] + tail[3:4]


def put(ref, width, state, decays):
    ref[:width, :] = state.astype(BF)
    if ref.shape[0] > width:
        ref[width:, :] = decay_rows(decays)


def times(one, other):
    return one[0] * other[0], one[1] * other[1]


def total_kernel(group, width, here_ref, mine_ref, got_ref, mine_first, got_first, total_ref):
    mine, got = state_of(mine_ref, width), state_of(got_ref, width)
    mine_decays, got_decays = decays_of(mine_first), decays_of(got_first)
    both = times(mine_decays, got_decays)

    @pl.when(here_ref[0] % 2 == 1)
    def _():
        put(total_ref, width, mine_decays[group] * got + mine, both)

    @pl.when(here_ref[0] % 2 == 0)
    def _():
        put(total_ref, width, got_decays[group] * mine + got, both)


def step_kernel(group, width, reach, here_ref, total_ref, got_ref, total_first, got_first, *refs):
    begin = len(refs) == 2
    new_before_ref, new_total_ref = refs[-2:]
    later = (here_ref[0] // reach) % 2 == 1
    got, total = state_of(got_ref, width), state_of(total_ref, width)
    got_decays, total_decays = decays_of(got_first), decays_of(total_first)
    both = times(total_decays, got_decays)

    @pl.when(later)
    def _():
        if begin:
            put(new_before_ref, width, got, got_decays)
        else:
            before_decays = decays_of(refs[1])
            put(new_before_ref, width, state_of(refs[0], width) + before_decays[group] * got,
                times(before_decays, got_decays))
        put(new_total_ref, width, total_decays[group] * got + total, both)

    @pl.when(jnp.logical_not(later))
    def _():
        if begin:
            one = jnp.ones_like(got_decays[0])
            put(new_before_ref, width, jnp.zeros_like(got), (one, one))
        else:
            put(new_before_ref, width, state_of(refs[0], width), decays_of(refs[1]))
        put(new_total_ref, width, got_decays[group] * total + got, both)


def last_kernel(group, reach, here_ref, got_ref, before_ref, before_first, mine_ref, theirs_ref, mine_first, theirs_first,
                keep_ref, send_ref):
    width = keep_ref.shape[0]
    later = (here_ref[0] // reach) % 2 == 1
    before_decay = jnp.where(later, decays_of(before_first)[group], 0.0)
    before = state_of(before_ref, width) + before_decay * state_of(got_ref, width)

    @pl.when(here_ref[0] % 2 == 1)
    def _():
        keep_ref[...] = (decays_of(theirs_first)[group] * before + state_of(theirs_ref, width)).astype(BF)
        send_ref[...] = before.astype(BF)

    @pl.when(here_ref[0] % 2 == 0)
    def _():
        send_ref[...] = (decays_of(mine_first)[group] * before + state_of(mine_ref, width)).astype(BF)
        keep_ref[...] = before.astype(BF)


def inner_kernel(heads, head_dim, own, group, fresh, here_ref, normed, keys, fall, skip, w_out_any, w, xs, *refs):
    half = (here_ref[0] + 1 - own) % 2
    rows = keys.shape[0]
    width = keys.shape[1] // 2
    size = xs.shape[1]
    if fresh:
        u, v, w_rows, scores_ref, sem = refs
    else:
        scores_ref, u, v, w_rows, sem = refs
    start = pl.multiple_of((half * 2 + group) * size, size)
    copies = [in_pieces(w_out_any.at[pl.ds(start, size), :], w_rows, sem, 0)]
    start_pieces(copies)
    if fresh:
        scores = dot_t(keys[:, width:], keys[:, :width])
        scores_ref[...] = jnp.where(iota((rows, rows), 0) >= iota((rows, rows), 1), scores, 0.0).astype(BF)
    scores = scores_ref[...]
    mid = rows // 2
    both = jnp.broadcast_to(jnp.concatenate([skip[...], skip[...]], axis=1), (EXTRA, 2 * heads))
    skip_two = split_two(both, heads)
    first = (half * 2 + group) * (size // head_dim)
    for j in range(size // CHUNK):
        cols = slice(j * CHUNK, (j + 1) * CHUNK)
        z = dot(normed[...], compact(w, j, 1)).astype(BF).astype(F32)
        gate = z * jax.nn.sigmoid(z)
        spread = spread_heads(first + j * (CHUNK // head_dim), heads, head_dim)
        gain = dot(skip_two, spread)[0:1]
        grown = dot(fall[...], spread)
        grown = grown * gate
        u[:, cols] = grown.astype(BF)
        top = dot(scores[:mid, :mid], xs[:mid, cols])
        low = dot(scores[mid:], xs[:, cols])
        for part, inner in ((slice(0, mid), top), (slice(mid, rows), low)):
            v[part, cols] = (grown[part] * (inner + gain * xs[part, cols].astype(F32))).astype(BF)
    wait_pieces(copies)


def mix_kernel(head_dim, places, last, here_ref, keys, base, gain, *refs):
    many = len(places)
    states, us, vs, ws = (refs[i * many:(i + 1) * many] for i in range(4))
    out = refs[4 * many]
    width = keys.shape[1] // 2
    size = us[0].shape[1]
    starts = [((here_ref[0] + 1 - own) % 2 * 2 + group) * size for own, group in places]
    same = (iota((CHUNK, CHUNK), 0) // head_dim) == (iota((CHUNK, CHUNK), 1) // head_dim)
    mean = jnp.where(same, 1.0 / head_dim, 0.0).astype(BF)
    work = []
    for state, u, v in zip(states, us, vs):
        for j in range(size // CHUNK):
            cols = slice(j * CHUNK, (j + 1) * CHUNK)
            carried = dot(keys[:, width:], state[:, cols])
            g = v[:, cols].astype(F32) + u[:, cols].astype(F32) * carried
            work.append((g, dot((g * g).astype(BF), mean)))
    steps = base.shape[1] // CHUNK
    totals = [base[:, n * CHUNK:(n + 1) * CHUNK].astype(F32) for n in range(steps)]
    for i in range(many):
        parts = []
        for j in range(size // CHUNK):
            g, m = work[i * (size // CHUNK) + j]
            row = gain[:, pl.ds(pl.multiple_of(starts[i] + j * CHUNK, CHUNK), CHUNK)]
            parts.append((g * lax.rsqrt(m + 1e-05) * row).astype(BF))
        mixed = jnp.concatenate(parts, axis=1)
        totals = [totals[n] + dot(mixed, ws[i][:, n * CHUNK:(n + 1) * CHUNK]) for n in range(steps)]
    copies = []
    for n, total in enumerate(totals):
        cols = slice(n * CHUNK, (n + 1) * CHUNK)
        if last:
            buf, sem = refs[4 * many + 1:]
            buf[:, cols] = total.astype(buf.dtype)
            copies.append(pltpu.make_async_copy(buf.at[:, cols], out.at[:, cols], sem.at[n]))
            copies[-1].start()
        else:
            out[:, cols] = total.astype(out.dtype)
    for c in copies:
        c.wait()


def body(frames, patch_cell, enc_in, enc_bias, enc_out, pos_table, norm_gain, w_pair, w_keys, w_step,
         step_bias, decay_code, skip_gain, out_gain, w_out):
    rows = frames.shape[0]
    pix = frames.shape[2]
    depth = enc_out.shape[1]
    heads = w_step.shape[1]
    head_dim = w_pair.shape[1] // (2 * heads)
    width = w_keys.shape[1] // 2
    size = heads * head_dim // 4
    peers = lax.axis_size("tm")
    here = lax.axis_index("tm").astype(jnp.int32).reshape(1)
    row = lambda v: v.reshape(1, -1)
    far = lambda v: pltpu.with_memory_space_constraint(v, pltpu.HBM)
    near = lambda shape, dtype=BF: pltpu.VMEM(shape, dtype)
    sems = lambda n: pltpu.SemaphoreType.DMA((n,))
    pair = lambda by: [(i, i ^ by) for i in range(peers)]
    after = lambda value, *first: lax.optimization_barrier((value,) + first)[0]

    def call(kernel, name, outs, ins, scratch=(), flops=0, out_spec=VM):
        specs = [spec for spec, _ in ins]
        cost = pl.CostEstimate(flops=flops, bytes_accessed=2**20, transcendentals=0)
        return pl.pallas_call(kernel, out_shape=tuple(outs), in_specs=specs, out_specs=(out_spec,) * len(outs),
                              scratch_shapes=list(scratch), compiler_params=params(24), name=name,
                              cost_estimate=cost)(*[v for _, v in ins])

    vm = lambda *vs: [(VM, v) for v in vs]
    hbm = lambda *vs: [(pl.BlockSpec(memory_space=pltpu.HBM), far(v)) for v in vs]
    where = [(SM, here)]

    part, message, weight = near((rows, size)), near((width + EXTRA, size)), near((depth, 2 * size))
    kinds = (message, near((width, size)))
    encoded, normed, keys, b_t, grow, fall, skip, gain, xs_o1, s_o1, w_o1, w_m1, w_o2, w_m2 = call(
        functools.partial(encode_kernel, heads, head_dim), "encode",
        (near((rows, depth)), near((rows, depth)), near((rows, 2 * width)), near((width, rows)),
         near((rows, 2 * heads)), near((rows, 2 * heads)), near((1, heads), F32), near((1, heads * head_dim), F32),
         part, message) + (weight,) * 4,
        where + [(SM, patch_cell)] + hbm(frames.reshape(rows, pix), enc_in, row(enc_bias), enc_out, pos_table, row(norm_gain),
                                         w_keys, w_step.T, row(step_bias), row(decay_code), row(skip_gain), row(out_gain),
                                         w_pair),
        [near((rows, pix)), near((pix, depth)), near((1, depth), F32), near((depth, depth)), near((EXTRA, depth)),
         near((1, depth), F32), near((depth, 2 * width)), near((heads, depth)), near((1, heads), F32),
         near((1, heads), jnp.int32), sems(7), pltpu.SemaphoreType.DMA((9, 2))],
        rows * depth * depth)

    long, short = 8 * rows * depth * size, rows * depth * size // 4

    def projected(own, group, w, *keys):
        return call(functools.partial(project_kernel, heads, head_dim, own, group), "project",
                    (part, kinds[group]) + (near((rows, rows)),) * len(keys),
                    where + vm(normed, b_t, grow, fall, w, *keys), (), long)

    scores = []

    def inner(own, group, w, xs, flops):
        outs = call(functools.partial(inner_kernel, heads, head_dim, own, group, not scores), "inner",
                    (part, part, near((size, depth))) + (() if scores else (near((rows, rows)),)),
                    where + vm(normed, keys, fall, skip) + hbm(w_out) + vm(w, xs, *scores),
                    [pltpu.SemaphoreType.DMA((1, 2))], flops)
        scores.extend(outs[3:])
        return outs[:3]

    def mixed(places, base, last, *groups):
        states, us, vs, ws = zip(*groups)
        shape = sds((rows, depth), BF) if last else near((rows, depth), F32)
        return call(functools.partial(mix_kernel, head_dim, places, last), "mix", (shape,),
                    where + vm(keys, base, gain, *states, *us, *vs, *ws),
                    [near((rows, depth)), sems(depth // CHUNK)] if last else [], short,
                    ANY if last else VM)[0]

    totals, befores, arriving, firsts = [None, None], [None, None], [None, None], {}
    done = {}

    def work(own, group, w, xs, stamp, flops):
        done[own, group] = inner(own, group, w, after(xs, stamp), flops)
        return done[own, group][0]

    def start_total(i, mine, theirs):
        totals[i], = call(functools.partial(total_kernel, i, width), "total", (kinds[i],),
                          where + vm(mine, theirs, s_m1, got_1))
        arriving[i] = lax.ppermute(totals[i], "tm", pair(2))

    def advance(i, reach, arrived):
        if i == 0:
            firsts[reach] = totals[0], arrived, befores[0]
        own, theirs, before = firsts[reach]
        carried = [] if reach == 2 else [befores[i], before]
        final = reach * 4 >= peers
        befores[i], totals[i] = call(
            functools.partial(step_kernel, i, width, reach), "step", (kinds[i], kinds[1] if final else kinds[i]),
            where + vm(totals[i], arrived, own, theirs, *carried))
        arriving[i] = lax.ppermute(totals[i], "tm", pair(2 * reach))

    def finish(i, arrived, mine, theirs):
        keep, send = call(functools.partial(last_kernel, i, peers // 2), "last", (kinds[1],) * 2,
                          where + vm(arrived, befores[i], befores[0], mine, theirs, s_m1, got_1))
        return keep, lax.ppermute(send, "tm", pair(1))

    got_1 = lax.ppermute(s_o1, "tm", pair(1))
    xs_m1, s_m1 = projected(1, 0, w_m1)
    start_total(0, s_m1, got_1)
    xs_o2, s_o2 = projected(0, 1, after(w_o2, totals[0]))
    got_2 = lax.ppermute(s_o2, "tm", pair(1))
    xs_m2, s_m2, early = projected(1, 1, after(w_m2, s_o2), keys)
    scores.append(early)
    start_total(1, s_m2, got_2)
    stamp = work(0, 0, w_o1, xs_o1, totals[1], long)
    advance(0, 2, after(arriving[0], stamp))
    stamp = work(1, 0, w_m1, xs_m1, befores[0], short)
    stamp = work(1, 1, w_m2, xs_m2, stamp, short)
    advance(1, 2, after(arriving[1], stamp))
    reach = 4
    while reach * 2 < peers:
        for i in range(2):
            advance(i, reach, arriving[i])
        reach *= 2
    keep_1, sent_1 = finish(0, after(arriving[0], befores[1]), s_m1, got_1)
    stamp = work(0, 1, w_o2, xs_o2, keep_1, short)
    mixing = mixed(((1, 0),), after(encoded, stamp), False, (keep_1, *done[1, 0]))
    keep_2, sent_2 = finish(1, after(arriving[1], mixing), s_m2, got_2)
    mixing = mixed(((0, 0), (1, 1)), after(mixing, keep_2), False, (sent_1, *done[0, 0]), (keep_2, *done[1, 1]))
    return mixed(((0, 1),), mixing, True, (sent_2, *done[0, 1])).reshape(rows, 1, depth)


def solution(mesh):
    placed = (P("tm", "space", None), P("space")) + (P(),) * 13
    return jax.shard_map(body, mesh=mesh, in_specs=placed, out_specs=P("tm", "space", None), check_vma=False)
```

```python
import functools

import jax
import jax.numpy as jnp
from jax import lax
from jax.experimental import pallas as pl
from jax.experimental.pallas import tpu as pltpu
from jax.sharding import PartitionSpec as P

BF = jnp.bfloat16
F32 = jnp.float32
VM = pl.BlockSpec(memory_space=pltpu.VMEM)
SM = pl.BlockSpec(memory_space=pltpu.SMEM)
ANY = pl.BlockSpec(memory_space=pl.ANY)
LANES = 128
CHUNK = 256
EXTRA = 16


def dot(a, b):
    return jnp.dot(a, b, preferred_element_type=F32)


def dot_t(a, b):
    return lax.dot_general(a, b, (((1,), (1,)), ((), ())), preferred_element_type=F32)


def iota(shape, axis):
    return lax.broadcasted_iota(jnp.int32, shape, axis)


def params(mib):
    return pltpu.CompilerParams(vmem_limit_bytes=mib * 2**20)


def sds(shape, dtype):
    return jax.ShapeDtypeStruct(shape, dtype)


def spread_heads(first_head, heads, head_dim):
    row = iota((2 * heads, CHUNK), 0)
    lane = iota((2 * heads, CHUNK), 1)
    row = jnp.where(row < heads, row, row - heads)
    return (row == first_head + lane // head_dim).astype(F32).astype(BF)


def split_two(value, heads):
    high = value.astype(BF).astype(F32)
    return jnp.where(iota(value.shape, 1) < heads, high, value - high).astype(BF)


def pick_half(tile_a, tile_b, part):
    half = LANES // 2
    low = iota(tile_a.shape, 1) < half
    if part == 0:
        return jnp.where(low, tile_a, pltpu.roll(tile_b, half, 1))
    return jnp.where(low, pltpu.roll(tile_a, half, 1), tile_b)


def compact(ref, j, part):
    start = j * 2 * CHUNK
    tiles = [ref[:, start + i:start + i + LANES] for i in range(0, 2 * CHUNK, LANES)]
    pairs = [pick_half(tiles[i], tiles[i + 1], part) for i in range(0, len(tiles), 2)]
    return jnp.concatenate(pairs, axis=1)


def project(first, w, xs_ref, s_ref, heads, head_dim, normed, b_t, grow, fall_end):
    width = b_t.shape[0]
    later = []
    for j in range(xs_ref.shape[1] // CHUNK):
        cols = slice(j * CHUNK, (j + 1) * CHUNK)
        spread = spread_heads(first + j * (CHUNK // head_dim), heads, head_dim)
        x = dot(normed[...], compact(w, j, 0)).astype(BF)
        scaled = (x.astype(F32) * dot(grow, spread)).astype(BF)
        xs_ref[:, cols] = scaled
        decay = dot(fall_end, spread)[EXTRA - 1:EXTRA]
        if s_ref.shape[0] > width:
            next_first = first + (xs_ref.shape[1] + j * CHUNK) // head_dim
            next_decay = dot(fall_end, spread_heads(next_first, heads, head_dim))[EXTRA - 1:EXTRA]
            s_ref[width:width + EXTRA, cols] = decay_rows((decay, next_decay))
        later.append((cols, scaled, decay))
    for cols, scaled, decay in later:
        s_ref[0:width, cols] = (dot(b_t, scaled) * decay).astype(BF)


def decay_rows(values):
    row = iota((EXTRA, values[0].shape[1]), 0)
    out = jnp.zeros(row.shape, F32)
    for k, value in enumerate(values):
        high = value.astype(BF).astype(F32)
        out = jnp.where(row == 2 * k, high, jnp.where(row == 2 * k + 1, value - high, out))
    return out.astype(BF)


def in_pieces(src, dst, sem, slot):
    block = dst.shape[0] // 2

    def piece(i):
        part = pl.ds(pl.multiple_of(i * block, block), block)
        return pltpu.make_async_copy(src.at[part, :], dst.at[part, :], sem.at[slot, i])

    return piece


def start_pieces(pieces):
    def go(i, carry):
        for piece in pieces:
            piece(i).start()
        return carry

    lax.fori_loop(0, 2, go, 0)


def wait_pieces(pieces):
    def go(i, carry):
        for piece in pieces:
            piece(i).wait()
        return carry

    lax.fori_loop(0, 2, go, 0)


def encode_kernel(heads, head_dim, here_ref, cell_ref, frames_any, enc_in_any, bias_any, enc_out_any, pos_any, gain_any,
                  w_keys_any, w_step_any, step_bias_any, code_any, skip_any, out_gain_any, w_pair_any,
                  encoded, normed, keys, b_t, grow, fall, skip, out_gain, xs_o1, s_o1, w_o1, w_m1, w_o2, w_m2,
                  frames, enc_in, bias, enc_out, pos, norm_gain, w_keys, w_step, step_bias, code, sem, wsem):
    half = 1 - here_ref[0] % 2
    cell = cell_ref[0]
    base = pl.multiple_of((cell // EXTRA) * EXTRA, EXTRA)
    small = [pltpu.make_async_copy(src, dst, sem.at[i]) for i, (src, dst) in enumerate((
        (bias_any, bias), (pos_any.at[pl.ds(base, EXTRA), :], pos), (gain_any, norm_gain), (step_bias_any, step_bias),
        (code_any, code), (skip_any, skip), (out_gain_any, out_gain)))]
    first = [in_pieces(src, dst, wsem, i) for i, (src, dst) in enumerate((
        (frames_any, frames), (enc_in_any, enc_in), (enc_out_any, enc_out), (w_keys_any, w_keys), (w_step_any, w_step)))]
    big = [in_pieces(group_columns(w_pair_any, dst, which, group), dst, wsem, 5 + i) for i, (which, group, dst) in enumerate((
        (half, 0, w_o1), (1 - half, 0, w_m1), (half, 1, w_o2), (1 - half, 1, w_m2)))]
    start_pieces(first[:2])
    for c in small:
        c.start()
    start_pieces(first[2:])
    rows, depth = encoded.shape
    block = rows // 2
    lower = (iota((rows, rows), 0) >= iota((rows, rows), 1)).astype(F32).astype(BF)
    small[0].wait()
    wait_pieces(first[:2])
    start_pieces(big)
    twice = lambda v: jnp.concatenate([v, v], axis=1)
    columns = [slice(j, j + CHUNK) for j in range(0, depth, CHUNK)]

    def hide(part):
        pieces = []
        for cols in columns:
            h = dot(frames[part, :], enc_in[:, cols]) + bias[:, cols]
            pieces.append(jax.nn.gelu(h, approximate=True).astype(BF))
        return jnp.concatenate(pieces, axis=1)

    def encode(part, hidden, row):
        square = jnp.zeros((block, 1), F32)
        for cols in columns:
            e = (dot(hidden, enc_out[:, cols]) + row[:, cols]).astype(BF)
            encoded[part, cols] = e
            e = e.astype(F32)
            square += jnp.sum(e * e, axis=1, keepdims=True)
        inv = lax.rsqrt(square / depth + 1e-05)
        pieces = []
        for cols in columns:
            piece = (encoded[part, cols].astype(F32) * inv * norm_gain[:, cols]).astype(BF)
            normed[part, cols] = piece
            pieces.append(piece)
        return jnp.concatenate(pieces, axis=1)

    def read_out(part, wide):
        k = dot(wide, w_keys[...]).astype(BF)
        keys[part, :] = k
        b_t[:, part] = k[:, :k.shape[1] // 2].T
        ws = w_step[...]
        raw = dot_t(wide, jnp.concatenate([ws, ws], axis=0)) + twice(step_bias[...])
        return jax.nn.sigmoid(raw).astype(BF)

    top, low = slice(0, block), slice(block, rows)
    hidden_top = hide(top)
    hidden_low = hide(low)
    for c in small[1:]:
        c.wait()
    wait_pieces(first[2:])
    row = jnp.sum(jnp.where(iota(pos.shape, 0) == cell - base, pos[...].astype(F32), 0.0), axis=0, keepdims=True)
    wide_top = encode(top, hidden_top, row)
    wide_low = encode(low, hidden_low, row)
    step = jnp.concatenate([read_out(top, wide_top), read_out(low, wide_low)], axis=0)
    cum = dot(lower, step) * twice(-0.0005 - 0.003 * code[...].astype(F32))
    g = split_two(jnp.exp(-cum), heads)
    f = split_two(jnp.exp(cum), heads)
    grow[...] = g
    fall[...] = f
    wait_pieces(big[:1])
    project(half * (heads // 2), w_o1, xs_o1, s_o1, heads, head_dim, normed, b_t[...], g, f[rows - EXTRA:])
    wait_pieces(big[1:])


def group_columns(w_any, like, half, group):
    size = like.shape[1]
    return w_any.at[:, pl.ds(pl.multiple_of((half * 2 + group) * size, size), size)]


def project_kernel(heads, head_dim, own, group, here_ref, normed, b_t, grow, fall, w, xs_ref, s_ref):
    half = (here_ref[0] + 1 - own) % 2
    rows = normed.shape[0]
    first = (half * 2 + group) * (xs_ref.shape[1] // head_dim)
    project(first, w, xs_ref, s_ref, heads, head_dim, normed, b_t[...], grow[...], fall[rows - EXTRA:])


def state_of(ref, width):
    return ref[:width, :].astype(F32)


def decays_of(ref):
    tail = ref[ref.shape[0] - EXTRA:, :].astype(F32)
    return tail[0:1] + tail[1:2], tail[2:3] + tail[3:4]


def put(ref, width, state, decays):
    ref[:width, :] = state.astype(BF)
    if ref.shape[0] > width:
        ref[width:, :] = decay_rows(decays)


def times(one, other):
    return one[0] * other[0], one[1] * other[1]


def total_kernel(group, width, here_ref, mine_ref, got_ref, mine_first, got_first, total_ref):
    mine, got = state_of(mine_ref, width), state_of(got_ref, width)
    mine_decays, got_decays = decays_of(mine_first), decays_of(got_first)
    both = times(mine_decays, got_decays)

    @pl.when(here_ref[0] % 2 == 1)
    def _():
        put(total_ref, width, mine_decays[group] * got + mine, both)

    @pl.when(here_ref[0] % 2 == 0)
    def _():
        put(total_ref, width, got_decays[group] * mine + got, both)


def step_kernel(group, width, reach, here_ref, total_ref, got_ref, total_first, got_first, *refs):
    begin = len(refs) == 2
    new_before_ref, new_total_ref = refs[-2:]
    later = (here_ref[0] // reach) % 2 == 1
    got, total = state_of(got_ref, width), state_of(total_ref, width)
    got_decays, total_decays = decays_of(got_first), decays_of(total_first)
    both = times(total_decays, got_decays)

    @pl.when(later)
    def _():
        if begin:
            put(new_before_ref, width, got, got_decays)
        else:
            before_decays = decays_of(refs[1])
            put(new_before_ref, width, state_of(refs[0], width) + before_decays[group] * got,
                times(before_decays, got_decays))
        put(new_total_ref, width, total_decays[group] * got + total, both)

    @pl.when(jnp.logical_not(later))
    def _():
        if begin:
            one = jnp.ones_like(got_decays[0])
            put(new_before_ref, width, jnp.zeros_like(got), (one, one))
        else:
            put(new_before_ref, width, state_of(refs[0], width), decays_of(refs[1]))
        put(new_total_ref, width, got_decays[group] * total + got, both)


def last_kernel(group, reach, here_ref, got_ref, before_ref, before_first, mine_ref, theirs_ref, mine_first, theirs_first,
                keep_ref, send_ref):
    width = keep_ref.shape[0]
    later = (here_ref[0] // reach) % 2 == 1
    before_decay = jnp.where(later, decays_of(before_first)[group], 0.0)
    before = state_of(before_ref, width) + before_decay * state_of(got_ref, width)

    @pl.when(here_ref[0] % 2 == 1)
    def _():
        keep_ref[...] = (decays_of(theirs_first)[group] * before + state_of(theirs_ref, width)).astype(BF)
        send_ref[...] = before.astype(BF)

    @pl.when(here_ref[0] % 2 == 0)
    def _():
        send_ref[...] = (decays_of(mine_first)[group] * before + state_of(mine_ref, width)).astype(BF)
        keep_ref[...] = before.astype(BF)


def inner_kernel(heads, head_dim, own, group, fresh, here_ref, normed, keys, fall, skip, w_out_any, w, xs, *refs):
    half = (here_ref[0] + 1 - own) % 2
    rows = keys.shape[0]
    width = keys.shape[1] // 2
    size = xs.shape[1]
    if fresh:
        u, v, w_rows, scores_ref, sem = refs
    else:
        scores_ref, u, v, w_rows, sem = refs
    start = pl.multiple_of((half * 2 + group) * size, size)
    copies = [in_pieces(w_out_any.at[pl.ds(start, size), :], w_rows, sem, 0)]
    start_pieces(copies)
    if fresh:
        scores = dot_t(keys[:, width:], keys[:, :width])
        scores_ref[...] = jnp.where(iota((rows, rows), 0) >= iota((rows, rows), 1), scores, 0.0).astype(BF)
    scores = scores_ref[...]
    mid = rows // 2
    both = jnp.broadcast_to(jnp.concatenate([skip[...], skip[...]], axis=1), (EXTRA, 2 * heads))
    skip_two = split_two(both, heads)
    first = (half * 2 + group) * (size // head_dim)
    for j in range(size // CHUNK):
        cols = slice(j * CHUNK, (j + 1) * CHUNK)
        z = dot(normed[...], compact(w, j, 1)).astype(BF).astype(F32)
        gate = z * jax.nn.sigmoid(z)
        spread = spread_heads(first + j * (CHUNK // head_dim), heads, head_dim)
        gain = dot(skip_two, spread)[0:1]
        grown = dot(fall[...], spread)
        grown = grown * gate
        u[:, cols] = grown.astype(BF)
        top = dot(scores[:mid, :mid], xs[:mid, cols])
        low = dot(scores[mid:], xs[:, cols])
        for part, inner in ((slice(0, mid), top), (slice(mid, rows), low)):
            v[part, cols] = (grown[part] * (inner + gain * xs[part, cols].astype(F32))).astype(BF)
    wait_pieces(copies)


def mix_kernel(head_dim, places, last, here_ref, keys, base, gain, *refs):
    many = len(places)
    states, us, vs, ws = (refs[i * many:(i + 1) * many] for i in range(4))
    out = refs[4 * many]
    width = keys.shape[1] // 2
    size = us[0].shape[1]
    starts = [((here_ref[0] + 1 - own) % 2 * 2 + group) * size for own, group in places]
    same = (iota((CHUNK, CHUNK), 0) // head_dim) == (iota((CHUNK, CHUNK), 1) // head_dim)
    mean = jnp.where(same, 1.0 / head_dim, 0.0).astype(BF)
    work = []
    for state, u, v in zip(states, us, vs):
        for j in range(size // CHUNK):
            cols = slice(j * CHUNK, (j + 1) * CHUNK)
            carried = dot(keys[:, width:], state[:, cols])
            g = v[:, cols].astype(F32) + u[:, cols].astype(F32) * carried
            work.append((g, dot((g * g).astype(BF), mean)))
    steps = base.shape[1] // CHUNK
    totals = [base[:, n * CHUNK:(n + 1) * CHUNK].astype(F32) for n in range(steps)]
    for i in range(many):
        parts = []
        for j in range(size // CHUNK):
            g, m = work[i * (size // CHUNK) + j]
            row = gain[:, pl.ds(pl.multiple_of(starts[i] + j * CHUNK, CHUNK), CHUNK)]
            parts.append((g * lax.rsqrt(m + 1e-05) * row).astype(BF))
        mixed = jnp.concatenate(parts, axis=1)
        totals = [totals[n] + dot(mixed, ws[i][:, n * CHUNK:(n + 1) * CHUNK]) for n in range(steps)]
    copies = []
    for n, total in enumerate(totals):
        cols = slice(n * CHUNK, (n + 1) * CHUNK)
        if last:
            buf, sem = refs[4 * many + 1:]
            buf[:, cols] = total.astype(buf.dtype)
            copies.append(pltpu.make_async_copy(buf.at[:, cols], out.at[:, cols], sem.at[n]))
            copies[-1].start()
        else:
            out[:, cols] = total.astype(out.dtype)
    for c in copies:
        c.wait()


def body(frames, patch_cell, enc_in, enc_bias, enc_out, pos_table, norm_gain, w_pair, w_keys, w_step,
         step_bias, decay_code, skip_gain, out_gain, w_out):
    rows = frames.shape[0]
    pix = frames.shape[2]
    depth = enc_out.shape[1]
    heads = w_step.shape[1]
    head_dim = w_pair.shape[1] // (2 * heads)
    width = w_keys.shape[1] // 2
    size = heads * head_dim // 4
    peers = lax.axis_size("tm")
    here = lax.axis_index("tm").astype(jnp.int32).reshape(1)
    row = lambda v: v.reshape(1, -1)
    far = lambda v: pltpu.with_memory_space_constraint(v, pltpu.HBM)
    near = lambda shape, dtype=BF: pltpu.VMEM(shape, dtype)
    sems = lambda n: pltpu.SemaphoreType.DMA((n,))
    pair = lambda by: [(i, i ^ by) for i in range(peers)]
    after = lambda value, *first: lax.optimization_barrier((value,) + first)[0]

    def call(kernel, name, outs, ins, scratch=(), flops=0, out_spec=VM):
        specs = [spec for spec, _ in ins]
        cost = pl.CostEstimate(flops=flops, bytes_accessed=2**20, transcendentals=0)
        return pl.pallas_call(kernel, out_shape=tuple(outs), in_specs=specs, out_specs=(out_spec,) * len(outs),
                              scratch_shapes=list(scratch), compiler_params=params(24), name=name,
                              cost_estimate=cost)(*[v for _, v in ins])

    vm = lambda *vs: [(VM, v) for v in vs]
    hbm = lambda *vs: [(pl.BlockSpec(memory_space=pltpu.HBM), far(v)) for v in vs]
    where = [(SM, here)]

    part, message, weight = near((rows, size)), near((width + EXTRA, size)), near((depth, 2 * size))
    kinds = (message, near((width, size)))
    encoded, normed, keys, b_t, grow, fall, skip, gain, xs_o1, s_o1, w_o1, w_m1, w_o2, w_m2 = call(
        functools.partial(encode_kernel, heads, head_dim), "encode",
        (near((rows, depth)), near((rows, depth)), near((rows, 2 * width)), near((width, rows)),
         near((rows, 2 * heads)), near((rows, 2 * heads)), near((1, heads), F32), near((1, heads * head_dim), F32),
         part, message) + (weight,) * 4,
        where + [(SM, patch_cell)] + hbm(frames.reshape(rows, pix), enc_in, row(enc_bias), enc_out, pos_table, row(norm_gain),
                                         w_keys, w_step.T, row(step_bias), row(decay_code), row(skip_gain), row(out_gain),
                                         w_pair),
        [near((rows, pix)), near((pix, depth)), near((1, depth), F32), near((depth, depth)), near((EXTRA, depth)),
         near((1, depth), F32), near((depth, 2 * width)), near((heads, depth)), near((1, heads), F32),
         near((1, heads), jnp.int32), sems(7), pltpu.SemaphoreType.DMA((9, 2))],
        rows * depth * depth)

    long, short = 4 * rows * depth * size, rows * depth * size // 4

    def projected(own, group, w):
        return call(functools.partial(project_kernel, heads, head_dim, own, group), "project",
                    (part, kinds[group]), where + vm(normed, b_t, grow, fall, w), (), long)

    scores = []

    def inner(own, group, w, xs, flops):
        outs = call(functools.partial(inner_kernel, heads, head_dim, own, group, not scores), "inner",
                    (part, part, near((size, depth))) + (() if scores else (near((rows, rows)),)),
                    where + vm(normed, keys, fall, skip) + hbm(w_out) + vm(w, xs, *scores),
                    [pltpu.SemaphoreType.DMA((1, 2))], flops)
        scores.extend(outs[3:])
        return outs[:3]

    def mixed(places, base, last, *groups):
        states, us, vs, ws = zip(*groups)
        shape = sds((rows, depth), BF) if last else near((rows, depth), F32)
        return call(functools.partial(mix_kernel, head_dim, places, last), "mix", (shape,),
                    where + vm(keys, base, gain, *states, *us, *vs, *ws),
                    [near((rows, depth)), sems(depth // CHUNK)] if last else [], short,
                    ANY if last else VM)[0]

    totals, befores, arriving, firsts = [None, None], [None, None], [None, None], {}
    done = {}

    def work(own, group, w, xs, stamp, flops):
        done[own, group] = inner(own, group, w, after(xs, stamp), flops)
        return done[own, group][0]

    def start_total(i, mine, theirs):
        totals[i], = call(functools.partial(total_kernel, i, width), "total", (kinds[i],),
                          where + vm(mine, theirs, s_m1, got_1))
        arriving[i] = lax.ppermute(totals[i], "tm", pair(2))

    def advance(i, reach, arrived):
        if i == 0:
            firsts[reach] = totals[0], arrived, befores[0]
        own, theirs, before = firsts[reach]
        carried = [] if reach == 2 else [befores[i], before]
        final = reach * 4 >= peers
        befores[i], totals[i] = call(
            functools.partial(step_kernel, i, width, reach), "step", (kinds[i], kinds[1] if final else kinds[i]),
            where + vm(totals[i], arrived, own, theirs, *carried))
        arriving[i] = lax.ppermute(totals[i], "tm", pair(2 * reach))

    def finish(i, arrived, mine, theirs):
        keep, send = call(functools.partial(last_kernel, i, peers // 2), "last", (kinds[1],) * 2,
                          where + vm(arrived, befores[i], befores[0], mine, theirs, s_m1, got_1))
        return keep, lax.ppermute(send, "tm", pair(1))

    got_1 = lax.ppermute(s_o1, "tm", pair(1))
    xs_m1, s_m1 = projected(1, 0, w_m1)
    start_total(0, s_m1, got_1)
    xs_o2, s_o2 = projected(0, 1, after(w_o2, totals[0]))
    got_2 = lax.ppermute(s_o2, "tm", pair(1))
    xs_m2, s_m2 = projected(1, 1, after(w_m2, s_o2))
    start_total(1, s_m2, got_2)
    stamp = work(0, 0, w_o1, xs_o1, totals[1], long)
    advance(0, 2, after(arriving[0], stamp))
    stamp = work(1, 0, w_m1, xs_m1, befores[0], short)
    stamp = work(1, 1, w_m2, xs_m2, stamp, short)
    advance(1, 2, after(arriving[1], stamp))
    reach = 4
    while reach * 2 < peers:
        for i in range(2):
            advance(i, reach, arriving[i])
        reach *= 2
    keep_1, sent_1 = finish(0, after(arriving[0], befores[1]), s_m1, got_1)
    stamp = work(0, 1, w_o2, xs_o2, keep_1, short)
    mixing = mixed(((1, 0),), after(encoded, stamp), False, (keep_1, *done[1, 0]))
    keep_2, sent_2 = finish(1, after(arriving[1], mixing), s_m2, got_2)
    mixing = mixed(((0, 0), (1, 1)), after(mixing, keep_2), False, (sent_1, *done[0, 0]), (keep_2, *done[1, 1]))
    return mixed(((0, 1),), mixing, True, (sent_2, *done[0, 1])).reshape(rows, 1, depth)


def solution(mesh):
    placed = (P("tm", "space", None), P("space")) + (P(),) * 13
    return jax.shard_map(body, mesh=mesh, in_specs=placed, out_specs=P("tm", "space", None), check_vma=False)
```
